32 devices in a mesh: tile: 8 (over y, x, core), kern: 4 (over z).
Axes of the slice: x: 2, y: 2, z: 4, core: 2. Of those that a mesh axis runs over, the one named last changes fastest.
Arguments:
- mask_pixels: bfloat16 [1152, 9216], P(None, 'tile'), may hold values from -6 to 6
- orientation: int32 [8, 2], P('tile'), may hold values 0 or 1
- target_pattern: int32 [1152, 9216], P('kern', 'tile'), may hold values 0 or 1
- kernel_real: float32 [4, 64, 64], P('kern'), may hold values from -6 to 6
- kernel_imag: float32 [4, 64, 64], P('kern'), may hold values from -6 to 6
- eigen_weights: float32 [4], P('kern'), may hold values from 0.01 to 0.1
Outputs:
- mask_gradient: float32 [1152, 9216], P('kern', 'tile')
The draws below stay inside these ranges and needn't reach their ends.
Inputs may be any that keep to these rules, and one draw needn't show every extreme that they name: `orientation`: 1 takes the neighbour's facing strip in order, 0 reversed; the entry for a side without neighbour is unused.
All inputs are finite; a program needn't handle non-finite values. No bound on the sum of `orientation` or of `target_pattern` on one device may be relied on, other than what follows from the above.
Results may differ from the reference program's by a relative error of at most 0.018.
Values may be sent and summed in bfloat16 or wider, within the bound.
No kernel may reach another device: no remote copies, remote signals or barrier semaphores. Data moves between devices by JAX's collectives and lax.ppermute only.
A program may use at most 64 MiB of HBM per device.

```python
import math
import jax
import jax.numpy as jnp
from jax import lax

N = 1152
HALO = 64
KF = 64
KERNELS = 4
TILES = 8
NE = 1280


def touch_ends(drawn, rng, smallest, top_value):
    dims = drawn.shape
    place = [jax.random.randint(jax.random.fold_in(rng, axis), (), 0, dims[axis]) for axis in range(len(dims))]
    drawn = drawn.at[tuple(place)].set(smallest)
    longest = dims.index(max(dims))
    place[longest] = (place[longest] + 1) % dims[longest]
    return drawn.at[tuple(place)].set(top_value)


def block_scale(own_key, shape, shards, low, largest):
    def one(dim, parts):
        heights = jax.random.uniform(jax.random.fold_in(jax.random.fold_in(own_key, 6), dim), (parts,), jnp.float32, low / len(shards), largest / len(shards))
        return jnp.repeat(jnp.exp(heights), shape[dim] // parts).reshape((-1,) + (1,) * (len(shape) - dim - 1))

    factor_of = one(*shards[0])
    for cut in shards[1:]:
        factor_of = factor_of * one(*cut)
    return factor_of


def scatter_about(key, dims, deviation, most, shards=(), kind=jnp.bfloat16):
    drawn = jax.random.normal(key, dims, jnp.float32) * deviation
    if len(shards) > 0:
        drawn = block_scale(key, dims, shards, -0.22, 0.18) * drawn
    return jnp.clip(drawn, min=-most, max=most).astype(kind)


def setup_inputs(seed: int = 0) -> dict:
    key_list = jax.random.split(jax.random.key(seed), 7)
    mask_pixels = scatter_about(key_list[0], (N, TILES * N), 1.0, 6.0, ((1, 8),))
    orientation = touch_ends((jax.random.randint(key_list[1], (TILES, 2), 0, 2) < 1).astype(jnp.int32), jax.random.fold_in(key_list[1], 1), 0, 1)
    target_pattern = touch_ends((jax.random.randint(key_list[2], (N, TILES * N), 0, 2) < 1).astype(jnp.int32), jax.random.fold_in(key_list[2], 1), 0, 1)
    kernel_real = scatter_about(key_list[3], (KERNELS, KF, KF), 1.0, 6.0, ((0, 4),), jnp.float32)
    kernel_imag = scatter_about(key_list[4], (KERNELS, KF, KF), 1.0, 6.0, ((0, 4),), jnp.float32)
    eigen_weights = jnp.clip(jnp.exp(math.log(0.1) - 2.3025851 * jax.random.uniform(key_list[5], (KERNELS,), jnp.float32) ** block_scale(key_list[5], (KERNELS,), ((0, 4),), -0.2, 0.2)), 0.01, 0.1)
    return dict(mask_pixels=mask_pixels, orientation=orientation, target_pattern=target_pattern, kernel_real=kernel_real, kernel_imag=kernel_imag, eigen_weights=eigen_weights)


STEEPNESS = 4.0
THRESHOLD = 1.0


def wave_tables(first, length):
    position = first + lax.iota(jnp.int32, length)
    frequency = lax.iota(jnp.int32, KF) - KF // 2
    phase = jnp.mod(position[:, None] * frequency[None, :], NE).astype(jnp.float32) * (2.0 * math.pi / NE)
    return jnp.cos(phase).astype(jnp.bfloat16), jnp.sin(phase).astype(jnp.bfloat16)


def transform_tables():
    cos_full, sin_full = wave_tables(0, NE)
    cos_mid = cos_full[HALO:HALO + N]
    sin_mid = sin_full[HALO:HALO + N]
    full_pair = jnp.concatenate([cos_full, sin_full], 1)
    mid_pair = jnp.concatenate([cos_mid, sin_mid], 1)
    to_columns = jnp.concatenate([jnp.concatenate([cos_mid.T, sin_mid.T], 1), jnp.concatenate([-sin_mid.T, cos_mid.T], 1)], 0)
    from_columns = jnp.concatenate([jnp.concatenate([cos_mid, -sin_mid], 1), jnp.concatenate([sin_mid, cos_mid], 1)], 0)
    to_extended = jnp.concatenate([jnp.concatenate([cos_full.T, sin_full.T], 1), jnp.concatenate([-sin_full.T, cos_full.T], 1)], 0)
    return full_pair, mid_pair, to_columns, from_columns, to_extended


def mask_spectrum(row_spectrum, mid_pair):
    blocks = lax.dot_general(mid_pair, row_spectrum, (((0,), (0,)), ((), ())), preferred_element_type=jnp.float32)
    spec_real = blocks[:KF, :KF] - blocks[KF:, KF:]
    spec_imag = -(blocks[:KF, KF:] + blocks[KF:, :KF])
    return spec_real, spec_imag


def column_fields(kernel_re, kernel_im, spec_real, spec_imag, to_columns):
    scale = 1.0 / (NE * KF)
    product = jnp.concatenate([kernel_re * spec_real - kernel_im * spec_imag, kernel_re * spec_imag + kernel_im * spec_real], 1) * scale
    columns = jnp.dot(product.astype(jnp.bfloat16), to_columns, preferred_element_type=jnp.float32).astype(jnp.bfloat16)
    return jnp.concatenate([columns, jnp.concatenate([-columns[:, N:], columns[:, :N]], 1)], 0)


def intensity_term(fields, weight):
    field_real = fields[..., :N].astype(jnp.float32)
    field_imag = fields[..., N:].astype(jnp.float32)
    return weight * (field_real * field_real + field_imag * field_imag)


def resist_slope(intensity, target_rows):
    resist = jax.nn.sigmoid(STEEPNESS * (intensity - THRESHOLD))
    return (2.0 * (resist - target_rows.astype(jnp.float32)) * STEEPNESS * resist * (1.0 - resist)).astype(jnp.bfloat16)


def weighted_fields(fields, slope):
    doubled = jnp.concatenate([slope, slope], 1).astype(jnp.float32)
    return (fields.astype(jnp.float32) * doubled).astype(jnp.bfloat16)


def adjoint_spectrum(blocks, kernel_re, kernel_im, weight):
    wave_real = blocks[:KF, :KF] + blocks[KF:, KF:]
    wave_imag = blocks[:KF, KF:] - blocks[KF:, :KF]
    factor = 2.0 * weight / (NE * KF)
    return factor * (kernel_re * wave_real + kernel_im * wave_imag), factor * (kernel_re * wave_imag - kernel_im * wave_real)


def extended_gradient(grad_real, grad_imag, row_pair, to_extended):
    combined = jnp.concatenate([grad_real, grad_imag], 1).astype(jnp.bfloat16)
    waves = jnp.dot(combined, to_extended, preferred_element_type=jnp.float32).astype(jnp.bfloat16)
    stacked = jnp.concatenate([waves[:, :NE], -waves[:, NE:]], 0)
    return jnp.dot(row_pair, stacked, preferred_element_type=jnp.float32)


def reference(mask_pixels, orientation, target_pattern, kernel_real, kernel_imag, eigen_weights):
    full_pair, mid_pair, to_columns, from_columns, to_extended = transform_tables()
    padded = jnp.pad(mask_pixels, ((0, 0), (HALO, HALO)))

    def one_tile(tile_index):
        offset = (tile_index * N).astype(jnp.int32)
        extended = lax.dynamic_slice(padded, (jnp.int32(0), offset), (N, NE))
        flag_pair = orientation[tile_index]
        left_rim = extended[:, :HALO]
        right_rim = extended[:, HALO + N:]
        left_rim = jnp.where(flag_pair[0] == 1, left_rim, left_rim[:, ::-1])
        right_rim = jnp.where(flag_pair[1] == 1, right_rim, right_rim[:, ::-1])
        extended = jnp.concatenate([left_rim, extended[:, HALO:HALO + N], right_rim], 1)
        row_spectrum = jnp.dot(extended, full_pair, preferred_element_type=jnp.float32).astype(jnp.bfloat16)
        spec_real, spec_imag = mask_spectrum(row_spectrum, mid_pair)

        def forward(running, kernel):
            one_real, one_imag, weight = kernel
            stacked = column_fields(one_real, one_imag, spec_real, spec_imag, to_columns)
            fields = jnp.dot(mid_pair, stacked, preferred_element_type=jnp.float32).astype(jnp.bfloat16)
            term = intensity_term(fields, weight).astype(jnp.bfloat16)
            return running + term.astype(jnp.float32), fields

        intensity, all_fields = lax.scan(forward, jnp.zeros((N, N), jnp.float32), (kernel_real, kernel_imag, eigen_weights))
        target_tile = lax.dynamic_slice(target_pattern, (jnp.int32(0), offset), (N, N))
        slope = resist_slope(intensity, target_tile)

        def backward(running, kernel):
            one_real, one_imag, weight, fields = kernel
            weighted = weighted_fields(fields, slope)
            partial_rows = jnp.dot(weighted, from_columns, preferred_element_type=jnp.float32).astype(jnp.bfloat16)
            blocks = lax.dot_general(mid_pair, partial_rows, (((0,), (0,)), ((), ())), preferred_element_type=jnp.float32)
            add_real, add_imag = adjoint_spectrum(blocks, one_real, one_imag, weight)
            return (running[0] + add_real, running[1] + add_imag), None

        empty = jnp.zeros((KF, KF), jnp.float32)
        (grad_real, grad_imag), unused = lax.scan(backward, (empty, empty), (kernel_real, kernel_imag, eigen_weights, all_fields))
        return extended_gradient(grad_real, grad_imag, mid_pair, to_extended)

    tile_grads = lax.map(one_tile, jnp.arange(TILES, dtype=jnp.int32))
    flag_left = orientation[:, 0][:, None, None]
    flag_right = orientation[:, 1][:, None, None]
    left_send = tile_grads[:, :, :HALO]
    right_send = tile_grads[:, :, HALO + N:]
    left_send = jnp.where(flag_left == 1, left_send, left_send[:, :, ::-1])
    right_send = jnp.where(flag_right == 1, right_send, right_send[:, :, ::-1])
    nothing = jnp.zeros((1, N, HALO), jnp.float32)
    from_left = jnp.concatenate([nothing, right_send[:-1]], 0)
    from_right = jnp.concatenate([left_send[1:], nothing], 0)
    middle = jnp.zeros((TILES, N, N - 2 * HALO), jnp.float32)
    gradient = tile_grads[:, :, HALO:HALO + N] + jnp.concatenate([from_left, middle, from_right], 2)
    return jnp.transpose(gradient, (1, 0, 2)).reshape(N, TILES * N)
```

```python
import functools
import math

import jax
import jax.numpy as jnp
import ml_dtypes
import numpy as np
from jax import lax
from jax.experimental import pallas as pl
from jax.experimental.pallas import tpu as pltpu
from jax.sharding import PartitionSpec as P

N = 1152
HALO = 64
KF = 64
NE = 1280
LANES = 128
PAIR = 2 * KF
BLOCKS = N // LANES
EDGE = PAIR
PACK = EDGE + KF + 16
BF16 = jnp.bfloat16
F32 = jnp.float32
VMEM_LIMIT = 32 * 1024 * 1024


def wave_tables():
    position = np.arange(NE)[:, None]
    frequency = np.arange(KF)[None, :] - KF // 2
    phase = np.mod(position * frequency, NE).astype(np.float64) * (2.0 * math.pi / NE)
    return np.cos(phase).astype(np.float32), np.sin(phase).astype(np.float32)


def transform_tables():
    cos, sin = wave_tables()
    full = np.concatenate([cos, sin], 1)
    mid = full[HALO : HALO + N]
    ct, st = cos[HALO : HALO + N].T, sin[HALO : HALO + N].T
    columns = np.concatenate(
        [
            np.stack([ct.reshape(KF, BLOCKS, LANES), st.reshape(KF, BLOCKS, LANES)], 2),
            np.stack([-st.reshape(KF, BLOCKS, LANES), ct.reshape(KF, BLOCKS, LANES)], 2),
        ],
        0,
    )
    to_columns = columns.transpose(1, 0, 2, 3).reshape(BLOCKS, PAIR, 2 * LANES)
    from_columns = to_columns.transpose(0, 2, 1)
    low, high = full[:HALO], full[HALO + N :]
    blank = np.zeros((HALO, PAIR), np.float32)
    rims = np.stack(
        [
            np.concatenate([blank, low[::-1]], 0),
            np.concatenate([blank, low], 0),
            np.concatenate([high[::-1], blank], 0),
            np.concatenate([high, blank], 0),
        ]
    )
    back = np.concatenate([cos.T, -sin.T], 0)
    back_low, back_high = back[:, :HALO], back[:, HALO + N :]
    blank = np.zeros((PAIR, HALO), np.float32)
    margins = np.stack(
        [
            np.concatenate([back_high[:, ::-1], blank], 1),
            np.concatenate([back_high, blank], 1),
            np.concatenate([blank, back_low[:, ::-1]], 1),
            np.concatenate([blank, back_low], 1),
        ]
    )
    tables = (mid, mid.T, to_columns, from_columns, rims, back[:, HALO : HALO + N], margins)
    return tuple(np.ascontiguousarray(one).astype(ml_dtypes.bfloat16) for one in tables)


def dot(a, b):
    return jnp.dot(a, b, preferred_element_type=F32)


def in_left_half(shape):
    return lax.broadcasted_iota(jnp.int32, shape, 1) < KF


def swap_halves(pair):
    return pltpu.roll(pair, KF, 1)


def call(body, name, outs, args, specs=None, grid=None, scratch=(), flops=0, moved=0):
    vmem = pl.BlockSpec(memory_space=pltpu.VMEM)
    extra = {} if grid is None else {"grid": grid}
    return pl.pallas_call(
        body,
        name=name,
        out_shape=outs,
        in_specs=specs,
        out_specs=jax.tree.map(lambda _: vmem, outs),
        scratch_shapes=list(scratch),
        compiler_params=pltpu.CompilerParams(vmem_limit_bytes=VMEM_LIMIT),
        cost_estimate=pl.CostEstimate(flops=flops, bytes_accessed=moved, transcendentals=0),
        **extra,
    )(*args)


def edges_body(first, last, mid_t, real, imag, weight, flags, up, down, side):
    scale = jnp.sqrt(jnp.full((KF, KF), 2.0 * weight[0], F32)) * (1.0 / (NE * KF))
    pair = jnp.concatenate([real[0] * scale, imag[0] * scale], 1).astype(BF16)
    row = lax.broadcasted_iota(jnp.int32, (16, LANES), 0)
    marks = jnp.where(row == 0, flags[0, 0].astype(F32), flags[0, 1].astype(F32)).astype(BF16)
    for out, strip in ((up, last), (down, first)):
        out[:EDGE, :] = dot(mid_t[...], strip[...]).astype(BF16)
        out[EDGE : EDGE + KF, :] = pair
        out[EDGE + KF :, :] = marks
    side[...] = pair


def middle_body(mask, mid, mid_t, out):
    rows = dot(mask[...], mid[...]).astype(BF16)
    part = dot(mid_t[...], rows)

    @pl.when(pl.program_id(0) == 0)
    def _():
        out[...] = part

    @pl.when(pl.program_id(0) > 0)
    def _():
        out[...] += part


def split_kernel(pair):
    left = in_left_half(pair.shape)
    other = swap_halves(pair)
    return jnp.where(left, pair, other), jnp.where(left, other, pair)


def fields_body(count, row_count, *refs):
    (flags, middle, target, mid, to_columns, from_columns, rims, own) = refs[:8]
    packs = refs[8 : 8 + count - 1]
    out, a_ref, e_ref, v_ref, u_ref = refs[8 + count - 1 :]
    tile = lax.axis_index("tile")
    tiles = lax.axis_size("tile")
    left = in_left_half((KF, PAIR))
    blocks = middle[...]
    low = jnp.where(flags[0, 0] == 1, rims[1], rims[0])
    low = jnp.where(tile == 0, jnp.zeros_like(low), low)
    high = jnp.where(flags[0, 1] == 1, rims[3], rims[2])
    high = jnp.where(tile == tiles - 1, jnp.zeros_like(high), high)
    blocks = blocks + dot(packs[0][:EDGE, :], low) + dot(packs[1][:EDGE, :], high)
    top, bottom = blocks[:KF], swap_halves(blocks[KF:])
    spectrum = jnp.where(left, top - bottom, -(top + bottom))
    turned = swap_halves(spectrum)
    turned = jnp.where(left, -turned, turned)
    kernels = [own[...].astype(F32)]
    for index, pack in enumerate(packs):
        start = EDGE if index < 2 else 0
        kernels.append(pack[start : start + KF, :].astype(F32))
    kernels = [split_kernel(one) for one in kernels]
    begin = pl.multiple_of(lax.axis_index("kern") * row_count, row_count)
    rows = mid[pl.ds(begin, row_count), :]
    for index, (real, imag) in enumerate(kernels):
        product = real * spectrum + imag * turned
        other = swap_halves(product)
        other = jnp.where(left, -other, other)
        stacked = jnp.concatenate([product, other], 0).astype(BF16)
        a_ref[index * row_count : (index + 1) * row_count, :] = dot(rows, stacked).astype(BF16)
    step = 32 if row_count % 32 == 0 else 16
    for block in range(BLOCKS):
        e_ref[...] = dot(a_ref[...], to_columns[block])
        for r in range(0, row_count, step):
            total = None
            parts = []
            for index in range(count):
                at = index * row_count + r
                real = e_ref[at : at + step, :LANES]
                imag = e_ref[at : at + step, LANES:]
                term = real * real + imag * imag
                total = term if total is None else total + term
            wanted = target[r : r + step, block * LANES : (block + 1) * LANES].astype(F32)
            bend = jnp.tanh(total - 2.0)
            slope = (bend + (1.0 - 2.0 * wanted)) * (1.0 - bend * bend)
            for index in range(count):
                at = index * row_count + r
                v_ref[at : at + step, :LANES] = (e_ref[at : at + step, :LANES] * slope).astype(BF16)
                v_ref[at : at + step, LANES:] = (e_ref[at : at + step, LANES:] * slope).astype(BF16)
        part = dot(v_ref[...], from_columns[block])
        if block == 0:
            u_ref[...] = part
        else:
            u_ref[...] += part
    wide = jnp.concatenate(
        [u_ref[i * row_count : (i + 1) * row_count, :].astype(BF16) for i in range(count)], 1
    )
    waves = lax.dot_general(rows, wide, (((0,), (0,)), ((), ())), preferred_element_type=F32)
    total = None
    for index, (real, imag) in enumerate(kernels):
        wave = waves[:, index * PAIR : (index + 1) * PAIR]
        top, bottom = wave[:KF], swap_halves(wave[KF:])
        wave = jnp.where(left, top + bottom, top - bottom)
        other = swap_halves(wave)
        other = jnp.where(left, other, -other)
        term = real * wave + imag * other
        total = term if total is None else total + term
    out[...] = total.astype(BF16)


def sum_body(count, *refs):
    total = refs[0][...].astype(F32)
    for one in refs[1:count]:
        total = total + one[...].astype(F32)
    refs[count][...] = total.astype(BF16)


def gradient_body(row_count, own, below, above, mark_below, mark_above, mid, back, margins, out):
    left = in_left_half((KF, PAIR))
    begin = pl.multiple_of(lax.axis_index("kern") * row_count, row_count)
    rows = mid[pl.ds(begin, row_count), :]
    waves = []
    for ref in (own, below, above):
        pair = ref[...].astype(F32)
        other = swap_halves(pair)
        other = jnp.where(left, -other, other)
        waves.append(dot(rows, jnp.concatenate([pair, other], 0).astype(BF16)).astype(BF16))
    low_mark = mark_below[EDGE + KF + 1 : EDGE + KF + 2, :].astype(F32)
    high_mark = mark_above[EDGE + KF : EDGE + KF + 1, :].astype(F32)
    low = jnp.where(low_mark == 1.0, margins[1].astype(F32), margins[0].astype(F32)).astype(BF16)
    high = jnp.where(high_mark == 1.0, margins[3].astype(F32), margins[2].astype(F32)).astype(BF16)
    out[:, :LANES] = dot(waves[0], back[:, :LANES]) + dot(waves[1], low)
    out[:, LANES : N - LANES] = dot(waves[0], back[:, LANES : N - LANES])
    out[:, N - LANES :] = dot(waves[0], back[:, N - LANES :]) + dot(waves[2], high)


def per_device(mask_pixels, orientation, target_pattern, kernel_real, kernel_imag, eigen_weights):
    tables = tuple(jnp.asarray(one) for one in transform_tables())
    mid, mid_t, to_columns, from_columns, rims, back, margins = tables
    tiles, count = lax.axis_size("tile"), lax.axis_size("kern")
    row_count = target_pattern.shape[0]
    vmem = pl.BlockSpec(memory_space=pltpu.VMEM)
    smem = pl.BlockSpec(memory_space=pltpu.SMEM)
    full = (0, 0)
    packed = jax.ShapeDtypeStruct((PACK, LANES), BF16)
    small = jax.ShapeDtypeStruct((KF, PAIR), BF16)

    up, down, side = call(
        edges_body,
        "edges",
        (packed, packed, small),
        (mask_pixels, mask_pixels, mid_t, kernel_real, kernel_imag, eigen_weights, orientation),
        [
            pl.BlockSpec((N, LANES), lambda i: (0, 0)),
            pl.BlockSpec((N, LANES), lambda i: (0, BLOCKS - 1)),
            vmem,
            vmem,
            vmem,
            smem,
            smem,
        ],
        grid=(1,),
        flops=2 * N * LANES * PAIR * 2,
        moved=N * LANES * 4,
    )

    def shifted(tile_step, kern_step):
        pairs = []
        for t in range(tiles):
            for k in range(count):
                there = ((t + tile_step) % tiles) * count + (k - kern_step) % count
                pairs.append((t * count + k, there))
        return pairs

    packs = []
    for kern_step in range(1, count):
        if kern_step <= 2:
            value, tile_step = ((up, 1), (down, -1))[kern_step - 1]
        else:
            value, tile_step = side, 0
        packs.append(lax.ppermute(value, ("tile", "kern"), shifted(tile_step, kern_step)))

    chunk = 384
    middle = call(
        middle_body,
        "middle",
        jax.ShapeDtypeStruct((PAIR, PAIR), F32),
        (mask_pixels, mid, mid_t),
        [
            pl.BlockSpec((chunk, N), lambda i: (i, 0)),
            vmem,
            pl.BlockSpec((PAIR, chunk), lambda i: (0, i)),
        ],
        grid=(N // chunk,),
        flops=4 * N * N * PAIR,
        moved=N * N * 2,
    )

    part = call(
        functools.partial(fields_body, count, row_count),
        "fields",
        small,
        (orientation, middle, target_pattern, mid, to_columns, from_columns, rims, side, *packs),
        [smem] + [vmem] * (7 + count - 1),
        scratch=[
            pltpu.VMEM((count * row_count, PAIR), BF16),
            pltpu.VMEM((count * row_count, 2 * LANES), F32),
            pltpu.VMEM((count * row_count, 2 * LANES), BF16),
            pltpu.VMEM((count * row_count, PAIR), F32),
        ],
        flops=8 * count * row_count * N * PAIR,
        moved=4 * row_count * N,
    )

    parts = [part]
    for kern_step in range(1, count):
        pairs = [(k, (k - kern_step) % count) for k in range(count)]
        parts.append(lax.ppermute(part, "kern", pairs))
    own = call(functools.partial(sum_body, count), "total", small, tuple(parts), [vmem] * count)
    forward = [(i, i + 1) for i in range(tiles - 1)]
    below = lax.ppermute(own, "tile", forward)
    above = lax.ppermute(own, "tile", [(target, source) for source, target in forward])
    return call(
        functools.partial(gradient_body, row_count),
        "gradient",
        jax.ShapeDtypeStruct((row_count, N), F32),
        (own, below, above, packs[0], packs[1], mid, back, margins),
        [vmem] * 8,
        flops=2 * row_count * PAIR * (N + 5 * PAIR),
        moved=4 * row_count * N,
    )


def solution(mesh):
    in_specs = (
        P(None, "tile"),
        P("tile", None),
        P("kern", "tile"),
        P("kern", None, None),
        P("kern", None, None),
        P("kern"),
    )
    out_specs = P("kern", "tile")
    return jax.shard_map(
        per_device, mesh=mesh, in_specs=in_specs, out_specs=out_specs, check_vma=False
    )
```

```python
import functools
import math

import jax
import jax.numpy as jnp
import ml_dtypes
import numpy as np
from jax import lax
from jax.experimental import pallas as pl
from jax.experimental.pallas import tpu as pltpu
from jax.sharding import PartitionSpec as P

N = 1152
HALO = 64
KF = 64
NE = 1280
LANES = 128
PAIR = 2 * KF
BLOCKS = N // LANES
EDGE = PAIR
PACK = EDGE + KF + 16
BF16 = jnp.bfloat16
F32 = jnp.float32
VMEM_LIMIT = 32 * 1024 * 1024


def wave_tables():
    position = np.arange(NE)[:, None]
    frequency = np.arange(KF)[None, :] - KF // 2
    phase = np.mod(position * frequency, NE).astype(np.float64) * (2.0 * math.pi / NE)
    return np.cos(phase).astype(np.float32), np.sin(phase).astype(np.float32)


def transform_tables():
    cos, sin = wave_tables()
    full = np.concatenate([cos, sin], 1)
    mid = full[HALO : HALO + N]
    ct, st = cos[HALO : HALO + N].T, sin[HALO : HALO + N].T
    columns = np.concatenate(
        [
            np.stack([ct.reshape(KF, BLOCKS, LANES), st.reshape(KF, BLOCKS, LANES)], 2),
            np.stack([-st.reshape(KF, BLOCKS, LANES), ct.reshape(KF, BLOCKS, LANES)], 2),
        ],
        0,
    )
    to_columns = columns.transpose(1, 0, 2, 3).reshape(BLOCKS, PAIR, 2 * LANES)
    from_columns = to_columns.transpose(0, 2, 1)
    low, high = full[:HALO], full[HALO + N :]
    blank = np.zeros((HALO, PAIR), np.float32)
    rims = np.stack(
        [
            np.concatenate([blank, low[::-1]], 0),
            np.concatenate([blank, low], 0),
            np.concatenate([high[::-1], blank], 0),
            np.concatenate([high, blank], 0),
        ]
    )
    back = np.concatenate([cos.T, -sin.T], 0)
    back_low, back_high = back[:, :HALO], back[:, HALO + N :]
    blank = np.zeros((PAIR, HALO), np.float32)
    margins = np.stack(
        [
            np.concatenate([back_high[:, ::-1], blank], 1),
            np.concatenate([back_high, blank], 1),
            np.concatenate([blank, back_low[:, ::-1]], 1),
            np.concatenate([blank, back_low], 1),
        ]
    )
    tables = (mid, mid.T, to_columns, from_columns, rims, back[:, HALO : HALO + N], margins)
    return tuple(np.ascontiguousarray(one).astype(ml_dtypes.bfloat16) for one in tables)


def dot(a, b):
    return jnp.dot(a, b, preferred_element_type=F32)


def in_left_half(shape):
    return lax.broadcasted_iota(jnp.int32, shape, 1) < KF


def swap_halves(pair):
    return pltpu.roll(pair, KF, 1)


def call(body, name, outs, args, specs=None, grid=None, scratch=(), flops=0, moved=0):
    vmem = pl.BlockSpec(memory_space=pltpu.VMEM)
    extra = {} if grid is None else {"grid": grid}
    return pl.pallas_call(
        body,
        name=name,
        out_shape=outs,
        in_specs=specs,
        out_specs=jax.tree.map(lambda _: vmem, outs),
        scratch_shapes=list(scratch),
        compiler_params=pltpu.CompilerParams(vmem_limit_bytes=VMEM_LIMIT),
        cost_estimate=pl.CostEstimate(flops=flops, bytes_accessed=moved, transcendentals=0),
        **extra,
    )(*args)


def edges_body(
    mask, mid_t, real, imag, weight, flags, up, down, side, strips, table, pair, scalar, marks, sems
):
    copies = [
        pltpu.make_async_copy(mid_t, table, sems.at[0]),
        pltpu.make_async_copy(mask.at[:, N - LANES :], strips.at[:, :LANES], sems.at[1]),
        pltpu.make_async_copy(mask.at[:, :LANES], strips.at[:, LANES:], sems.at[2]),
        pltpu.make_async_copy(real.at[0], pair.at[0], sems.at[3]),
        pltpu.make_async_copy(imag.at[0], pair.at[1], sems.at[4]),
        pltpu.make_async_copy(weight, scalar, sems.at[5]),
        pltpu.make_async_copy(flags, marks, sems.at[6]),
    ]
    for copy in copies:
        copy.start()
    for copy in copies[3:]:
        copy.wait()
    scale = jnp.sqrt(jnp.full((KF, KF), 2.0 * scalar[0], F32)) * (1.0 / (NE * KF))
    kernel = jnp.concatenate([pair[0] * scale, pair[1] * scale], 1).astype(BF16)
    row = lax.broadcasted_iota(jnp.int32, (16, LANES), 0)
    sides = jnp.where(row == 0, marks[0, 0].astype(F32), marks[0, 1].astype(F32)).astype(BF16)
    side[...] = kernel
    for out in (up, down):
        out[EDGE : EDGE + KF, :] = kernel
        out[EDGE + KF :, :] = sides
    for copy in copies[:3]:
        copy.wait()
    both = dot(table[...], strips[...]).astype(BF16)
    up[:EDGE, :] = both[:, :LANES]
    down[:EDGE, :] = both[:, LANES:]


def middle_body(mask, mid, mid_t, out):
    rows = dot(mask[...], mid[...]).astype(BF16)
    part = dot(mid_t[...], rows)

    @pl.when(pl.program_id(0) == 0)
    def _():
        out[...] = part

    @pl.when(pl.program_id(0) > 0)
    def _():
        out[...] += part


def split_kernel(pair):
    left = in_left_half(pair.shape)
    other = swap_halves(pair)
    return jnp.where(left, pair, other), jnp.where(left, other, pair)


def fields_body(count, row_count, *refs):
    (flags, middle, target, mid, to_columns, from_columns, rims, own) = refs[:8]
    packs = refs[8 : 8 + count - 1]
    out, a_ref, e_ref, v_ref, u_ref = refs[8 + count - 1 :]
    tile = lax.axis_index("tile")
    tiles = lax.axis_size("tile")
    left = in_left_half((KF, PAIR))
    blocks = middle[...]
    low = jnp.where(flags[0, 0] == 1, rims[1], rims[0])
    low = jnp.where(tile == 0, jnp.zeros_like(low), low)
    high = jnp.where(flags[0, 1] == 1, rims[3], rims[2])
    high = jnp.where(tile == tiles - 1, jnp.zeros_like(high), high)
    blocks = blocks + dot(packs[0][:EDGE, :], low) + dot(packs[1][:EDGE, :], high)
    top, bottom = blocks[:KF], swap_halves(blocks[KF:])
    spectrum = jnp.where(left, top - bottom, -(top + bottom))
    turned = swap_halves(spectrum)
    turned = jnp.where(left, -turned, turned)
    kernels = [own[...].astype(F32)]
    for index, pack in enumerate(packs):
        start = EDGE if index < 2 else 0
        kernels.append(pack[start : start + KF, :].astype(F32))
    kernels = [split_kernel(one) for one in kernels]
    begin = pl.multiple_of(lax.axis_index("kern") * row_count, row_count)
    rows = mid[pl.ds(begin, row_count), :]
    for index, (real, imag) in enumerate(kernels):
        product = real * spectrum + imag * turned
        other = swap_halves(product)
        other = jnp.where(left, -other, other)
        stacked = jnp.concatenate([product, other], 0).astype(BF16)
        a_ref[index * row_count : (index + 1) * row_count, :] = dot(rows, stacked).astype(BF16)
    step = 32 if row_count % 32 == 0 else 16
    for block in range(BLOCKS):
        e_ref[...] = dot(a_ref[...], to_columns[block])
        for r in range(0, row_count, step):
            total = None
            parts = []
            for index in range(count):
                at = index * row_count + r
                real = e_ref[at : at + step, :LANES]
                imag = e_ref[at : at + step, LANES:]
                term = real * real + imag * imag
                total = term if total is None else total + term
            wanted = target[r : r + step, block * LANES : (block + 1) * LANES].astype(F32)
            bend = jnp.tanh(total - 2.0)
            slope = (bend + (1.0 - 2.0 * wanted)) * (1.0 - bend * bend)
            for index in range(count):
                at = index * row_count + r
                v_ref[at : at + step, :LANES] = (e_ref[at : at + step, :LANES] * slope).astype(BF16)
                v_ref[at : at + step, LANES:] = (e_ref[at : at + step, LANES:] * slope).astype(BF16)
        part = dot(v_ref[...], from_columns[block])
        if block == 0:
            u_ref[...] = part
        else:
            u_ref[...] += part
    wide = jnp.concatenate(
        [u_ref[i * row_count : (i + 1) * row_count, :].astype(BF16) for i in range(count)], 1
    )
    waves = lax.dot_general(rows, wide, (((0,), (0,)), ((), ())), preferred_element_type=F32)
    total = None
    for index, (real, imag) in enumerate(kernels):
        wave = waves[:, index * PAIR : (index + 1) * PAIR]
        top, bottom = wave[:KF], swap_halves(wave[KF:])
        wave = jnp.where(left, top + bottom, top - bottom)
        other = swap_halves(wave)
        other = jnp.where(left, other, -other)
        term = real * wave + imag * other
        total = term if total is None else total + term
    for index in range(count):
        out[index] = total.astype(BF16)


def sum_body(count, parts, out):
    total = parts[0].astype(F32)
    for index in range(1, count):
        total = total + parts[index].astype(F32)
    out[...] = total.astype(BF16)


def gradient_body(row_count, own, below, above, mark_below, mark_above, mid, back, margins, out):
    left = in_left_half((KF, PAIR))
    begin = pl.multiple_of(lax.axis_index("kern") * row_count, row_count)
    rows = mid[pl.ds(begin, row_count), :]
    waves = []
    for ref in (own, below, above):
        pair = ref[...].astype(F32)
        other = swap_halves(pair)
        other = jnp.where(left, -other, other)
        waves.append(dot(rows, jnp.concatenate([pair, other], 0).astype(BF16)).astype(BF16))
    low_mark = mark_below[EDGE + KF + 1 : EDGE + KF + 2, :].astype(F32)
    high_mark = mark_above[EDGE + KF : EDGE + KF + 1, :].astype(F32)
    low = jnp.where(low_mark == 1.0, margins[1].astype(F32), margins[0].astype(F32)).astype(BF16)
    high = jnp.where(high_mark == 1.0, margins[3].astype(F32), margins[2].astype(F32)).astype(BF16)
    out[:, :LANES] = dot(waves[0], back[:, :LANES]) + dot(waves[1], low)
    out[:, LANES : N - LANES] = dot(waves[0], back[:, LANES : N - LANES])
    out[:, N - LANES :] = dot(waves[0], back[:, N - LANES :]) + dot(waves[2], high)


def per_device(mask_pixels, orientation, target_pattern, kernel_real, kernel_imag, eigen_weights):
    tables = tuple(jnp.asarray(one) for one in transform_tables())
    mid, mid_t, to_columns, from_columns, rims, back, margins = tables
    tiles, count = lax.axis_size("tile"), lax.axis_size("kern")
    row_count = target_pattern.shape[0]
    vmem = pl.BlockSpec(memory_space=pltpu.VMEM)
    smem = pl.BlockSpec(memory_space=pltpu.SMEM)
    packed = jax.ShapeDtypeStruct((PACK, LANES), BF16)
    small = jax.ShapeDtypeStruct((KF, PAIR), BF16)

    up, down, side = call(
        edges_body,
        "edges",
        (packed, packed, small),
        (mask_pixels, mid_t, kernel_real, kernel_imag, eigen_weights, orientation),
        [pl.BlockSpec(memory_space=pltpu.HBM)] * 6,
        scratch=[
            pltpu.VMEM((N, 2 * LANES), BF16),
            pltpu.VMEM((PAIR, N), BF16),
            pltpu.VMEM((2, KF, KF), F32),
            pltpu.SMEM((1,), F32),
            pltpu.SMEM((1, 2), jnp.int32),
            pltpu.SemaphoreType.DMA((7,)),
        ],
        flops=2 * N * LANES * PAIR * 2,
        moved=N * LANES * 4,
    )

    def shifted(tile_step, kern_step):
        pairs = []
        for t in range(tiles):
            for k in range(count):
                there = ((t + tile_step) % tiles) * count + (k - kern_step) % count
                pairs.append((t * count + k, there))
        return pairs

    packs = []
    for kern_step in range(1, count):
        if kern_step <= 2:
            value, tile_step = ((up, 1), (down, -1))[kern_step - 1]
        else:
            value, tile_step = side, 0
        packs.append(lax.ppermute(value, ("tile", "kern"), shifted(tile_step, kern_step)))

    chunk = 384
    middle = call(
        middle_body,
        "middle",
        jax.ShapeDtypeStruct((PAIR, PAIR), F32),
        (mask_pixels, mid, mid_t),
        [
            pl.BlockSpec((chunk, N), lambda i: (i, 0)),
            vmem,
            pl.BlockSpec((PAIR, chunk), lambda i: (0, i)),
        ],
        grid=(N // chunk,),
        flops=4 * N * N * PAIR,
        moved=N * N * 2,
    )

    part = call(
        functools.partial(fields_body, count, row_count),
        "fields",
        jax.ShapeDtypeStruct((count, KF, PAIR), BF16),
        (orientation, middle, target_pattern, mid, to_columns, from_columns, rims, side, *packs),
        [smem] + [vmem] * (7 + count - 1),
        scratch=[
            pltpu.VMEM((count * row_count, PAIR), BF16),
            pltpu.VMEM((count * row_count, 2 * LANES), F32),
            pltpu.VMEM((count * row_count, 2 * LANES), BF16),
            pltpu.VMEM((count * row_count, PAIR), F32),
        ],
        flops=8 * count * row_count * N * PAIR,
        moved=4 * row_count * N,
    )

    parts = lax.all_to_all(part, "kern", 0, 0)
    own = call(functools.partial(sum_body, count), "total", small, (parts,), [vmem])
    forward = [(i, i + 1) for i in range(tiles - 1)]
    below = lax.ppermute(own, "tile", forward)
    above = lax.ppermute(own, "tile", [(target, source) for source, target in forward])
    return call(
        functools.partial(gradient_body, row_count),
        "gradient",
        jax.ShapeDtypeStruct((row_count, N), F32),
        (own, below, above, packs[0], packs[1], mid, back, margins),
        [vmem] * 8,
        flops=2 * row_count * PAIR * (N + 5 * PAIR),
        moved=4 * row_count * N,
    )


def solution(mesh):
    in_specs = (
        P(None, "tile"),
        P("tile", None),
        P("kern", "tile"),
        P("kern", None, None),
        P("kern", None, None),
        P("kern"),
    )
    out_specs = P("kern", "tile")
    return jax.shard_map(
        per_device, mesh=mesh, in_specs=in_specs, out_specs=out_specs, check_vma=False
    )
```

```python
import functools
import math

import jax
import jax.numpy as jnp
import ml_dtypes
import numpy as np
from jax import lax
from jax.experimental import pallas as pl
from jax.experimental.pallas import tpu as pltpu
from jax.sharding import PartitionSpec as P

N = 1152
HALO = 64
KF = 64
NE = 1280
LANES = 128
PAIR = 2 * KF
BLOCKS = N // LANES
EDGE = PAIR
PACK = EDGE + KF + 16
BF16 = jnp.bfloat16
F32 = jnp.float32
VMEM_LIMIT = 32 * 1024 * 1024
EDGES_LIMIT = 62 * 1024 * 1024
MIDDLE_LIMIT = 61 * 1024 * 1024


def wave_tables():
    position = np.arange(NE)[:, None]
    frequency = np.arange(KF)[None, :] - KF // 2
    phase = np.mod(position * frequency, NE).astype(np.float64) * (2.0 * math.pi / NE)
    return np.cos(phase).astype(np.float32), np.sin(phase).astype(np.float32)


def transform_tables():
    cos, sin = wave_tables()
    full = np.concatenate([cos, sin], 1)
    mid = full[HALO : HALO + N]
    ct, st = cos[HALO : HALO + N].T, sin[HALO : HALO + N].T
    columns = np.concatenate(
        [
            np.stack([ct.reshape(KF, BLOCKS, LANES), st.reshape(KF, BLOCKS, LANES)], 2),
            np.stack([-st.reshape(KF, BLOCKS, LANES), ct.reshape(KF, BLOCKS, LANES)], 2),
        ],
        0,
    )
    to_columns = columns.transpose(1, 0, 2, 3).reshape(BLOCKS, PAIR, 2 * LANES)
    from_columns = to_columns.transpose(0, 2, 1)
    low, high = full[:HALO], full[HALO + N :]
    blank = np.zeros((HALO, PAIR), np.float32)
    rims = np.stack(
        [
            np.concatenate([blank, low[::-1]], 0),
            np.concatenate([blank, low], 0),
            np.concatenate([high[::-1], blank], 0),
            np.concatenate([high, blank], 0),
        ]
    )
    back = np.concatenate([cos.T, -sin.T], 0)
    back_low, back_high = back[:, :HALO], back[:, HALO + N :]
    blank = np.zeros((PAIR, HALO), np.float32)
    margins = np.stack(
        [
            np.concatenate([back_high[:, ::-1], blank], 1),
            np.concatenate([back_high, blank], 1),
            np.concatenate([blank, back_low[:, ::-1]], 1),
            np.concatenate([blank, back_low], 1),
        ]
    )
    tables = (mid, mid.T, to_columns, from_columns, rims, back[:, HALO : HALO + N], margins)
    return tuple(np.ascontiguousarray(one).astype(ml_dtypes.bfloat16) for one in tables)


def dot(a, b):
    return jnp.dot(a, b, preferred_element_type=F32)


def in_left_half(shape):
    return lax.broadcasted_iota(jnp.int32, shape, 1) < KF


def swap_halves(pair):
    return pltpu.roll(pair, KF, 1)


def kern_steps(count):
    return (1, 3, 2) if count == 4 else range(1, count)


def destination(k, step, count):
    return k ^ step if count == 4 else (k - step) % count


def call(body, name, outs, args, specs=None, grid=None, scratch=(), flops=0, moved=0, vmem_bytes=VMEM_LIMIT):
    vmem = pl.BlockSpec(memory_space=pltpu.VMEM)
    extra = {} if grid is None else {"grid": grid}
    return pl.pallas_call(
        body,
        name=name,
        out_shape=outs,
        in_specs=specs,
        out_specs=jax.tree.map(lambda _: vmem, outs),
        scratch_shapes=list(scratch),
        compiler_params=pltpu.CompilerParams(vmem_limit_bytes=vmem_bytes),
        cost_estimate=pl.CostEstimate(flops=flops, bytes_accessed=moved, transcendentals=0),
        **extra,
    )(*args)


def edges_body(
    mask, mid_t, real, imag, weight, flags, mate, other, side, strips, table, pair, scalar, marks, sems
):
    odd = lax.rem(lax.axis_index("tile"), 2)
    facing = pl.multiple_of((1 - odd) * (N - LANES), LANES)
    facing_other = pl.multiple_of(odd * (N - LANES), LANES)
    copies = [
        pltpu.make_async_copy(mid_t, table, sems.at[0]),
        pltpu.make_async_copy(mask.at[:, pl.ds(facing, LANES)], strips.at[:, :LANES], sems.at[1]),
        pltpu.make_async_copy(mask.at[:, pl.ds(facing_other, LANES)], strips.at[:, LANES:], sems.at[2]),
        pltpu.make_async_copy(real.at[0], pair.at[0], sems.at[3]),
        pltpu.make_async_copy(imag.at[0], pair.at[1], sems.at[4]),
        pltpu.make_async_copy(weight, scalar, sems.at[5]),
        pltpu.make_async_copy(flags, marks, sems.at[6]),
    ]
    for copy in copies:
        copy.start()
    for copy in copies[3:]:
        copy.wait()
    scale = jnp.sqrt(jnp.full((KF, KF), 2.0 * scalar[0], F32)) * (1.0 / (NE * KF))
    kernel = jnp.concatenate([pair[0] * scale, pair[1] * scale], 1).astype(BF16)
    row = lax.broadcasted_iota(jnp.int32, (16, LANES), 0)
    sides = jnp.where(row == 0, marks[0, 0].astype(F32), marks[0, 1].astype(F32)).astype(BF16)
    side[...] = kernel
    for out in (mate, other):
        out[EDGE : EDGE + KF, :] = kernel
        out[EDGE + KF :, :] = sides
    for copy in copies[:3]:
        copy.wait()
    both = dot(table[...], strips[...]).astype(BF16)
    mate[:EDGE, :] = both[:, :LANES]
    other[:EDGE, :] = both[:, LANES:]


def middle_body(mask, mid, mid_t, out):
    rows = dot(mask[...], mid[...]).astype(BF16)
    part = dot(mid_t[...], rows)

    @pl.when(pl.program_id(0) == 0)
    def _():
        out[...] = part

    @pl.when(pl.program_id(0) > 0)
    def _():
        out[...] += part


def split_kernel(pair):
    left = in_left_half(pair.shape)
    other = swap_halves(pair)
    return jnp.where(left, pair, other), jnp.where(left, other, pair)


def fields_body(count, row_count, *refs):
    (flags, middle, target, mid, to_columns, from_columns, rims, own) = refs[:8]
    packs = refs[8 : 8 + count - 1]
    out, a_ref, e_ref, v_ref, u_ref = refs[8 + count - 1 :]
    tile = lax.axis_index("tile")
    tiles = lax.axis_size("tile")
    left = in_left_half((KF, PAIR))
    blocks = middle[...]
    low = jnp.where(flags[0, 0] == 1, rims[1], rims[0])
    low = jnp.where(tile == 0, jnp.zeros_like(low), low)
    high = jnp.where(flags[0, 1] == 1, rims[3], rims[2])
    high = jnp.where(tile == tiles - 1, jnp.zeros_like(high), high)
    odd = lax.rem(tile, 2) == 1
    low, high = jnp.where(odd, low, high), jnp.where(odd, high, low)
    blocks = blocks + dot(packs[1][:EDGE, :], low) + dot(packs[0][:EDGE, :], high)
    top, bottom = blocks[:KF], swap_halves(blocks[KF:])
    spectrum = jnp.where(left, top - bottom, -(top + bottom))
    turned = swap_halves(spectrum)
    turned = jnp.where(left, -turned, turned)
    kernels = [own[...].astype(F32)]
    for index, pack in enumerate(packs):
        start = EDGE if index < 2 else 0
        kernels.append(pack[start : start + KF, :].astype(F32))
    kernels = [split_kernel(one) for one in kernels]
    begin = pl.multiple_of(lax.axis_index("kern") * row_count, row_count)
    rows = mid[pl.ds(begin, row_count), :]
    for index, (real, imag) in enumerate(kernels):
        product = real * spectrum + imag * turned
        other = swap_halves(product)
        other = jnp.where(left, -other, other)
        stacked = jnp.concatenate([product, other], 0).astype(BF16)
        a_ref[index * row_count : (index + 1) * row_count, :] = dot(rows, stacked).astype(BF16)
    step = 32 if row_count % 32 == 0 else 16
    e_ref[0] = dot(a_ref[...], to_columns[0])
    for block in range(BLOCKS):
        now = block % 2
        if block + 1 < BLOCKS:
            e_ref[1 - now] = dot(a_ref[...], to_columns[block + 1])
        for r in range(0, row_count, step):
            total = None
            for index in range(count):
                at = index * row_count + r
                real = e_ref[now, at : at + step, :LANES]
                imag = e_ref[now, at : at + step, LANES:]
                term = real * real + imag * imag
                total = term if total is None else total + term
            wanted = target[r : r + step, block * LANES : (block + 1) * LANES].astype(F32)
            bend = jnp.tanh(total - 2.0)
            slope = (bend + (1.0 - 2.0 * wanted)) * (1.0 - bend * bend)
            for index in range(count):
                at = index * row_count + r
                for half in (slice(0, LANES), slice(LANES, 2 * LANES)):
                    field = e_ref[now, at : at + step, half]
                    v_ref[now, at : at + step, half] = (field * slope).astype(BF16)
        part = dot(v_ref[now], from_columns[block])
        if block == 0:
            u_ref[...] = part
        else:
            u_ref[...] += part
    wide = jnp.concatenate(
        [u_ref[i * row_count : (i + 1) * row_count, :].astype(BF16) for i in range(count)], 1
    )
    waves = lax.dot_general(rows, wide, (((0,), (0,)), ((), ())), preferred_element_type=F32)
    total = None
    for index, (real, imag) in enumerate(kernels):
        wave = waves[:, index * PAIR : (index + 1) * PAIR]
        top, bottom = wave[:KF], swap_halves(wave[KF:])
        wave = jnp.where(left, top + bottom, top - bottom)
        other = swap_halves(wave)
        other = jnp.where(left, other, -other)
        term = real * wave + imag * other
        total = term if total is None else total + term
    out[...] = total.astype(BF16)


def sum_body(count, *refs):
    total = refs[0][...].astype(F32)
    for one in refs[1:count]:
        total = total + one[...].astype(F32)
    refs[count][...] = total.astype(BF16)


def gradient_body(row_count, own, near, far, near_pack, far_pack, mid, back, margins, out):
    left = in_left_half((KF, PAIR))
    begin = pl.multiple_of(lax.axis_index("kern") * row_count, row_count)
    rows = mid[pl.ds(begin, row_count), :]
    waves = []
    for ref in (own, near, far):
        pair = ref[...].astype(F32)
        other = swap_halves(pair)
        other = jnp.where(left, -other, other)
        waves.append(dot(rows, jnp.concatenate([pair, other], 0).astype(BF16)).astype(BF16))
    odd = lax.rem(lax.axis_index("tile"), 2) == 1
    below, above = jnp.where(odd, waves[1], waves[2]), jnp.where(odd, waves[2], waves[1])
    near_marks = near_pack[EDGE + KF :, :].astype(F32)
    far_marks = far_pack[EDGE + KF :, :].astype(F32)
    low_mark = jnp.where(odd, near_marks, far_marks)[1:2]
    high_mark = jnp.where(odd, far_marks, near_marks)[0:1]
    low = jnp.where(low_mark == 1.0, margins[1].astype(F32), margins[0].astype(F32)).astype(BF16)
    high = jnp.where(high_mark == 1.0, margins[3].astype(F32), margins[2].astype(F32)).astype(BF16)
    out[:, :LANES] = dot(waves[0], back[:, :LANES]) + dot(below, low)
    out[:, LANES : N - LANES] = dot(waves[0], back[:, LANES : N - LANES])
    out[:, N - LANES :] = dot(waves[0], back[:, N - LANES :]) + dot(above, high)


def per_device(mask_pixels, orientation, target_pattern, kernel_real, kernel_imag, eigen_weights):
    tables = tuple(jnp.asarray(one) for one in transform_tables())
    mid, mid_t, to_columns, from_columns, rims, back, margins = tables
    tiles, count = lax.axis_size("tile"), lax.axis_size("kern")
    row_count = target_pattern.shape[0]
    vmem = pl.BlockSpec(memory_space=pltpu.VMEM)
    smem = pl.BlockSpec(memory_space=pltpu.SMEM)
    packed = jax.ShapeDtypeStruct((PACK, LANES), BF16)
    small = jax.ShapeDtypeStruct((KF, PAIR), BF16)

    mate, other, side = call(
        edges_body,
        "edges",
        (packed, packed, small),
        (mask_pixels, mid_t, kernel_real, kernel_imag, eigen_weights, orientation),
        [pl.BlockSpec(memory_space=pltpu.HBM)] * 6,
        scratch=[
            pltpu.VMEM((N, 2 * LANES), BF16),
            pltpu.VMEM((PAIR, N), BF16),
            pltpu.VMEM((2, KF, KF), F32),
            pltpu.SMEM((1,), F32),
            pltpu.SMEM((1, 2), jnp.int32),
            pltpu.SemaphoreType.DMA((7,)),
        ],
        flops=2 * N * LANES * PAIR * 2,
        moved=N * LANES * 4,
        vmem_bytes=EDGES_LIMIT,
    )

    def swapped(move_tile, step):
        pairs = []
        for t in range(tiles):
            for k in range(count):
                pairs.append((t * count + k, move_tile(t) * count + destination(k, step, count)))
        return pairs

    def chip_mate(t):
        return t ^ 1

    def other_side(t):
        return (t + 1 if t % 2 else t - 1) % tiles

    packs = []
    for step in kern_steps(count):
        value, move_tile = {0: (other, other_side), 1: (mate, chip_mate)}.get(
            len(packs), (side, lambda t: t)
        )
        packs.append(lax.ppermute(value, ("tile", "kern"), swapped(move_tile, step)))

    chunk = 384
    middle = call(
        middle_body,
        "middle",
        jax.ShapeDtypeStruct((PAIR, PAIR), F32),
        (mask_pixels, mid, mid_t),
        [
            pl.BlockSpec((chunk, N), lambda i: (i, 0)),
            vmem,
            pl.BlockSpec((PAIR, chunk), lambda i: (0, i)),
        ],
        grid=(N // chunk,),
        flops=4 * N * N * PAIR,
        moved=N * N * 2,
        vmem_bytes=MIDDLE_LIMIT,
    )

    part = call(
        functools.partial(fields_body, count, row_count),
        "fields",
        small,
        (orientation, middle, target_pattern, mid, to_columns, from_columns, rims, side, *packs),
        [smem] + [vmem] * (7 + count - 1),
        scratch=[
            pltpu.VMEM((count * row_count, PAIR), BF16),
            pltpu.VMEM((2, count * row_count, 2 * LANES), F32),
            pltpu.VMEM((2, count * row_count, 2 * LANES), BF16),
            pltpu.VMEM((count * row_count, PAIR), F32),
        ],
        flops=8 * count * row_count * N * PAIR,
        moved=4 * row_count * N,
    )

    parts = [part]
    for step in kern_steps(count):
        pairs = [(k, destination(k, step, count)) for k in range(count)]
        parts.append(lax.ppermute(part, "kern", pairs))
    own = call(functools.partial(sum_body, count), "total", small, tuple(parts), [vmem] * count)
    near = lax.ppermute(own, "tile", [(t, chip_mate(t)) for t in range(tiles)])
    inner = [t for t in range(tiles) if 0 < t < tiles - 1]
    far = lax.ppermute(own, "tile", [(t, other_side(t)) for t in inner])
    return call(
        functools.partial(gradient_body, row_count),
        "gradient",
        jax.ShapeDtypeStruct((row_count, N), F32),
        (own, near, far, packs[1], packs[0], mid, back, margins),
        [vmem] * 8,
        flops=2 * row_count * PAIR * (N + 5 * PAIR),
        moved=4 * row_count * N,
    )


def solution(mesh):
    in_specs = (
        P(None, "tile"),
        P("tile", None),
        P("kern", "tile"),
        P("kern", None, None),
        P("kern", None, None),
        P("kern"),
    )
    out_specs = P("kern", "tile")
    return jax.shard_map(
        per_device, mesh=mesh, in_specs=in_specs, out_specs=out_specs, check_vma=False
    )
```

```python
import functools
import math

import jax
import jax.numpy as jnp
import ml_dtypes
import numpy as np
from jax import lax
from jax.experimental import pallas as pl
from jax.experimental.pallas import tpu as pltpu
from jax.sharding import PartitionSpec as P

N = 1152
HALO = 64
KF = 64
NE = 1280
LANES = 128
PAIR = 2 * KF
BLOCKS = N // LANES
EDGE = PAIR
PACK = EDGE + KF + 16
BF16 = jnp.bfloat16
F32 = jnp.float32
VMEM_LIMIT = 32 * 1024 * 1024


def wave_tables():
    position = np.arange(NE)[:, None]
    frequency = np.arange(KF)[None, :] - KF // 2
    phase = np.mod(position * frequency, NE).astype(np.float64) * (2.0 * math.pi / NE)
    return np.cos(phase).astype(np.float32), np.sin(phase).astype(np.float32)


def transform_tables():
    cos, sin = wave_tables()
    full = np.concatenate([cos, sin], 1)
    mid = full[HALO : HALO + N]
    ct, st = cos[HALO : HALO + N].T, sin[HALO : HALO + N].T
    columns = np.concatenate(
        [
            np.stack([ct.reshape(KF, BLOCKS, LANES), st.reshape(KF, BLOCKS, LANES)], 2),
            np.stack([-st.reshape(KF, BLOCKS, LANES), ct.reshape(KF, BLOCKS, LANES)], 2),
        ],
        0,
    )
    to_columns = columns.transpose(1, 0, 2, 3).reshape(BLOCKS, PAIR, 2 * LANES)
    from_columns = to_columns.transpose(0, 2, 1)
    low, high = full[:HALO], full[HALO + N :]
    blank = np.zeros((HALO, PAIR), np.float32)
    rims = np.stack(
        [
            np.concatenate([blank, low[::-1]], 0),
            np.concatenate([blank, low], 0),
            np.concatenate([high[::-1], blank], 0),
            np.concatenate([high, blank], 0),
        ]
    )
    back = np.concatenate([cos.T, -sin.T], 0)
    back_low, back_high = back[:, :HALO], back[:, HALO + N :]
    blank = np.zeros((PAIR, HALO), np.float32)
    margins = np.stack(
        [
            np.concatenate([back_high[:, ::-1], blank], 1),
            np.concatenate([back_high, blank], 1),
            np.concatenate([blank, back_low[:, ::-1]], 1),
            np.concatenate([blank, back_low], 1),
        ]
    )
    tables = (mid, mid.T, to_columns, from_columns, rims, back[:, HALO : HALO + N], margins)
    return tuple(np.ascontiguousarray(one).astype(ml_dtypes.bfloat16) for one in tables)


def dot(a, b):
    return jnp.dot(a, b, preferred_element_type=F32)


def in_left_half(shape):
    return lax.broadcasted_iota(jnp.int32, shape, 1) < KF


def swap_halves(pair):
    return pltpu.roll(pair, KF, 1)


def kern_steps(count):
    return (1, 3, 2) if count == 4 else range(1, count)


def destination(k, step, count):
    return k ^ step if count == 4 else (k - step) % count


def call(body, name, outs, args, specs=None, grid=None, scratch=(), flops=0, moved=0, vmem_bytes=VMEM_LIMIT):
    vmem = pl.BlockSpec(memory_space=pltpu.VMEM)
    extra = {} if grid is None else {"grid": grid}
    return pl.pallas_call(
        body,
        name=name,
        out_shape=outs,
        in_specs=specs,
        out_specs=jax.tree.map(lambda _: vmem, outs),
        scratch_shapes=list(scratch),
        compiler_params=pltpu.CompilerParams(vmem_limit_bytes=vmem_bytes),
        cost_estimate=pl.CostEstimate(flops=flops, bytes_accessed=moved, transcendentals=0),
        **extra,
    )(*args)


def edges_body(
    mask, mid, mid_t, real, imag, weight, flags, mate, other, side, held, tall, table, pair, marks, sems
):
    odd = lax.rem(lax.axis_index("tile"), 2) == 1
    copies = [
        pltpu.make_async_copy(mid_t, table, sems.at[0]),
        pltpu.make_async_copy(mask.at[:, :LANES], held.at[:, :LANES], sems.at[1]),
        pltpu.make_async_copy(mask.at[:, N - LANES :], held.at[:, N - LANES :], sems.at[2]),
        pltpu.make_async_copy(real.at[0], pair.at[0], sems.at[3]),
        pltpu.make_async_copy(imag.at[0], pair.at[1], sems.at[4]),
        pltpu.make_async_copy(flags, marks, sems.at[5]),
    ]
    inner = pltpu.make_async_copy(
        mask.at[:, LANES : N - LANES], held.at[:, LANES : N - LANES], sems.at[6]
    )
    columns = pltpu.make_async_copy(mid, tall, sems.at[7])
    for copy in copies:
        copy.start()
    inner.start()
    columns.start()
    for copy in copies[3:]:
        copy.wait()
    scale = jnp.sqrt(jnp.full((KF, KF), 2.0 * weight[0], F32)) * (1.0 / (NE * KF))
    kernel = jnp.concatenate([pair[0] * scale, pair[1] * scale], 1).astype(BF16)
    row = lax.broadcasted_iota(jnp.int32, (16, LANES), 0)
    sides = jnp.where(row == 0, marks[0, 0].astype(F32), marks[0, 1].astype(F32)).astype(BF16)
    side[...] = kernel
    for out in (mate, other):
        out[EDGE : EDGE + KF, :] = kernel
        out[EDGE + KF :, :] = sides
    for copy in copies[:3]:
        copy.wait()
    strips = jnp.concatenate([held[:, :LANES], held[:, N - LANES :]], 1)
    both = dot(table[...], strips)
    first, last = both[:, :LANES], both[:, LANES:]
    mate[:EDGE, :] = jnp.where(odd, first, last).astype(BF16)
    other[:EDGE, :] = jnp.where(odd, last, first).astype(BF16)
    inner.wait()
    columns.wait()


def middle_body(mask, mid, mid_t, out):
    out[...] = dot(mid_t[...], dot(mask[...], mid[...]).astype(BF16))


def split_kernel(pair):
    left = in_left_half(pair.shape)
    other = swap_halves(pair)
    return jnp.where(left, pair, other), jnp.where(left, other, pair)


def fields_body(count, row_count, *refs):
    (flags, middle, target, mid, to_columns, from_columns, rims, own) = refs[:8]
    packs = refs[8 : 8 + count - 1]
    out, a_ref, e_ref, v_ref, u_ref = refs[8 + count - 1 :]
    tile = lax.axis_index("tile")
    tiles = lax.axis_size("tile")
    left = in_left_half((KF, PAIR))
    blocks = middle[...]
    low = jnp.where(flags[0, 0] == 1, rims[1], rims[0])
    low = jnp.where(tile == 0, jnp.zeros_like(low), low)
    high = jnp.where(flags[0, 1] == 1, rims[3], rims[2])
    high = jnp.where(tile == tiles - 1, jnp.zeros_like(high), high)
    odd = lax.rem(tile, 2) == 1
    low, high = jnp.where(odd, low, high), jnp.where(odd, high, low)
    blocks = blocks + dot(packs[1][:EDGE, :], low) + dot(packs[0][:EDGE, :], high)
    top, bottom = blocks[:KF], swap_halves(blocks[KF:])
    spectrum = jnp.where(left, top - bottom, -(top + bottom))
    turned = swap_halves(spectrum)
    turned = jnp.where(left, -turned, turned)
    kernels = [own[...].astype(F32)]
    for index, pack in enumerate(packs):
        start = EDGE if index < 2 else 0
        kernels.append(pack[start : start + KF, :].astype(F32))
    kernels = [split_kernel(one) for one in kernels]
    begin = pl.multiple_of(lax.axis_index("kern") * row_count, row_count)
    rows = mid[pl.ds(begin, row_count), :]
    for index, (real, imag) in enumerate(kernels):
        product = real * spectrum + imag * turned
        other = swap_halves(product)
        other = jnp.where(left, -other, other)
        stacked = jnp.concatenate([product, other], 0).astype(BF16)
        a_ref[index * row_count : (index + 1) * row_count, :] = dot(rows, stacked).astype(BF16)
    step = 32 if row_count % 32 == 0 else 16
    e_ref[0] = dot(a_ref[...], to_columns[0])
    for block in range(BLOCKS):
        now = block % 2
        if block + 1 < BLOCKS:
            e_ref[1 - now] = dot(a_ref[...], to_columns[block + 1])
        for r in range(0, row_count, step):
            total = None
            for index in range(count):
                at = index * row_count + r
                real = e_ref[now, at : at + step, :LANES]
                imag = e_ref[now, at : at + step, LANES:]
                term = real * real + imag * imag
                total = term if total is None else total + term
            wanted = target[r : r + step, block * LANES : (block + 1) * LANES].astype(F32)
            bend = jnp.tanh(total - 2.0)
            slope = (bend + (1.0 - 2.0 * wanted)) * (1.0 - bend * bend)
            for index in range(count):
                at = index * row_count + r
                for half in (slice(0, LANES), slice(LANES, 2 * LANES)):
                    field = e_ref[now, at : at + step, half]
                    v_ref[now, at : at + step, half] = (field * slope).astype(BF16)
        part = dot(v_ref[now], from_columns[block])
        if block == 0:
            u_ref[...] = part
        else:
            u_ref[...] += part
    wide = jnp.concatenate(
        [u_ref[i * row_count : (i + 1) * row_count, :].astype(BF16) for i in range(count)], 1
    )
    waves = lax.dot_general(rows, wide, (((0,), (0,)), ((), ())), preferred_element_type=F32)
    total = None
    for index, (real, imag) in enumerate(kernels):
        wave = waves[:, index * PAIR : (index + 1) * PAIR]
        top, bottom = wave[:KF], swap_halves(wave[KF:])
        wave = jnp.where(left, top + bottom, top - bottom)
        other = swap_halves(wave)
        other = jnp.where(left, other, -other)
        term = real * wave + imag * other
        total = term if total is None else total + term
    out[...] = total.astype(BF16)


def sum_body(count, *refs):
    total = refs[0][...].astype(F32)
    for one in refs[1:count]:
        total = total + one[...].astype(F32)
    refs[count][...] = total.astype(BF16)


def gradient_body(row_count, own, near, far, near_pack, far_pack, mid, back, margins, out):
    left = in_left_half((KF, PAIR))
    begin = pl.multiple_of(lax.axis_index("kern") * row_count, row_count)
    rows = mid[pl.ds(begin, row_count), :]
    waves = []
    for ref in (own, near, far):
        pair = ref[...].astype(F32)
        other = swap_halves(pair)
        other = jnp.where(left, -other, other)
        waves.append(dot(rows, jnp.concatenate([pair, other], 0).astype(BF16)).astype(BF16))
    odd = lax.rem(lax.axis_index("tile"), 2) == 1
    below, above = jnp.where(odd, waves[1], waves[2]), jnp.where(odd, waves[2], waves[1])
    near_marks = near_pack[EDGE + KF :, :].astype(F32)
    far_marks = far_pack[EDGE + KF :, :].astype(F32)
    low_mark = jnp.where(odd, near_marks, far_marks)[1:2]
    high_mark = jnp.where(odd, far_marks, near_marks)[0:1]
    low = jnp.where(low_mark == 1.0, margins[1].astype(F32), margins[0].astype(F32)).astype(BF16)
    high = jnp.where(high_mark == 1.0, margins[3].astype(F32), margins[2].astype(F32)).astype(BF16)
    out[:, :LANES] = dot(waves[0], back[:, :LANES]) + dot(below, low)
    out[:, LANES : N - LANES] = dot(waves[0], back[:, LANES : N - LANES])
    out[:, N - LANES :] = dot(waves[0], back[:, N - LANES :]) + dot(above, high)


def far_off(array):
    return pltpu.with_memory_space_constraint(array, pltpu.HBM)


def per_device(mask_pixels, orientation, target_pattern, kernel_real, kernel_imag, eigen_weights):
    tables = tuple(jnp.asarray(one) for one in transform_tables())
    mid, mid_t, to_columns, from_columns, rims, back, margins = tables
    tiles, count = lax.axis_size("tile"), lax.axis_size("kern")
    row_count = target_pattern.shape[0]
    vmem = pl.BlockSpec(memory_space=pltpu.VMEM)
    smem = pl.BlockSpec(memory_space=pltpu.SMEM)
    hbm = pl.BlockSpec(memory_space=pltpu.HBM)
    packed = jax.ShapeDtypeStruct((PACK, LANES), BF16)
    small = jax.ShapeDtypeStruct((KF, PAIR), BF16)

    mate, other, side, held, mid, mid_t = call(
        edges_body,
        "edges",
        (
            pltpu.VMEM((PACK, LANES), BF16),
            pltpu.VMEM((PACK, LANES), BF16),
            pltpu.VMEM((KF, PAIR), BF16),
            pltpu.VMEM((N, N), BF16),
            pltpu.VMEM((N, PAIR), BF16),
            pltpu.VMEM((PAIR, N), BF16),
        ),
        (
            *(far_off(one) for one in (mask_pixels, mid, mid_t, kernel_real, kernel_imag)),
            eigen_weights,
            far_off(orientation),
        ),
        [hbm] * 5 + [smem, hbm],
        scratch=[
            pltpu.VMEM((2, KF, KF), F32),
            pltpu.SMEM((1, 2), jnp.int32),
            pltpu.SemaphoreType.DMA((8,)),
        ],
        flops=2 * N * LANES * PAIR * 2,
        moved=N * LANES * 4,
    )

    def swapped(move_tile, step):
        pairs = []
        for t in range(tiles):
            for k in range(count):
                pairs.append((t * count + k, move_tile(t) * count + destination(k, step, count)))
        return pairs

    def chip_mate(t):
        return t ^ 1

    def other_side(t):
        return (t + 1 if t % 2 else t - 1) % tiles

    packs = []
    for step in kern_steps(count):
        value, move_tile = {0: (other, other_side), 1: (mate, chip_mate)}.get(
            len(packs), (side, lambda t: t)
        )
        packs.append(lax.ppermute(value, ("tile", "kern"), swapped(move_tile, step)))

    middle = call(
        middle_body,
        "middle",
        jax.ShapeDtypeStruct((PAIR, PAIR), F32),
        (held, mid, mid_t),
        [vmem] * 3,
        flops=4 * N * N * PAIR,
        moved=N * N * 2,
    )

    part = call(
        functools.partial(fields_body, count, row_count),
        "fields",
        small,
        (orientation, middle, target_pattern, mid, to_columns, from_columns, rims, side, *packs),
        [smem] + [vmem] * (7 + count - 1),
        scratch=[
            pltpu.VMEM((count * row_count, PAIR), BF16),
            pltpu.VMEM((2, count * row_count, 2 * LANES), F32),
            pltpu.VMEM((2, count * row_count, 2 * LANES), BF16),
            pltpu.VMEM((count * row_count, PAIR), F32),
        ],
        flops=8 * count * row_count * N * PAIR,
        moved=4 * row_count * N,
    )

    parts = [part]
    for step in kern_steps(count):
        pairs = [(k, destination(k, step, count)) for k in range(count)]
        parts.append(lax.ppermute(part, "kern", pairs))
    own = call(functools.partial(sum_body, count), "total", small, tuple(parts), [vmem] * count)
    near = lax.ppermute(own, "tile", [(t, chip_mate(t)) for t in range(tiles)])
    inner = [t for t in range(tiles) if 0 < t < tiles - 1]
    far = lax.ppermute(own, "tile", [(t, other_side(t)) for t in inner])
    return call(
        functools.partial(gradient_body, row_count),
        "gradient",
        jax.ShapeDtypeStruct((row_count, N), F32),
        (own, near, far, packs[1], packs[0], mid, back, margins),
        [vmem] * 8,
        flops=2 * row_count * PAIR * (N + 5 * PAIR),
        moved=4 * row_count * N,
    )


def solution(mesh):
    in_specs = (
        P(None, "tile"),
        P("tile", None),
        P("kern", "tile"),
        P("kern", None, None),
        P("kern", None, None),
        P("kern"),
    )
    out_specs = P("kern", "tile")
    return jax.shard_map(
        per_device, mesh=mesh, in_specs=in_specs, out_specs=out_specs, check_vma=False
    )
```

```python
import functools
import math

import jax
import jax.numpy as jnp
import ml_dtypes
import numpy as np
from jax import lax
from jax.experimental import pallas as pl
from jax.experimental.pallas import tpu as pltpu
from jax.sharding import PartitionSpec as P

N = 1152
HALO = 64
KF = 64
NE = 1280
LANES = 128
PAIR = 2 * KF
BLOCKS = N // LANES
EDGE = KF
WIDE = 3
PACK = EDGE + KF + 16
BF16 = jnp.bfloat16
F32 = jnp.float32
VMEM_LIMIT = 32 * 1024 * 1024


def wave_tables():
    position = np.arange(NE)[:, None]
    frequency = np.arange(KF)[None, :] - KF // 2
    phase = np.mod(position * frequency, NE).astype(np.float64) * (2.0 * math.pi / NE)
    return np.cos(phase).astype(np.float32), np.sin(phase).astype(np.float32)


def transform_tables():
    cos, sin = wave_tables()
    full = np.concatenate([cos, sin], 1)
    mid = full[HALO : HALO + N]
    ct, st = cos[HALO : HALO + N].T, sin[HALO : HALO + N].T
    columns = np.concatenate(
        [
            np.stack([ct.reshape(KF, BLOCKS, LANES), st.reshape(KF, BLOCKS, LANES)], 2),
            np.stack([-st.reshape(KF, BLOCKS, LANES), ct.reshape(KF, BLOCKS, LANES)], 2),
        ],
        0,
    )
    to_columns = columns.transpose(1, 0, 2, 3).reshape(BLOCKS, PAIR, 2 * LANES)
    from_columns = to_columns.transpose(0, 2, 1).reshape(BLOCKS // WIDE, WIDE * 2 * LANES, PAIR)
    low, high = full[:HALO], full[HALO + N :]
    blank = np.zeros((HALO, PAIR), np.float32)
    rims = np.stack(
        [
            np.concatenate([low[::-1], blank], 0),
            np.concatenate([low, blank], 0),
            np.concatenate([high[::-1], blank], 0),
            np.concatenate([high, blank], 0),
        ]
    )
    back = np.concatenate([cos.T, -sin.T], 0)
    back_low, back_high = back[:, :HALO], back[:, HALO + N :]
    blank = np.zeros((PAIR, HALO), np.float32)
    margins = np.stack(
        [
            np.concatenate([back_high[:, ::-1], blank], 1),
            np.concatenate([back_high, blank], 1),
            np.concatenate([blank, back_low[:, ::-1]], 1),
            np.concatenate([blank, back_low], 1),
        ]
    )
    tables = (mid, mid.T, to_columns, from_columns, rims, back[:, HALO : HALO + N], margins)
    return tuple(np.ascontiguousarray(one).astype(ml_dtypes.bfloat16) for one in tables)


def dot(a, b):
    return jnp.dot(a, b, preferred_element_type=F32)


def in_left_half(shape):
    return lax.broadcasted_iota(jnp.int32, shape, 1) < KF


def swap_halves(pair):
    return pltpu.roll(pair, KF, 1)


def kern_steps(count):
    return (1, 3, 2) if count == 4 else range(1, count)


def destination(k, step, count):
    return k ^ step if count == 4 else (k - step) % count


def call(
    body, name, outs, args, specs, out_specs=None, scratch=(), flops=0, moved=0, alias=None
):
    vmem = pl.BlockSpec(memory_space=pltpu.VMEM)
    if out_specs is None:
        out_specs = tuple(vmem for _ in outs) if isinstance(outs, tuple) else vmem
    return pl.pallas_call(
        body,
        name=name,
        out_shape=outs,
        in_specs=specs,
        out_specs=out_specs,
        scratch_shapes=list(scratch),
        input_output_aliases=alias or {},
        compiler_params=pltpu.CompilerParams(vmem_limit_bytes=VMEM_LIMIT),
        cost_estimate=pl.CostEstimate(flops=flops, bytes_accessed=moved, transcendentals=0),
    )(*args)


def edges_body(
    mask, mid, mid_t, real, imag, weight, flags, mate, other, side, held, tall, table, pair, marks, sems
):
    odd = lax.rem(lax.axis_index("tile"), 2) == 1
    copies = [
        pltpu.make_async_copy(mid_t, table, sems.at[0]),
        pltpu.make_async_copy(mask.at[:, :LANES], held.at[:, :LANES], sems.at[1]),
        pltpu.make_async_copy(mask.at[:, N - LANES :], held.at[:, N - LANES :], sems.at[2]),
        pltpu.make_async_copy(real.at[0], pair.at[0], sems.at[3]),
        pltpu.make_async_copy(imag.at[0], pair.at[1], sems.at[4]),
        pltpu.make_async_copy(flags, marks, sems.at[5]),
    ]
    inner = pltpu.make_async_copy(
        mask.at[:, LANES : N - LANES], held.at[:, LANES : N - LANES], sems.at[6]
    )
    columns = pltpu.make_async_copy(mid, tall, sems.at[7])
    for copy in copies:
        copy.start()
    inner.start()
    columns.start()
    for copy in copies[3:]:
        copy.wait()
    scale = jnp.sqrt(jnp.full((KF, KF), 2.0 * weight[0], F32)) * (1.0 / (NE * KF))
    kernel = jnp.concatenate([pair[0] * scale, pair[1] * scale], 1).astype(BF16)
    row = lax.broadcasted_iota(jnp.int32, (16, LANES), 0)
    sides = jnp.where(row == 0, marks[0, 0].astype(F32), marks[0, 1].astype(F32)).astype(BF16)
    side[...] = kernel
    for out in (mate, other):
        out[EDGE : EDGE + KF, :] = kernel
        out[EDGE + KF :, :] = sides
    for copy in copies[:3]:
        copy.wait()
    strips = jnp.concatenate([held[:, :LANES], held[:, N - LANES :]], 1)
    both = dot(table[...], strips)
    left = in_left_half((KF, LANES))
    first, last = both[:, :LANES], both[:, LANES:]
    first = jnp.where(left, first[:KF], swap_halves(first[KF:]))
    last = jnp.where(left, swap_halves(last[:KF]), last[KF:])
    mate[:EDGE, :] = jnp.where(odd, first, last).astype(BF16)
    other[:EDGE, :] = jnp.where(odd, last, first).astype(BF16)
    inner.wait()
    columns.wait()


def middle_body(mask, mid, mid_t, out):
    out[...] = dot(mid_t[...], dot(mask[...], mid[...]).astype(BF16))


def split_kernel(pair):
    left = in_left_half(pair.shape)
    other = swap_halves(pair)
    return jnp.where(left, pair, other), jnp.where(left, other, pair)


def fields_body(count, row_count, *refs):
    (flags, middle, target, mid, to_columns, from_columns, rims, own) = refs[:8]
    packs = refs[8 : 8 + count - 1]
    out, a_ref, e_ref, v_ref, u_ref = refs[8 + count - 1 :]
    tile = lax.axis_index("tile")
    tiles = lax.axis_size("tile")
    left = in_left_half((KF, PAIR))
    blocks = middle[...]
    low = jnp.where(flags[0, 0] == 1, rims[1], rims[0])
    low = jnp.where(tile == 0, jnp.zeros_like(low), low)
    high = jnp.where(flags[0, 1] == 1, rims[3], rims[2])
    high = jnp.where(tile == tiles - 1, jnp.zeros_like(high), high)
    odd = lax.rem(tile, 2) == 1
    low, high = jnp.where(odd, low, high), jnp.where(odd, high, low)
    for pack, table in ((packs[1], low), (packs[0], high)):
        edge = pack[:EDGE, :].astype(F32)
        edge = jnp.concatenate([edge, swap_halves(edge)], 0).astype(BF16)
        blocks = blocks + dot(edge, table)
    top, bottom = blocks[:KF], swap_halves(blocks[KF:])
    spectrum = jnp.where(left, top - bottom, -(top + bottom))
    turned = swap_halves(spectrum)
    turned = jnp.where(left, -turned, turned)
    kernels = [own[...].astype(F32)]
    for index, pack in enumerate(packs):
        start = EDGE if index < 2 else 0
        kernels.append(pack[start : start + KF, :].astype(F32))
    kernels = [split_kernel(one) for one in kernels]
    begin = pl.multiple_of(lax.axis_index("kern") * row_count, row_count)
    rows = mid[pl.ds(begin, row_count), :]
    for index, (real, imag) in enumerate(kernels):
        product = real * spectrum + imag * turned
        other = swap_halves(product)
        other = jnp.where(left, -other, other)
        stacked = jnp.concatenate([product, other], 0).astype(BF16)
        a_ref[index * row_count : (index + 1) * row_count, :] = dot(rows, stacked).astype(BF16)
    step = 32 if row_count % 32 == 0 else 16
    e_ref[0] = dot(a_ref[...], to_columns[0]).astype(BF16)
    for block in range(BLOCKS):
        now = block % 2
        group, place = divmod(block, WIDE)
        if block + 1 < BLOCKS:
            e_ref[1 - now] = dot(a_ref[...], to_columns[block + 1]).astype(BF16)
        for r in range(0, row_count, step):
            total = None
            for index in range(count):
                at = index * row_count + r
                real = e_ref[now, at : at + step, :LANES].astype(F32)
                imag = e_ref[now, at : at + step, LANES:].astype(F32)
                term = real * real + imag * imag
                total = term if total is None else total + term
            wanted = target[r : r + step, block * LANES : (block + 1) * LANES].astype(F32)
            bend = jnp.tanh(total - 2.0)
            slope = ((bend + (1.0 - 2.0 * wanted)) * (1.0 - bend * bend)).astype(BF16)
            for index in range(count):
                at = index * row_count + r
                for half in range(2):
                    field = e_ref[now, at : at + step, half * LANES : (half + 1) * LANES]
                    column = (2 * place + half) * LANES
                    v_ref[group % 2, at : at + step, column : column + LANES] = field * slope
        if place == WIDE - 1:
            part = dot(v_ref[group % 2], from_columns[group])
            if group == 0:
                u_ref[...] = part
            else:
                u_ref[...] += part
    wide = jnp.concatenate(
        [u_ref[i * row_count : (i + 1) * row_count, :].astype(BF16) for i in range(count)], 1
    )
    waves = lax.dot_general(rows, wide, (((0,), (0,)), ((), ())), preferred_element_type=F32)
    total = None
    for index, (real, imag) in enumerate(kernels):
        wave = waves[:, index * PAIR : (index + 1) * PAIR]
        top, bottom = wave[:KF], swap_halves(wave[KF:])
        wave = jnp.where(left, top + bottom, top - bottom)
        other = swap_halves(wave)
        other = jnp.where(left, other, -other)
        term = real * wave + imag * other
        total = term if total is None else total + term
    out[...] = total.astype(BF16)


def sum_body(count, *refs):
    total = refs[0][...].astype(F32)
    for one in refs[1:count]:
        total = total + one[...].astype(F32)
    refs[count][...] = total.astype(BF16)


def row_waves(rows, pair):
    pair = pair.astype(F32)
    other = swap_halves(pair)
    other = jnp.where(in_left_half(pair.shape), -other, other)
    return dot(rows, jnp.concatenate([pair, other], 0).astype(BF16)).astype(BF16)


def own_rows(mid, row_count):
    begin = pl.multiple_of(lax.axis_index("kern") * row_count, row_count)
    return mid[pl.ds(begin, row_count), :]


def inner_body(row_count, own, mid, back, out, waves, held, sems):
    wave = row_waves(own_rows(mid, row_count), own[...])
    waves[...] = wave
    half = BLOCKS // 2 * LANES
    copies = []
    for index, (first, last) in enumerate(((0, half), (half, N - 2 * LANES))):
        held[:, first:last] = dot(wave, back[:, LANES + first : LANES + last])
        copies.append(
            pltpu.make_async_copy(
                held.at[:, first:last], out.at[:, LANES + first : LANES + last], sems.at[index]
            )
        )
        copies[-1].start()
    for copy in copies:
        copy.wait()


def outer_body(
    row_count, near, far, near_pack, far_pack, mid, back, margins, waves, begun, out, held, sems
):
    rows = own_rows(mid, row_count)
    near_wave, far_wave = row_waves(rows, near[...]), row_waves(rows, far[...])
    odd = lax.rem(lax.axis_index("tile"), 2) == 1
    below, above = jnp.where(odd, near_wave, far_wave), jnp.where(odd, far_wave, near_wave)
    near_marks = near_pack[EDGE + KF :, :].astype(F32)
    far_marks = far_pack[EDGE + KF :, :].astype(F32)
    low_mark = jnp.where(odd, near_marks, far_marks)[1:2]
    high_mark = jnp.where(odd, far_marks, near_marks)[0:1]
    low = jnp.where(low_mark == 1.0, margins[1].astype(F32), margins[0].astype(F32)).astype(BF16)
    high = jnp.where(high_mark == 1.0, margins[3].astype(F32), margins[2].astype(F32)).astype(BF16)
    copies = []
    for side, first, wave, table in ((0, 0, below, low), (1, N - LANES, above, high)):
        columns = slice(first, first + LANES)
        held[side] = dot(waves[...], back[:, columns]) + dot(wave, table)
        copies.append(pltpu.make_async_copy(held.at[side], out.at[:, columns], sems.at[side]))
        copies[-1].start()
    for copy in copies:
        copy.wait()


def far_off(array):
    return pltpu.with_memory_space_constraint(array, pltpu.HBM)


def per_device(mask_pixels, orientation, target_pattern, kernel_real, kernel_imag, eigen_weights):
    tables = tuple(jnp.asarray(one) for one in transform_tables())
    mid, mid_t, to_columns, from_columns, rims, back, margins = tables
    tiles, count = lax.axis_size("tile"), lax.axis_size("kern")
    row_count = target_pattern.shape[0]
    vmem = pl.BlockSpec(memory_space=pltpu.VMEM)
    smem = pl.BlockSpec(memory_space=pltpu.SMEM)
    hbm = pl.BlockSpec(memory_space=pltpu.HBM)
    packed = jax.ShapeDtypeStruct((PACK, LANES), BF16)
    small = jax.ShapeDtypeStruct((KF, PAIR), BF16)

    mate, other, side, held, mid, mid_t = call(
        edges_body,
        "edges",
        (
            pltpu.VMEM((PACK, LANES), BF16),
            pltpu.VMEM((PACK, LANES), BF16),
            pltpu.VMEM((KF, PAIR), BF16),
            pltpu.VMEM((N, N), BF16),
            pltpu.VMEM((N, PAIR), BF16),
            pltpu.VMEM((PAIR, N), BF16),
        ),
        (
            *(far_off(one) for one in (mask_pixels, mid, mid_t, kernel_real, kernel_imag)),
            eigen_weights,
            far_off(orientation),
        ),
        [hbm] * 5 + [smem, hbm],
        scratch=[
            pltpu.VMEM((2, KF, KF), F32),
            pltpu.SMEM((1, 2), jnp.int32),
            pltpu.SemaphoreType.DMA((8,)),
        ],
        flops=2 * N * LANES * PAIR * 2,
        moved=N * LANES * 4,
    )

    def swapped(move_tile, step):
        pairs = []
        for t in range(tiles):
            for k in range(count):
                pairs.append((t * count + k, move_tile(t) * count + destination(k, step, count)))
        return pairs

    def chip_mate(t):
        return t ^ 1

    def other_side(t):
        return (t + 1 if t % 2 else t - 1) % tiles

    packs = []
    for step in kern_steps(count):
        value, move_tile = {0: (other, other_side), 1: (mate, chip_mate)}.get(
            len(packs), (side, lambda t: t)
        )
        packs.append(lax.ppermute(value, ("tile", "kern"), swapped(move_tile, step)))

    middle = call(
        middle_body,
        "middle",
        jax.ShapeDtypeStruct((PAIR, PAIR), F32),
        (held, mid, mid_t),
        [vmem] * 3,
        flops=4 * N * N * PAIR,
        moved=N * N * 2,
    )

    part = call(
        functools.partial(fields_body, count, row_count),
        "fields",
        small,
        (orientation, middle, target_pattern, mid, to_columns, from_columns, rims, side, *packs),
        [smem] + [vmem] * (7 + count - 1),
        scratch=[
            pltpu.VMEM((count * row_count, PAIR), BF16),
            pltpu.VMEM((2, count * row_count, 2 * LANES), BF16),
            pltpu.VMEM((2, count * row_count, 2 * WIDE * LANES), BF16),
            pltpu.VMEM((count * row_count, PAIR), F32),
        ],
        flops=8 * count * row_count * N * PAIR,
        moved=4 * row_count * N,
    )

    parts = [part]
    for step in kern_steps(count):
        pairs = [(k, destination(k, step, count)) for k in range(count)]
        parts.append(lax.ppermute(part, "kern", pairs))
    own = call(functools.partial(sum_body, count), "total", small, tuple(parts), [vmem] * count)
    near = lax.ppermute(own, "tile", [(t, chip_mate(t)) for t in range(tiles)])
    inner = [t for t in range(tiles) if 0 < t < tiles - 1]
    far = lax.ppermute(own, "tile", [(t, other_side(t)) for t in inner])
    begun, waves = call(
        functools.partial(inner_body, row_count),
        "inner",
        (jax.ShapeDtypeStruct((row_count, N), F32), pltpu.VMEM((row_count, PAIR), BF16)),
        (own, mid, back),
        [vmem] * 3,
        (hbm, vmem),
        scratch=[
            pltpu.VMEM((row_count, N - 2 * LANES), F32),
            pltpu.SemaphoreType.DMA((2,)),
        ],
        flops=2 * row_count * PAIR * N,
        moved=4 * row_count * N,
    )
    return call(
        functools.partial(outer_body, row_count),
        "outer",
        jax.ShapeDtypeStruct((row_count, N), F32),
        (near, far, packs[1], packs[0], mid, back, margins, waves, begun),
        [vmem] * 8 + [hbm],
        hbm,
        scratch=[
            pltpu.VMEM((2, row_count, LANES), F32),
            pltpu.SemaphoreType.DMA((2,)),
        ],
        flops=2 * row_count * PAIR * 6 * PAIR,
        moved=4 * row_count * 2 * LANES,
        alias={8: 0},
    )


def solution(mesh):
    in_specs = (
        P(None, "tile"),
        P("tile", None),
        P("kern", "tile"),
        P("kern", None, None),
        P("kern", None, None),
        P("kern"),
    )
    out_specs = P("kern", "tile")
    return jax.shard_map(
        per_device, mesh=mesh, in_specs=in_specs, out_specs=out_specs, check_vma=False
    )
```

```python
import functools
import math

import jax
import jax.numpy as jnp
import ml_dtypes
import numpy as np
from jax import lax
from jax.experimental import pallas as pl
from jax.experimental.pallas import tpu as pltpu
from jax.sharding import PartitionSpec as P

N = 1152
HALO = 64
KF = 64
NE = 1280
LANES = 128
PAIR = 2 * KF
BLOCKS = N // LANES
EDGE = KF
PACK = EDGE + KF + 16
BF16 = jnp.bfloat16
F32 = jnp.float32
VMEM_LIMIT = 32 * 1024 * 1024


def wave_tables():
    position = np.arange(NE)[:, None]
    frequency = np.arange(KF)[None, :] - KF // 2
    phase = np.mod(position * frequency, NE).astype(np.float64) * (2.0 * math.pi / NE)
    return np.cos(phase).astype(np.float32), np.sin(phase).astype(np.float32)


def transform_tables():
    cos, sin = wave_tables()
    full = np.concatenate([cos, sin], 1)
    mid = full[HALO : HALO + N]
    ct, st = cos[HALO : HALO + N].T, sin[HALO : HALO + N].T
    columns = np.concatenate(
        [
            np.stack([ct.reshape(KF, BLOCKS, LANES), st.reshape(KF, BLOCKS, LANES)], 2),
            np.stack([-st.reshape(KF, BLOCKS, LANES), ct.reshape(KF, BLOCKS, LANES)], 2),
        ],
        0,
    )
    to_columns = columns.transpose(1, 0, 2, 3).reshape(BLOCKS, PAIR, 2 * LANES)
    from_columns = to_columns.transpose(0, 2, 1)
    low, high = full[:HALO], full[HALO + N :]
    blank = np.zeros((HALO, PAIR), np.float32)
    rims = np.stack(
        [
            np.concatenate([low[::-1], blank], 0),
            np.concatenate([low, blank], 0),
            np.concatenate([high[::-1], blank], 0),
            np.concatenate([high, blank], 0),
        ]
    )
    back = np.concatenate([cos.T, -sin.T], 0)
    back_low, back_high = back[:, :HALO], back[:, HALO + N :]
    blank = np.zeros((PAIR, HALO), np.float32)
    margins = np.stack(
        [
            np.concatenate([back_high[:, ::-1], blank], 1),
            np.concatenate([back_high, blank], 1),
            np.concatenate([blank, back_low[:, ::-1]], 1),
            np.concatenate([blank, back_low], 1),
        ]
    )
    tables = (mid, mid.T, to_columns, from_columns, rims, back[:, HALO : HALO + N], margins)
    return tuple(np.ascontiguousarray(one).astype(ml_dtypes.bfloat16) for one in tables)


def dot(a, b):
    return jnp.dot(a, b, preferred_element_type=F32)


def in_left_half(shape):
    return lax.broadcasted_iota(jnp.int32, shape, 1) < KF


def swap_halves(pair):
    return pltpu.roll(pair, KF, 1)


def kern_steps(count):
    return (1, 3, 2) if count == 4 else range(1, count)


def destination(k, step, count):
    return k ^ step if count == 4 else (k - step) % count


def call(
    body, name, outs, args, specs, out_specs=None, scratch=(), flops=0, moved=0, alias=None
):
    vmem = pl.BlockSpec(memory_space=pltpu.VMEM)
    if out_specs is None:
        out_specs = tuple(vmem for _ in outs) if isinstance(outs, tuple) else vmem
    return pl.pallas_call(
        body,
        name=name,
        out_shape=outs,
        in_specs=specs,
        out_specs=out_specs,
        scratch_shapes=list(scratch),
        input_output_aliases=alias or {},
        compiler_params=pltpu.CompilerParams(vmem_limit_bytes=VMEM_LIMIT),
        cost_estimate=pl.CostEstimate(flops=flops, bytes_accessed=moved, transcendentals=0),
    )(*args)


def edges_body(
    mask, mid, mid_t, real, imag, weight, flags, mate, other, side, held, tall, table, pair, marks, sems
):
    odd = lax.rem(lax.axis_index("tile"), 2) == 1
    copies = [
        pltpu.make_async_copy(mid_t, table, sems.at[0]),
        pltpu.make_async_copy(mask.at[:, :LANES], held.at[:, :LANES], sems.at[1]),
        pltpu.make_async_copy(mask.at[:, N - LANES :], held.at[:, N - LANES :], sems.at[2]),
        pltpu.make_async_copy(real.at[0], pair.at[0], sems.at[3]),
        pltpu.make_async_copy(imag.at[0], pair.at[1], sems.at[4]),
        pltpu.make_async_copy(flags, marks, sems.at[5]),
    ]
    inner = pltpu.make_async_copy(
        mask.at[:, LANES : N - LANES], held.at[:, LANES : N - LANES], sems.at[6]
    )
    columns = pltpu.make_async_copy(mid, tall, sems.at[7])
    for copy in copies:
        copy.start()
    inner.start()
    columns.start()
    for copy in copies[3:]:
        copy.wait()
    scale = jnp.sqrt(jnp.full((KF, KF), 2.0 * weight[0], F32)) * (1.0 / (NE * KF))
    kernel = jnp.concatenate([pair[0] * scale, pair[1] * scale], 1).astype(BF16)
    row = lax.broadcasted_iota(jnp.int32, (16, LANES), 0)
    sides = jnp.where(row == 0, marks[0, 0].astype(F32), marks[0, 1].astype(F32)).astype(BF16)
    side[...] = kernel
    for out in (mate, other):
        out[EDGE : EDGE + KF, :] = kernel
        out[EDGE + KF :, :] = sides
    for copy in copies[:3]:
        copy.wait()
    strips = jnp.concatenate([held[:, :LANES], held[:, N - LANES :]], 1)
    both = dot(table[...], strips)
    left = in_left_half((KF, LANES))
    first, last = both[:, :LANES], both[:, LANES:]
    first = jnp.where(left, first[:KF], swap_halves(first[KF:]))
    last = jnp.where(left, swap_halves(last[:KF]), last[KF:])
    mate[:EDGE, :] = jnp.where(odd, first, last).astype(BF16)
    other[:EDGE, :] = jnp.where(odd, last, first).astype(BF16)
    inner.wait()
    columns.wait()


def middle_body(mask, mid, mid_t, out):
    out[...] = dot(mid_t[...], dot(mask[...], mid[...]).astype(BF16))


def split_kernel(pair):
    left = in_left_half(pair.shape)
    other = swap_halves(pair)
    return jnp.where(left, pair, other), jnp.where(left, other, pair)


def fields_body(count, row_count, *refs):
    (flags, middle, target, mid, to_columns, from_columns, rims, own) = refs[:8]
    packs = refs[8 : 8 + count - 1]
    out, a_ref, e_ref, v_ref, u_ref = refs[8 + count - 1 :]
    tile = lax.axis_index("tile")
    tiles = lax.axis_size("tile")
    left = in_left_half((KF, PAIR))
    blocks = middle[...]
    low = jnp.where(flags[0, 0] == 1, rims[1], rims[0])
    low = jnp.where(tile == 0, jnp.zeros_like(low), low)
    high = jnp.where(flags[0, 1] == 1, rims[3], rims[2])
    high = jnp.where(tile == tiles - 1, jnp.zeros_like(high), high)
    odd = lax.rem(tile, 2) == 1
    low, high = jnp.where(odd, low, high), jnp.where(odd, high, low)
    for pack, table in ((packs[1], low), (packs[0], high)):
        edge = pack[:EDGE, :].astype(F32)
        edge = jnp.concatenate([edge, swap_halves(edge)], 0).astype(BF16)
        blocks = blocks + dot(edge, table)
    top, bottom = blocks[:KF], swap_halves(blocks[KF:])
    spectrum = jnp.where(left, top - bottom, -(top + bottom))
    turned = swap_halves(spectrum)
    turned = jnp.where(left, -turned, turned)
    kernels = [own[...].astype(F32)]
    for index, pack in enumerate(packs):
        start = EDGE if index < 2 else 0
        kernels.append(pack[start : start + KF, :].astype(F32))
    kernels = [split_kernel(one) for one in kernels]
    begin = pl.multiple_of(lax.axis_index("kern") * row_count, row_count)
    rows = mid[pl.ds(begin, row_count), :]
    for index, (real, imag) in enumerate(kernels):
        product = real * spectrum + imag * turned
        other = swap_halves(product)
        other = jnp.where(left, -other, other)
        stacked = jnp.concatenate([product, other], 0).astype(BF16)
        a_ref[index * row_count : (index + 1) * row_count, :] = dot(rows, stacked).astype(BF16)
    step = 32 if row_count % 32 == 0 else 16
    steps = list(range(0, row_count, step))
    shares = [steps[i * len(steps) // count : (i + 1) * len(steps) // count] for i in range(count)]
    e_ref[0] = dot(a_ref[...], to_columns[0]).astype(BF16)
    for block in range(BLOCKS + 1):
        now = block % 2
        for share in range(count):
            mine = slice(share * row_count, (share + 1) * row_count)
            if block + 1 < BLOCKS:
                e_ref[1 - now, mine, :] = dot(a_ref[mine, :], to_columns[block + 1]).astype(BF16)
            if block > 0:
                part = dot(v_ref[1 - now, mine, :], from_columns[block - 1])
                u_ref[mine, :] = part if block == 1 else u_ref[mine, :] + part
            if block == BLOCKS:
                continue
            for r in shares[share]:
                total = None
                for index in range(count):
                    at = index * row_count + r
                    real = e_ref[now, at : at + step, :LANES]
                    imag = e_ref[now, at : at + step, LANES:]
                    term = (real * real + imag * imag).astype(F32)
                    total = term if total is None else total + term
                wanted = target[r : r + step, block * LANES : (block + 1) * LANES].astype(F32)
                bend = jnp.tanh(total - 2.0)
                slope = ((bend + (1.0 - 2.0 * wanted)) * (1.0 - bend * bend)).astype(BF16)
                for index in range(count):
                    at = index * row_count + r
                    for half in (slice(0, LANES), slice(LANES, 2 * LANES)):
                        v_ref[now, at : at + step, half] = e_ref[now, at : at + step, half] * slope
    wide = jnp.concatenate(
        [u_ref[i * row_count : (i + 1) * row_count, :].astype(BF16) for i in range(count)], 1
    )
    waves = lax.dot_general(rows, wide, (((0,), (0,)), ((), ())), preferred_element_type=F32)
    total = None
    for index, (real, imag) in enumerate(kernels):
        wave = waves[:, index * PAIR : (index + 1) * PAIR]
        top, bottom = wave[:KF], swap_halves(wave[KF:])
        wave = jnp.where(left, top + bottom, top - bottom)
        other = swap_halves(wave)
        other = jnp.where(left, other, -other)
        term = real * wave + imag * other
        total = term if total is None else total + term
    out[...] = total.astype(BF16)


def sum_body(count, *refs):
    total = refs[0][...].astype(F32)
    for one in refs[1:count]:
        total = total + one[...].astype(F32)
    refs[count][...] = total.astype(BF16)


def row_waves(rows, pair):
    pair = pair.astype(F32)
    other = swap_halves(pair)
    other = jnp.where(in_left_half(pair.shape), -other, other)
    return dot(rows, jnp.concatenate([pair, other], 0).astype(BF16)).astype(BF16)


def own_rows(mid, row_count):
    begin = pl.multiple_of(lax.axis_index("kern") * row_count, row_count)
    return mid[pl.ds(begin, row_count), :]


def inner_body(row_count, own, mid, back, out, waves, held, sems):
    wave = row_waves(own_rows(mid, row_count), own[...])
    waves[...] = wave
    half = BLOCKS // 2 * LANES
    copies = []
    for index, (first, last) in enumerate(((0, half), (half, N - 2 * LANES))):
        held[:, first:last] = dot(wave, back[:, LANES + first : LANES + last])
        copies.append(
            pltpu.make_async_copy(
                held.at[:, first:last], out.at[:, LANES + first : LANES + last], sems.at[index]
            )
        )
        copies[-1].start()
    for copy in copies:
        copy.wait()


def outer_body(
    row_count, near, far, near_pack, far_pack, mid, back, margins, waves, begun, out, held, sems
):
    rows = own_rows(mid, row_count)
    near_wave, far_wave = row_waves(rows, near[...]), row_waves(rows, far[...])
    odd = lax.rem(lax.axis_index("tile"), 2) == 1
    below, above = jnp.where(odd, near_wave, far_wave), jnp.where(odd, far_wave, near_wave)
    near_marks = near_pack[EDGE + KF :, :].astype(F32)
    far_marks = far_pack[EDGE + KF :, :].astype(F32)
    low_mark = jnp.where(odd, near_marks, far_marks)[1:2]
    high_mark = jnp.where(odd, far_marks, near_marks)[0:1]
    low = jnp.where(low_mark == 1.0, margins[1].astype(F32), margins[0].astype(F32)).astype(BF16)
    high = jnp.where(high_mark == 1.0, margins[3].astype(F32), margins[2].astype(F32)).astype(BF16)
    copies = []
    for side, first, wave, table in ((0, 0, below, low), (1, N - LANES, above, high)):
        columns = slice(first, first + LANES)
        held[side] = dot(waves[...], back[:, columns]) + dot(wave, table)
        copies.append(pltpu.make_async_copy(held.at[side], out.at[:, columns], sems.at[side]))
        copies[-1].start()
    for copy in copies:
        copy.wait()


def far_off(array):
    return pltpu.with_memory_space_constraint(array, pltpu.HBM)


def per_device(mask_pixels, orientation, target_pattern, kernel_real, kernel_imag, eigen_weights):
    tables = tuple(jnp.asarray(one) for one in transform_tables())
    mid, mid_t, to_columns, from_columns, rims, back, margins = tables
    tiles, count = lax.axis_size("tile"), lax.axis_size("kern")
    row_count = target_pattern.shape[0]
    vmem = pl.BlockSpec(memory_space=pltpu.VMEM)
    smem = pl.BlockSpec(memory_space=pltpu.SMEM)
    hbm = pl.BlockSpec(memory_space=pltpu.HBM)
    packed = jax.ShapeDtypeStruct((PACK, LANES), BF16)
    small = jax.ShapeDtypeStruct((KF, PAIR), BF16)

    mate, other, side, held, mid, mid_t = call(
        edges_body,
        "edges",
        (
            pltpu.VMEM((PACK, LANES), BF16),
            pltpu.VMEM((PACK, LANES), BF16),
            pltpu.VMEM((KF, PAIR), BF16),
            pltpu.VMEM((N, N), BF16),
            pltpu.VMEM((N, PAIR), BF16),
            pltpu.VMEM((PAIR, N), BF16),
        ),
        (
            *(far_off(one) for one in (mask_pixels, mid, mid_t, kernel_real, kernel_imag)),
            eigen_weights,
            far_off(orientation),
        ),
        [hbm] * 5 + [smem, hbm],
        scratch=[
            pltpu.VMEM((2, KF, KF), F32),
            pltpu.SMEM((1, 2), jnp.int32),
            pltpu.SemaphoreType.DMA((8,)),
        ],
        flops=2 * N * LANES * PAIR * 2,
        moved=N * LANES * 4,
    )

    def swapped(move_tile, step):
        pairs = []
        for t in range(tiles):
            for k in range(count):
                pairs.append((t * count + k, move_tile(t) * count + destination(k, step, count)))
        return pairs

    def chip_mate(t):
        return t ^ 1

    def other_side(t):
        return (t + 1 if t % 2 else t - 1) % tiles

    packs = []
    for step in kern_steps(count):
        value, move_tile = {0: (other, other_side), 1: (mate, chip_mate)}.get(
            len(packs), (side, lambda t: t)
        )
        packs.append(lax.ppermute(value, ("tile", "kern"), swapped(move_tile, step)))

    middle = call(
        middle_body,
        "middle",
        jax.ShapeDtypeStruct((PAIR, PAIR), F32),
        (held, mid, mid_t),
        [vmem] * 3,
        flops=4 * N * N * PAIR,
        moved=N * N * 2,
    )

    part = call(
        functools.partial(fields_body, count, row_count),
        "fields",
        small,
        (orientation, middle, target_pattern, mid, to_columns, from_columns, rims, side, *packs),
        [smem] + [vmem] * (7 + count - 1),
        scratch=[
            pltpu.VMEM((count * row_count, PAIR), BF16),
            pltpu.VMEM((2, count * row_count, 2 * LANES), BF16),
            pltpu.VMEM((2, count * row_count, 2 * LANES), BF16),
            pltpu.VMEM((count * row_count, PAIR), F32),
        ],
        flops=8 * count * row_count * N * PAIR,
        moved=4 * row_count * N,
    )

    def summed(parts):
        return call(
            functools.partial(sum_body, len(parts)), "total", small, parts, [vmem] * len(parts)
        )

    def moved(value, step):
        pairs = [(k, destination(k, step, count)) for k in range(count)]
        return lax.ppermute(value, "kern", pairs)

    if count == 4:
        own = summed((part, moved(part, 1)))
        own = summed((own, moved(own, 2)))
    else:
        own = summed((part, *(moved(part, step) for step in kern_steps(count))))
    near = lax.ppermute(own, "tile", [(t, chip_mate(t)) for t in range(tiles)])
    inner = [t for t in range(tiles) if 0 < t < tiles - 1]
    far = lax.ppermute(own, "tile", [(t, other_side(t)) for t in inner])
    begun, waves = call(
        functools.partial(inner_body, row_count),
        "inner",
        (jax.ShapeDtypeStruct((row_count, N), F32), pltpu.VMEM((row_count, PAIR), BF16)),
        (own, mid, back),
        [vmem] * 3,
        (hbm, vmem),
        scratch=[
            pltpu.VMEM((row_count, N - 2 * LANES), F32),
            pltpu.SemaphoreType.DMA((2,)),
        ],
        flops=2 * row_count * PAIR * N,
        moved=4 * row_count * N,
    )
    return call(
        functools.partial(outer_body, row_count),
        "outer",
        jax.ShapeDtypeStruct((row_count, N), F32),
        (near, far, packs[1], packs[0], mid, back, margins, waves, begun),
        [vmem] * 8 + [hbm],
        hbm,
        scratch=[
            pltpu.VMEM((2, row_count, LANES), F32),
            pltpu.SemaphoreType.DMA((2,)),
        ],
        flops=2 * row_count * PAIR * 6 * PAIR,
        moved=4 * row_count * 2 * LANES,
        alias={8: 0},
    )


def solution(mesh):
    in_specs = (
        P(None, "tile"),
        P("tile", None),
        P("kern", "tile"),
        P("kern", None, None),
        P("kern", None, None),
        P("kern"),
    )
    out_specs = P("kern", "tile")
    return jax.shard_map(
        per_device, mesh=mesh, in_specs=in_specs, out_specs=out_specs, check_vma=False
    )
```

```python
import functools
import math

import jax
import jax.numpy as jnp
import ml_dtypes
import numpy as np
from jax import lax
from jax.experimental import pallas as pl
from jax.experimental.pallas import tpu as pltpu
from jax.sharding import PartitionSpec as P

N = 1152
HALO = 64
KF = 64
NE = 1280
LANES = 128
PAIR = 2 * KF
BLOCKS = N // LANES
EDGE = KF
WIDE = 3
GROUPS = BLOCKS // WIDE
MARKS = 16
BF16 = jnp.bfloat16
F32 = jnp.float32
VMEM_LIMIT = 32 * 1024 * 1024


def wave_tables():
    position = np.arange(NE)[:, None]
    frequency = np.arange(KF)[None, :] - KF // 2
    phase = np.mod(position * frequency, NE).astype(np.float64) * (2.0 * math.pi / NE)
    return np.cos(phase).astype(np.float32), np.sin(phase).astype(np.float32)


def transform_tables():
    cos, sin = wave_tables()
    full = np.concatenate([cos, sin], 1)
    mid = full[HALO : HALO + N]
    ct, st = cos[HALO : HALO + N].T, sin[HALO : HALO + N].T
    columns = np.concatenate(
        [
            np.stack([ct.reshape(KF, BLOCKS, LANES), st.reshape(KF, BLOCKS, LANES)], 2),
            np.stack([-st.reshape(KF, BLOCKS, LANES), ct.reshape(KF, BLOCKS, LANES)], 2),
        ],
        0,
    )
    to_columns = columns.transpose(1, 0, 2, 3).reshape(GROUPS, WIDE, PAIR, 2 * LANES)
    to_columns = to_columns.transpose(0, 2, 1, 3).reshape(GROUPS, PAIR, WIDE * 2 * LANES)
    from_columns = to_columns.transpose(0, 2, 1)
    low, high = full[:HALO], full[HALO + N :]
    blank = np.zeros((HALO, PAIR), np.float32)
    rims = np.stack(
        [
            np.concatenate([low[::-1], blank], 0),
            np.concatenate([low, blank], 0),
            np.concatenate([high[::-1], blank], 0),
            np.concatenate([high, blank], 0),
        ]
    )
    back = np.concatenate([cos.T, -sin.T], 0)
    back_low, back_high = back[:, :HALO], back[:, HALO + N :]
    blank = np.zeros((PAIR, HALO), np.float32)
    margins = np.stack(
        [
            np.concatenate([back_high[:, ::-1], blank], 1),
            np.concatenate([back_high, blank], 1),
            np.concatenate([blank, back_low[:, ::-1]], 1),
            np.concatenate([blank, back_low], 1),
        ]
    )
    tables = (mid, mid.T, to_columns, from_columns, rims, back[:, HALO : HALO + N], margins)
    return tuple(np.ascontiguousarray(one).astype(ml_dtypes.bfloat16) for one in tables)


def dot(a, b):
    return jnp.dot(a, b, preferred_element_type=F32)


def in_left_half(shape):
    return lax.broadcasted_iota(jnp.int32, shape, 1) < KF


def swap_halves(pair):
    return pltpu.roll(pair, KF, 1)


def destination(k, step, count):
    return k ^ step if count == 4 else (k - step) % count


def call(
    body, name, outs, args, specs, out_specs=None, scratch=(), flops=0, moved=0, alias=None
):
    vmem = pl.BlockSpec(memory_space=pltpu.VMEM)
    if out_specs is None:
        out_specs = tuple(vmem for _ in outs) if isinstance(outs, tuple) else vmem
    return pl.pallas_call(
        body,
        name=name,
        out_shape=outs,
        in_specs=specs,
        out_specs=out_specs,
        scratch_shapes=list(scratch),
        input_output_aliases=alias or {},
        compiler_params=pltpu.CompilerParams(vmem_limit_bytes=VMEM_LIMIT),
        cost_estimate=pl.CostEstimate(flops=flops, bytes_accessed=moved, transcendentals=0),
    )(*args)


def edges_body(
    mask, mid, mid_t, real, imag, weight, flags, mate, other, side, held, tall, table, pair, marks, sems
):
    odd = lax.rem(lax.axis_index("tile"), 2) == 1
    copies = [
        pltpu.make_async_copy(mid_t, table, sems.at[0]),
        pltpu.make_async_copy(mask.at[:, :LANES], held.at[:, :LANES], sems.at[1]),
        pltpu.make_async_copy(mask.at[:, N - LANES :], held.at[:, N - LANES :], sems.at[2]),
        pltpu.make_async_copy(real.at[0], pair.at[0], sems.at[3]),
        pltpu.make_async_copy(imag.at[0], pair.at[1], sems.at[4]),
        pltpu.make_async_copy(flags, marks, sems.at[5]),
    ]
    inner = pltpu.make_async_copy(
        mask.at[:, LANES : N - LANES], held.at[:, LANES : N - LANES], sems.at[6]
    )
    columns = pltpu.make_async_copy(mid, tall, sems.at[7])
    for copy in copies:
        copy.start()
    inner.start()
    columns.start()
    for copy in copies[3:]:
        copy.wait()
    scale = jnp.sqrt(jnp.full((KF, KF), 2.0 * weight[0], F32)) * (1.0 / (NE * KF))
    kernel = jnp.concatenate([pair[0] * scale, pair[1] * scale], 1).astype(BF16)
    row = lax.broadcasted_iota(jnp.int32, (16, LANES), 0)
    sides = jnp.where(row == 0, marks[0, 0].astype(F32), marks[0, 1].astype(F32)).astype(BF16)
    side[...] = kernel
    mate[EDGE : 2 * EDGE, :] = kernel
    mate[2 * EDGE :, :] = sides
    other[EDGE:, :] = sides
    for copy in copies[:3]:
        copy.wait()
    strips = jnp.concatenate([held[:, :LANES], held[:, N - LANES :]], 1)
    both = dot(table[...], strips)
    left = in_left_half((KF, LANES))
    first, last = both[:, :LANES], both[:, LANES:]
    first = jnp.where(left, first[:KF], swap_halves(first[KF:]))
    last = jnp.where(left, swap_halves(last[:KF]), last[KF:])
    mate[:EDGE, :] = jnp.where(odd, first, last).astype(BF16)
    other[:EDGE, :] = jnp.where(odd, last, first).astype(BF16)
    inner.wait()
    columns.wait()


def middle_body(mask, mid, mid_t, out):
    out[...] = dot(mid_t[...], dot(mask[...], mid[...]).astype(BF16))


def split_kernel(pair):
    left = in_left_half(pair.shape)
    other = swap_halves(pair)
    return jnp.where(left, pair, other), jnp.where(left, other, pair)


def fields_body(count, row_count, *refs):
    (flags, middle, target, mid, to_columns, from_columns, rims, own) = refs[:8]
    near_pack, *others, far_edge = refs[8 : 8 + count]
    out, a_ref, e_ref, v_ref, u_ref = refs[8 + count :]
    tile = lax.axis_index("tile")
    tiles = lax.axis_size("tile")
    left = in_left_half((KF, PAIR))
    blocks = middle[...]
    low = jnp.where(flags[0, 0] == 1, rims[1], rims[0])
    low = jnp.where(tile == 0, jnp.zeros_like(low), low)
    high = jnp.where(flags[0, 1] == 1, rims[3], rims[2])
    high = jnp.where(tile == tiles - 1, jnp.zeros_like(high), high)
    odd = lax.rem(tile, 2) == 1
    low, high = jnp.where(odd, low, high), jnp.where(odd, high, low)
    for pack, table in ((near_pack, low), (far_edge, high)):
        edge = pack[:EDGE, :].astype(F32)
        edge = jnp.concatenate([edge, swap_halves(edge)], 0).astype(BF16)
        blocks = blocks + dot(edge, table)
    top, bottom = blocks[:KF], swap_halves(blocks[KF:])
    spectrum = jnp.where(left, top - bottom, -(top + bottom))
    turned = swap_halves(spectrum)
    turned = jnp.where(left, -turned, turned)
    kernels = [own[...].astype(F32)]
    kernels.append(near_pack[EDGE : 2 * EDGE, :].astype(F32))
    kernels += [one[...].astype(F32) for one in others]
    kernels = [split_kernel(one) for one in kernels]
    begin = pl.multiple_of(lax.axis_index("kern") * row_count, row_count)
    rows = mid[pl.ds(begin, row_count), :]
    for index, (real, imag) in enumerate(kernels):
        product = real * spectrum + imag * turned
        other = swap_halves(product)
        other = jnp.where(left, -other, other)
        stacked = jnp.concatenate([product, other], 0).astype(BF16)
        a_ref[index * row_count : (index + 1) * row_count, :] = dot(rows, stacked).astype(BF16)
    step = 32 if row_count % 32 == 0 else 16
    e_ref[0] = dot(a_ref[...], to_columns[0])
    for group in range(GROUPS):
        now = group % 2
        if group + 1 < GROUPS:
            e_ref[1 - now] = dot(a_ref[...], to_columns[group + 1])
        for place in range(WIDE):
            first = (group * WIDE + place) * LANES
            halves = [slice((2 * place + half) * LANES, (2 * place + half + 1) * LANES) for half in range(2)]
            for r in range(0, row_count, step):
                total = None
                for index in range(count):
                    at = index * row_count + r
                    real, imag = (e_ref[now, at : at + step, half] for half in halves)
                    term = real * real + imag * imag
                    total = term if total is None else total + term
                wanted = target[r : r + step, first : first + LANES].astype(F32)
                bend = jnp.tanh(total - 2.0)
                slope = (bend + (1.0 - 2.0 * wanted)) * (1.0 - bend * bend)
                for index in range(count):
                    at = index * row_count + r
                    for half in halves:
                        field = e_ref[now, at : at + step, half] * slope
                        v_ref[now, at : at + step, half] = field.astype(BF16)
        part = dot(v_ref[now], from_columns[group])
        if group == 0:
            u_ref[...] = part
        else:
            u_ref[...] += part
    wide = jnp.concatenate(
        [u_ref[i * row_count : (i + 1) * row_count, :].astype(BF16) for i in range(count)], 1
    )
    waves = lax.dot_general(rows, wide, (((0,), (0,)), ((), ())), preferred_element_type=F32)
    total = None
    for index, (real, imag) in enumerate(kernels):
        wave = waves[:, index * PAIR : (index + 1) * PAIR]
        top, bottom = wave[:KF], swap_halves(wave[KF:])
        wave = jnp.where(left, top + bottom, top - bottom)
        other = swap_halves(wave)
        other = jnp.where(left, other, -other)
        term = real * wave + imag * other
        total = term if total is None else total + term
    out[...] = total.astype(BF16)


def sum_body(count, *refs):
    total = refs[0][...].astype(F32)
    for one in refs[1:count]:
        total = total + one[...].astype(F32)
    refs[count][...] = total.astype(BF16)


def row_waves(rows, pair):
    pair = pair.astype(F32)
    other = swap_halves(pair)
    other = jnp.where(in_left_half(pair.shape), -other, other)
    return dot(rows, jnp.concatenate([pair, other], 0).astype(BF16)).astype(BF16)


def own_rows(mid, row_count):
    begin = pl.multiple_of(lax.axis_index("kern") * row_count, row_count)
    return mid[pl.ds(begin, row_count), :]


def inner_body(row_count, own, mid, back, out, waves, held, sems):
    wave = row_waves(own_rows(mid, row_count), own[...])
    waves[...] = wave
    half = BLOCKS // 2 * LANES
    copies = []
    for index, (first, last) in enumerate(((0, half), (half, N - 2 * LANES))):
        held[:, first:last] = dot(wave, back[:, LANES + first : LANES + last])
        copies.append(
            pltpu.make_async_copy(
                held.at[:, first:last], out.at[:, LANES + first : LANES + last], sems.at[index]
            )
        )
        copies[-1].start()
    for copy in copies:
        copy.wait()


def outer_body(
    row_count, near, far, near_pack, far_edge, mid, back, margins, waves, begun, out, held, sems
):
    rows = own_rows(mid, row_count)
    near_wave, far_wave = row_waves(rows, near[...]), row_waves(rows, far[...])
    odd = lax.rem(lax.axis_index("tile"), 2) == 1
    below, above = jnp.where(odd, near_wave, far_wave), jnp.where(odd, far_wave, near_wave)
    near_marks = near_pack[2 * EDGE :, :].astype(F32)
    far_marks = far_edge[EDGE:, :].astype(F32)
    low_mark = jnp.where(odd, near_marks, far_marks)[1:2]
    high_mark = jnp.where(odd, far_marks, near_marks)[0:1]
    low = jnp.where(low_mark == 1.0, margins[1].astype(F32), margins[0].astype(F32)).astype(BF16)
    high = jnp.where(high_mark == 1.0, margins[3].astype(F32), margins[2].astype(F32)).astype(BF16)
    copies = []
    for side, first, wave, table in ((0, 0, below, low), (1, N - LANES, above, high)):
        columns = slice(first, first + LANES)
        held[side] = dot(waves[...], back[:, columns]) + dot(wave, table)
        copies.append(pltpu.make_async_copy(held.at[side], out.at[:, columns], sems.at[side]))
        copies[-1].start()
    for copy in copies:
        copy.wait()


def far_off(array):
    return pltpu.with_memory_space_constraint(array, pltpu.HBM)


def per_device(mask_pixels, orientation, target_pattern, kernel_real, kernel_imag, eigen_weights):
    tables = tuple(jnp.asarray(one) for one in transform_tables())
    mid, mid_t, to_columns, from_columns, rims, back, margins = tables
    tiles, count = lax.axis_size("tile"), lax.axis_size("kern")
    row_count = target_pattern.shape[0]
    vmem = pl.BlockSpec(memory_space=pltpu.VMEM)
    smem = pl.BlockSpec(memory_space=pltpu.SMEM)
    hbm = pl.BlockSpec(memory_space=pltpu.HBM)
    small = jax.ShapeDtypeStruct((KF, PAIR), BF16)

    mate, other, side, held, mid, mid_t = call(
        edges_body,
        "edges",
        (
            pltpu.VMEM((2 * EDGE + MARKS, LANES), BF16),
            pltpu.VMEM((EDGE + MARKS, LANES), BF16),
            pltpu.VMEM((KF, PAIR), BF16),
            pltpu.VMEM((N, N), BF16),
            pltpu.VMEM((N, PAIR), BF16),
            pltpu.VMEM((PAIR, N), BF16),
        ),
        (
            *(far_off(one) for one in (mask_pixels, mid, mid_t, kernel_real, kernel_imag)),
            eigen_weights,
            far_off(orientation),
        ),
        [hbm] * 5 + [smem, hbm],
        scratch=[
            pltpu.VMEM((2, KF, KF), F32),
            pltpu.SMEM((1, 2), jnp.int32),
            pltpu.SemaphoreType.DMA((8,)),
        ],
        flops=2 * N * LANES * PAIR * 2,
        moved=N * LANES * 4,
    )

    def swapped(move_tile, step):
        pairs = []
        for t in range(tiles):
            for k in range(count):
                pairs.append((t * count + k, move_tile(t) * count + destination(k, step, count)))
        return pairs

    def chip_mate(t):
        return t ^ 1

    def other_side(t):
        return (t + 1 if t % 2 else t - 1) % tiles

    both = ("tile", "kern")
    far_edge = lax.ppermute(other, both, swapped(other_side, 0))
    near_pack = lax.ppermute(mate, both, swapped(chip_mate, 1))
    kernels = [lax.ppermute(side, both, swapped(lambda t: t, step)) for step in range(2, count)]

    middle = call(
        middle_body,
        "middle",
        jax.ShapeDtypeStruct((PAIR, PAIR), F32),
        (held, mid, mid_t),
        [vmem] * 3,
        flops=4 * N * N * PAIR,
        moved=N * N * 2,
    )

    part = call(
        functools.partial(fields_body, count, row_count),
        "fields",
        small,
        (orientation, middle, target_pattern, mid, to_columns, from_columns, rims, side, near_pack, *kernels, far_edge),
        [smem] + [vmem] * (7 + count),
        scratch=[
            pltpu.VMEM((count * row_count, PAIR), BF16),
            pltpu.VMEM((2, count * row_count, 2 * WIDE * LANES), F32),
            pltpu.VMEM((2, count * row_count, 2 * WIDE * LANES), BF16),
            pltpu.VMEM((count * row_count, PAIR), F32),
        ],
        flops=8 * count * row_count * N * PAIR,
        moved=4 * row_count * N,
    )

    parts = [part]
    for step in range(1, count):
        pairs = [(k, destination(k, step, count)) for k in range(count)]
        parts.append(lax.ppermute(part, "kern", pairs))
    own = call(functools.partial(sum_body, count), "total", small, tuple(parts), [vmem] * count)
    near = lax.ppermute(own, "tile", [(t, chip_mate(t)) for t in range(tiles)])
    inner = [t for t in range(tiles) if 0 < t < tiles - 1]
    far = lax.ppermute(own, "tile", [(t, other_side(t)) for t in inner])
    begun, waves = call(
        functools.partial(inner_body, row_count),
        "inner",
        (jax.ShapeDtypeStruct((row_count, N), F32), pltpu.VMEM((row_count, PAIR), BF16)),
        (own, mid, back),
        [vmem] * 3,
        (hbm, vmem),
        scratch=[
            pltpu.VMEM((row_count, N - 2 * LANES), F32),
            pltpu.SemaphoreType.DMA((2,)),
        ],
        flops=2 * row_count * PAIR * N,
        moved=4 * row_count * N,
    )
    return call(
        functools.partial(outer_body, row_count),
        "outer",
        jax.ShapeDtypeStruct((row_count, N), F32),
        (near, far, near_pack, far_edge, mid, back, margins, waves, begun),
        [vmem] * 8 + [hbm],
        hbm,
        scratch=[
            pltpu.VMEM((2, row_count, LANES), F32),
            pltpu.SemaphoreType.DMA((2,)),
        ],
        flops=2 * row_count * PAIR * 6 * PAIR,
        moved=4 * row_count * 2 * LANES,
        alias={8: 0},
    )


def solution(mesh):
    in_specs = (
        P(None, "tile"),
        P("tile", None),
        P("kern", "tile"),
        P("kern", None, None),
        P("kern", None, None),
        P("kern"),
    )
    out_specs = P("kern", "tile")
    return jax.shard_map(
        per_device, mesh=mesh, in_specs=in_specs, out_specs=out_specs, check_vma=False
    )
```

```python
import functools
import math

import jax
import jax.numpy as jnp
import ml_dtypes
import numpy as np
from jax import lax
from jax.experimental import pallas as pl
from jax.experimental.pallas import tpu as pltpu
from jax.sharding import PartitionSpec as P

N = 1152
HALO = 64
KF = 64
NE = 1280
LANES = 128
PAIR = 2 * KF
BLOCKS = N // LANES
EDGE = KF
WIDE = 3
GROUPS = BLOCKS // WIDE
MARKS = 16
BF16 = jnp.bfloat16
F32 = jnp.float32
VMEM_LIMIT = 32 * 1024 * 1024


def wave_tables():
    position = np.arange(NE)[:, None]
    frequency = np.arange(KF)[None, :] - KF // 2
    phase = np.mod(position * frequency, NE).astype(np.float64) * (2.0 * math.pi / NE)
    return np.cos(phase).astype(np.float32), np.sin(phase).astype(np.float32)


def transform_tables():
    cos, sin = wave_tables()
    full = np.concatenate([cos, sin], 1)
    mid = full[HALO : HALO + N]
    ct, st = cos[HALO : HALO + N].T, sin[HALO : HALO + N].T
    columns = np.concatenate(
        [
            np.stack([ct.reshape(KF, BLOCKS, LANES), st.reshape(KF, BLOCKS, LANES)], 2),
            np.stack([-st.reshape(KF, BLOCKS, LANES), ct.reshape(KF, BLOCKS, LANES)], 2),
        ],
        0,
    )
    to_columns = columns.transpose(1, 0, 2, 3).reshape(GROUPS, WIDE, PAIR, 2 * LANES)
    to_columns = to_columns.transpose(0, 2, 1, 3).reshape(GROUPS, PAIR, WIDE * 2 * LANES)
    from_columns = to_columns.transpose(0, 2, 1)
    low, high = full[:HALO], full[HALO + N :]
    blank = np.zeros((HALO, PAIR), np.float32)
    rims = np.stack(
        [
            np.concatenate([low[::-1], blank], 0),
            np.concatenate([low, blank], 0),
            np.concatenate([high[::-1], blank], 0),
            np.concatenate([high, blank], 0),
        ]
    )
    back = np.concatenate([cos.T, -sin.T], 0)
    back_low, back_high = back[:, :HALO], back[:, HALO + N :]
    blank = np.zeros((PAIR, HALO), np.float32)
    margins = np.stack(
        [
            np.concatenate([back_high[:, ::-1], blank], 1),
            np.concatenate([back_high, blank], 1),
            np.concatenate([blank, back_low[:, ::-1]], 1),
            np.concatenate([blank, back_low], 1),
        ]
    )
    tables = (mid, mid.T, to_columns, from_columns, rims, back[:, HALO : HALO + N], margins)
    return tuple(np.ascontiguousarray(one).astype(ml_dtypes.bfloat16) for one in tables)


def dot(a, b):
    return jnp.dot(a, b, preferred_element_type=F32)


def in_left_half(shape):
    return lax.broadcasted_iota(jnp.int32, shape, 1) < KF


def swap_halves(pair):
    return pltpu.roll(pair, KF, 1)


def destination(k, step, count):
    return k ^ step if count == 4 else (k - step) % count


def call(
    body, name, outs, args, specs, out_specs=None, scratch=(), flops=0, moved=0
):
    vmem = pl.BlockSpec(memory_space=pltpu.VMEM)
    if out_specs is None:
        out_specs = tuple(vmem for _ in outs) if isinstance(outs, tuple) else vmem
    return pl.pallas_call(
        body,
        name=name,
        out_shape=outs,
        in_specs=specs,
        out_specs=out_specs,
        scratch_shapes=list(scratch),
        compiler_params=pltpu.CompilerParams(vmem_limit_bytes=VMEM_LIMIT),
        cost_estimate=pl.CostEstimate(flops=flops, bytes_accessed=moved, transcendentals=0),
    )(*args)


def edges_body(
    mask, mid, mid_t, real, imag, weight, flags, mate, other, side, held, tall, table, pair, marks, sems
):
    odd = lax.rem(lax.axis_index("tile"), 2) == 1
    copies = [
        pltpu.make_async_copy(mid_t, table, sems.at[0]),
        pltpu.make_async_copy(mask.at[:, :LANES], held.at[:, :LANES], sems.at[1]),
        pltpu.make_async_copy(mask.at[:, N - LANES :], held.at[:, N - LANES :], sems.at[2]),
        pltpu.make_async_copy(real.at[0], pair.at[0], sems.at[3]),
        pltpu.make_async_copy(imag.at[0], pair.at[1], sems.at[4]),
        pltpu.make_async_copy(flags, marks, sems.at[5]),
    ]
    inner = pltpu.make_async_copy(
        mask.at[:, LANES : N - LANES], held.at[:, LANES : N - LANES], sems.at[6]
    )
    columns = pltpu.make_async_copy(mid, tall, sems.at[7])
    for copy in copies:
        copy.start()
    inner.start()
    columns.start()
    for copy in copies[3:]:
        copy.wait()
    scale = jnp.sqrt(jnp.full((KF, KF), 2.0 * weight[0], F32)) * (1.0 / (NE * KF))
    kernel = jnp.concatenate([pair[0] * scale, pair[1] * scale], 1).astype(BF16)
    row = lax.broadcasted_iota(jnp.int32, (16, LANES), 0)
    sides = jnp.where(row == 0, marks[0, 0].astype(F32), marks[0, 1].astype(F32)).astype(BF16)
    side[...] = kernel
    mate[EDGE : 2 * EDGE, :] = kernel
    mate[2 * EDGE :, :] = sides
    other[EDGE:, :] = sides
    for copy in copies[:3]:
        copy.wait()
    strips = jnp.concatenate([held[:, :LANES], held[:, N - LANES :]], 1)
    both = dot(table[...], strips)
    left = in_left_half((KF, LANES))
    first, last = both[:, :LANES], both[:, LANES:]
    first = jnp.where(left, first[:KF], swap_halves(first[KF:]))
    last = jnp.where(left, swap_halves(last[:KF]), last[KF:])
    mate[:EDGE, :] = jnp.where(odd, first, last).astype(BF16)
    other[:EDGE, :] = jnp.where(odd, last, first).astype(BF16)
    inner.wait()
    columns.wait()


def middle_body(mask, mid, mid_t, out):
    out[...] = dot(mid_t[...], dot(mask[...], mid[...]).astype(BF16))


def split_kernel(pair):
    left = in_left_half(pair.shape)
    other = swap_halves(pair)
    return jnp.where(left, pair, other), jnp.where(left, other, pair)


def fields_body(count, row_count, *refs):
    (flags, middle, target, mid, to_columns, from_columns, rims, own) = refs[:8]
    near_pack, *others, far_edge = refs[8 : 8 + count]
    out, a_ref, e_ref, v_ref, u_ref = refs[8 + count :]
    tile = lax.axis_index("tile")
    tiles = lax.axis_size("tile")
    left = in_left_half((KF, PAIR))
    blocks = middle[...]
    low = jnp.where(flags[0, 0] == 1, rims[1], rims[0])
    low = jnp.where(tile == 0, jnp.zeros_like(low), low)
    high = jnp.where(flags[0, 1] == 1, rims[3], rims[2])
    high = jnp.where(tile == tiles - 1, jnp.zeros_like(high), high)
    odd = lax.rem(tile, 2) == 1
    low, high = jnp.where(odd, low, high), jnp.where(odd, high, low)
    for pack, table in ((near_pack, low), (far_edge, high)):
        edge = pack[:EDGE, :].astype(F32)
        edge = jnp.concatenate([edge, swap_halves(edge)], 0).astype(BF16)
        blocks = blocks + dot(edge, table)
    top, bottom = blocks[:KF], swap_halves(blocks[KF:])
    spectrum = jnp.where(left, top - bottom, -(top + bottom))
    turned = swap_halves(spectrum)
    turned = jnp.where(left, -turned, turned)
    kernels = [own[...].astype(F32)]
    kernels.append(near_pack[EDGE : 2 * EDGE, :].astype(F32))
    kernels += [one[...].astype(F32) for one in others]
    kernels = [split_kernel(one) for one in kernels]
    begin = pl.multiple_of(lax.axis_index("kern") * row_count, row_count)
    rows = mid[pl.ds(begin, row_count), :]
    for index, (real, imag) in enumerate(kernels):
        product = real * spectrum + imag * turned
        other = swap_halves(product)
        other = jnp.where(left, -other, other)
        stacked = jnp.concatenate([product, other], 0).astype(BF16)
        a_ref[index * row_count : (index + 1) * row_count, :] = dot(rows, stacked).astype(BF16)
    step = 32 if row_count % 32 == 0 else 16
    e_ref[0] = dot(a_ref[...], to_columns[0])
    for group in range(GROUPS):
        now = group % 2
        if group + 1 < GROUPS:
            e_ref[1 - now] = dot(a_ref[...], to_columns[group + 1])
        for place in range(WIDE):
            first = (group * WIDE + place) * LANES
            halves = [slice((2 * place + half) * LANES, (2 * place + half + 1) * LANES) for half in range(2)]
            for r in range(0, row_count, step):
                total = None
                for index in range(count):
                    at = index * row_count + r
                    real, imag = (e_ref[now, at : at + step, half] for half in halves)
                    term = real * real + imag * imag
                    total = term if total is None else total + term
                wanted = target[r : r + step, first : first + LANES].astype(F32)
                decay = jnp.exp(4.0 - 2.0 * total)
                resist = pl.reciprocal(1.0 + decay, approx=True)
                slope = (resist - wanted) * (8.0 * decay) * (resist * resist)
                for index in range(count):
                    at = index * row_count + r
                    for half in halves:
                        field = e_ref[now, at : at + step, half] * slope
                        v_ref[now, at : at + step, half] = field.astype(BF16)
        part = dot(v_ref[now], from_columns[group])
        if group == 0:
            u_ref[...] = part
        else:
            u_ref[...] += part
    wide = jnp.concatenate(
        [u_ref[i * row_count : (i + 1) * row_count, :].astype(BF16) for i in range(count)], 1
    )
    waves = lax.dot_general(rows, wide, (((0,), (0,)), ((), ())), preferred_element_type=F32)
    total = None
    for index, (real, imag) in enumerate(kernels):
        wave = waves[:, index * PAIR : (index + 1) * PAIR]
        top, bottom = wave[:KF], swap_halves(wave[KF:])
        wave = jnp.where(left, top + bottom, top - bottom)
        other = swap_halves(wave)
        other = jnp.where(left, other, -other)
        term = real * wave + imag * other
        total = term if total is None else total + term
    out[...] = total.astype(BF16)


def sum_body(count, *refs):
    total = refs[0][...].astype(F32)
    for one in refs[1:count]:
        total = total + one[...].astype(F32)
    refs[count][...] = total.astype(BF16)


def row_waves(rows, pair):
    pair = pair.astype(F32)
    other = swap_halves(pair)
    other = jnp.where(in_left_half(pair.shape), -other, other)
    return dot(rows, jnp.concatenate([pair, other], 0).astype(BF16)).astype(BF16)


def own_rows(mid, row_count):
    begin = pl.multiple_of(lax.axis_index("kern") * row_count, row_count)
    return mid[pl.ds(begin, row_count), :]


def inner_body(row_count, own, mid, back, out):
    out[...] = dot(row_waves(own_rows(mid, row_count), own[...]), back[...])


def outer_body(
    row_count, near, far, near_pack, far_edge, mid, margins, begun, out, held, sems
):
    inner = pltpu.make_async_copy(
        begun.at[:, LANES : N - LANES], out.at[:, LANES : N - LANES], sems.at[2]
    )
    inner.start()
    rows = own_rows(mid, row_count)
    near_wave, far_wave = row_waves(rows, near[...]), row_waves(rows, far[...])
    odd = lax.rem(lax.axis_index("tile"), 2) == 1
    below, above = jnp.where(odd, near_wave, far_wave), jnp.where(odd, far_wave, near_wave)
    near_marks = near_pack[2 * EDGE :, :].astype(F32)
    far_marks = far_edge[EDGE:, :].astype(F32)
    low_mark = jnp.where(odd, near_marks, far_marks)[1:2]
    high_mark = jnp.where(odd, far_marks, near_marks)[0:1]
    low = jnp.where(low_mark == 1.0, margins[1].astype(F32), margins[0].astype(F32)).astype(BF16)
    high = jnp.where(high_mark == 1.0, margins[3].astype(F32), margins[2].astype(F32)).astype(BF16)
    copies = []
    for side, first, wave, table in ((0, 0, below, low), (1, N - LANES, above, high)):
        columns = slice(first, first + LANES)
        held[side] = begun[:, columns] + dot(wave, table)
        copies.append(pltpu.make_async_copy(held.at[side], out.at[:, columns], sems.at[side]))
        copies[-1].start()
    for copy in (inner, *copies):
        copy.wait()


def far_off(array):
    return pltpu.with_memory_space_constraint(array, pltpu.HBM)


def per_device(mask_pixels, orientation, target_pattern, kernel_real, kernel_imag, eigen_weights):
    tables = tuple(jnp.asarray(one) for one in transform_tables())
    mid, mid_t, to_columns, from_columns, rims, back, margins = tables
    tiles, count = lax.axis_size("tile"), lax.axis_size("kern")
    row_count = target_pattern.shape[0]
    vmem = pl.BlockSpec(memory_space=pltpu.VMEM)
    smem = pl.BlockSpec(memory_space=pltpu.SMEM)
    hbm = pl.BlockSpec(memory_space=pltpu.HBM)
    small = jax.ShapeDtypeStruct((KF, PAIR), BF16)

    mate, other, side, held, mid, mid_t = call(
        edges_body,
        "edges",
        (
            pltpu.VMEM((2 * EDGE + MARKS, LANES), BF16),
            pltpu.VMEM((EDGE + MARKS, LANES), BF16),
            pltpu.VMEM((KF, PAIR), BF16),
            pltpu.VMEM((N, N), BF16),
            pltpu.VMEM((N, PAIR), BF16),
            pltpu.VMEM((PAIR, N), BF16),
        ),
        (
            *(far_off(one) for one in (mask_pixels, mid, mid_t, kernel_real, kernel_imag)),
            eigen_weights,
            far_off(orientation),
        ),
        [hbm] * 5 + [smem, hbm],
        scratch=[
            pltpu.VMEM((2, KF, KF), F32),
            pltpu.SMEM((1, 2), jnp.int32),
            pltpu.SemaphoreType.DMA((8,)),
        ],
        flops=2 * N * LANES * PAIR * 2,
        moved=N * LANES * 4,
    )

    def swapped(move_tile, step):
        pairs = []
        for t in range(tiles):
            for k in range(count):
                pairs.append((t * count + k, move_tile(t) * count + destination(k, step, count)))
        return pairs

    def chip_mate(t):
        return t ^ 1

    def other_side(t):
        return (t + 1 if t % 2 else t - 1) % tiles

    both = ("tile", "kern")
    far_edge = lax.ppermute(other, both, swapped(other_side, 0))
    near_pack = lax.ppermute(mate, both, swapped(chip_mate, 1))
    kernels = [lax.ppermute(side, both, swapped(lambda t: t, step)) for step in range(2, count)]

    middle = call(
        middle_body,
        "middle",
        jax.ShapeDtypeStruct((PAIR, PAIR), F32),
        (held, mid, mid_t),
        [vmem] * 3,
        flops=4 * N * N * PAIR,
        moved=N * N * 2,
    )

    part = call(
        functools.partial(fields_body, count, row_count),
        "fields",
        small,
        (orientation, middle, target_pattern, mid, to_columns, from_columns, rims, side, near_pack, *kernels, far_edge),
        [smem] + [vmem] * (7 + count),
        scratch=[
            pltpu.VMEM((count * row_count, PAIR), BF16),
            pltpu.VMEM((2, count * row_count, 2 * WIDE * LANES), F32),
            pltpu.VMEM((2, count * row_count, 2 * WIDE * LANES), BF16),
            pltpu.VMEM((count * row_count, PAIR), F32),
        ],
        flops=8 * count * row_count * N * PAIR,
        moved=4 * row_count * N,
    )

    parts = [part]
    for step in range(1, count):
        pairs = [(k, destination(k, step, count)) for k in range(count)]
        parts.append(lax.ppermute(part, "kern", pairs))
    own = call(functools.partial(sum_body, count), "total", small, tuple(parts), [vmem] * count)
    near = lax.ppermute(own, "tile", [(t, chip_mate(t)) for t in range(tiles)])
    inner = [t for t in range(tiles) if 0 < t < tiles - 1]
    far = lax.ppermute(own, "tile", [(t, other_side(t)) for t in inner])
    begun = call(
        functools.partial(inner_body, row_count),
        "inner",
        pltpu.VMEM((row_count, N), F32),
        (own, mid, back),
        [vmem] * 3,
        flops=2 * row_count * PAIR * N,
        moved=4 * row_count * N,
    )
    return call(
        functools.partial(outer_body, row_count),
        "outer",
        jax.ShapeDtypeStruct((row_count, N), F32),
        (near, far, near_pack, far_edge, mid, margins, begun),
        [vmem] * 7,
        hbm,
        scratch=[
            pltpu.VMEM((2, row_count, LANES), F32),
            pltpu.SemaphoreType.DMA((3,)),
        ],
        flops=2 * row_count * PAIR * 6 * PAIR,
        moved=4 * row_count * 2 * LANES,
    )


def solution(mesh):
    in_specs = (
        P(None, "tile"),
        P("tile", None),
        P("kern", "tile"),
        P("kern", None, None),
        P("kern", None, None),
        P("kern"),
    )
    out_specs = P("kern", "tile")
    return jax.shard_map(
        per_device, mesh=mesh, in_specs=in_specs, out_specs=out_specs, check_vma=False
    )
```

```python
import functools
import math

import jax
import jax.numpy as jnp
import ml_dtypes
import numpy as np
from jax import lax
from jax.experimental import pallas as pl
from jax.experimental.pallas import tpu as pltpu
from jax.sharding import PartitionSpec as P

N = 1152
HALO = 64
KF = 64
NE = 1280
LANES = 128
PAIR = 2 * KF
BLOCKS = N // LANES
EDGE = KF
WIDE = 3
GROUPS = BLOCKS // WIDE
MARKS = 16
BF16 = jnp.bfloat16
F32 = jnp.float32
VMEM_LIMIT = 32 * 1024 * 1024


def wave_tables():
    position = np.arange(NE)[:, None]
    frequency = np.arange(KF)[None, :] - KF // 2
    phase = np.mod(position * frequency, NE).astype(np.float64) * (2.0 * math.pi / NE)
    return np.cos(phase).astype(np.float32), np.sin(phase).astype(np.float32)


def transform_tables():
    cos, sin = wave_tables()
    full = np.concatenate([cos, sin], 1)
    mid = full[HALO : HALO + N]
    ct, st = cos[HALO : HALO + N].T, sin[HALO : HALO + N].T
    columns = np.concatenate(
        [
            np.stack([ct.reshape(KF, BLOCKS, LANES), st.reshape(KF, BLOCKS, LANES)], 2),
            np.stack([-st.reshape(KF, BLOCKS, LANES), ct.reshape(KF, BLOCKS, LANES)], 2),
        ],
        0,
    )
    to_columns = columns.transpose(1, 0, 2, 3).reshape(GROUPS, WIDE, PAIR, 2 * LANES)
    to_columns = to_columns.transpose(0, 2, 1, 3).reshape(GROUPS, PAIR, WIDE * 2 * LANES)
    from_columns = to_columns.transpose(0, 2, 1)
    low, high = full[:HALO], full[HALO + N :]
    blank = np.zeros((HALO, PAIR), np.float32)
    rims = np.stack(
        [
            np.concatenate([low[::-1], blank], 0),
            np.concatenate([low, blank], 0),
            np.concatenate([high[::-1], blank], 0),
            np.concatenate([high, blank], 0),
        ]
    )
    back = np.concatenate([cos.T, -sin.T], 0)
    back_low, back_high = back[:, :HALO], back[:, HALO + N :]
    blank = np.zeros((PAIR, HALO), np.float32)
    margins = np.stack(
        [
            np.concatenate([back_high[:, ::-1], blank], 1),
            np.concatenate([back_high, blank], 1),
            np.concatenate([blank, back_low[:, ::-1]], 1),
            np.concatenate([blank, back_low], 1),
        ]
    )
    tables = (mid, mid.T, to_columns, from_columns, rims, back[:, HALO : HALO + N], margins)
    return tuple(np.ascontiguousarray(one).astype(ml_dtypes.bfloat16) for one in tables)


def dot(a, b):
    return jnp.dot(a, b, preferred_element_type=F32)


def in_left_half(shape):
    return lax.broadcasted_iota(jnp.int32, shape, 1) < KF


def swap_halves(pair):
    return pltpu.roll(pair, KF, 1)


def destination(k, step, count):
    return k ^ step if count == 4 else (k - step) % count


def call(
    body, name, outs, args, specs, out_specs=None, scratch=(), flops=0, moved=0
):
    vmem = pl.BlockSpec(memory_space=pltpu.VMEM)
    if out_specs is None:
        out_specs = tuple(vmem for _ in outs) if isinstance(outs, tuple) else vmem
    return pl.pallas_call(
        body,
        name=name,
        out_shape=outs,
        in_specs=specs,
        out_specs=out_specs,
        scratch_shapes=list(scratch),
        compiler_params=pltpu.CompilerParams(vmem_limit_bytes=VMEM_LIMIT),
        cost_estimate=pl.CostEstimate(flops=flops, bytes_accessed=moved, transcendentals=0),
    )(*args)


def edges_body(
    mask, mid, mid_t, real, imag, weight, flags, mate, other, side, held, tall, table, pair, marks, sems
):
    odd = lax.rem(lax.axis_index("tile"), 2) == 1
    copies = [
        pltpu.make_async_copy(mid_t, table, sems.at[0]),
        pltpu.make_async_copy(mask.at[:, :LANES], held.at[:, :LANES], sems.at[1]),
        pltpu.make_async_copy(mask.at[:, N - LANES :], held.at[:, N - LANES :], sems.at[2]),
        pltpu.make_async_copy(real.at[0], pair.at[0], sems.at[3]),
        pltpu.make_async_copy(imag.at[0], pair.at[1], sems.at[4]),
        pltpu.make_async_copy(flags, marks, sems.at[5]),
    ]
    inner = pltpu.make_async_copy(
        mask.at[:, LANES : N - LANES], held.at[:, LANES : N - LANES], sems.at[6]
    )
    columns = pltpu.make_async_copy(mid, tall, sems.at[7])
    for copy in copies:
        copy.start()
    inner.start()
    columns.start()
    for copy in copies[3:]:
        copy.wait()
    scale = jnp.sqrt(jnp.full((KF, KF), 2.0 * weight[0], F32)) * (1.0 / (NE * KF))
    kernel = jnp.concatenate([pair[0] * scale, pair[1] * scale], 1).astype(BF16)
    row = lax.broadcasted_iota(jnp.int32, (16, LANES), 0)
    sides = jnp.where(row == 0, marks[0, 0].astype(F32), marks[0, 1].astype(F32)).astype(BF16)
    side[...] = kernel
    mate[EDGE : 2 * EDGE, :] = kernel
    mate[2 * EDGE :, :] = sides
    other[EDGE:, :] = sides
    for copy in copies[:3]:
        copy.wait()
    strips = jnp.concatenate([held[:, :LANES], held[:, N - LANES :]], 1)
    both = dot(table[...], strips)
    left = in_left_half((KF, LANES))
    first, last = both[:, :LANES], both[:, LANES:]
    first = jnp.where(left, first[:KF], swap_halves(first[KF:]))
    last = jnp.where(left, swap_halves(last[:KF]), last[KF:])
    mate[:EDGE, :] = jnp.where(odd, first, last).astype(BF16)
    other[:EDGE, :] = jnp.where(odd, last, first).astype(BF16)
    inner.wait()
    columns.wait()


def middle_body(mask, mid, mid_t, out):
    out[...] = dot(mid_t[...], dot(mask[...], mid[...]).astype(BF16))


def split_kernel(pair):
    left = in_left_half(pair.shape)
    other = swap_halves(pair)
    return jnp.where(left, pair, other), jnp.where(left, other, pair)


def fields_body(count, row_count, *refs):
    (flags, middle, target, mid, to_columns, from_columns, rims, own) = refs[:8]
    near_pack, *others, far_edge = refs[8 : 8 + count]
    out, a_ref, e_ref, v_ref, u_ref = refs[8 + count :]
    tile = lax.axis_index("tile")
    tiles = lax.axis_size("tile")
    left = in_left_half((KF, PAIR))
    blocks = middle[...]
    low = jnp.where(flags[0, 0] == 1, rims[1], rims[0])
    low = jnp.where(tile == 0, jnp.zeros_like(low), low)
    high = jnp.where(flags[0, 1] == 1, rims[3], rims[2])
    high = jnp.where(tile == tiles - 1, jnp.zeros_like(high), high)
    odd = lax.rem(tile, 2) == 1
    low, high = jnp.where(odd, low, high), jnp.where(odd, high, low)
    for pack, table in ((near_pack, low), (far_edge, high)):
        edge = pack[:EDGE, :].astype(F32)
        edge = jnp.concatenate([edge, swap_halves(edge)], 0).astype(BF16)
        blocks = blocks + dot(edge, table)
    top, bottom = blocks[:KF], swap_halves(blocks[KF:])
    spectrum = jnp.where(left, top - bottom, -(top + bottom))
    turned = swap_halves(spectrum)
    turned = jnp.where(left, -turned, turned)
    kernels = [own[...].astype(F32)]
    kernels.append(near_pack[EDGE : 2 * EDGE, :].astype(F32))
    kernels += [one[...].astype(F32) for one in others]
    kernels = [split_kernel(one) for one in kernels]
    begin = pl.multiple_of(lax.axis_index("kern") * row_count, row_count)
    rows = mid[pl.ds(begin, row_count), :]
    stacks = []
    for real, imag in kernels:
        product = real * spectrum + imag * turned
        other = swap_halves(product)
        other = jnp.where(left, -other, other)
        stacks.append(jnp.concatenate([product, other], 0).astype(BF16))
    waves = dot(rows, jnp.concatenate(stacks, 1)).astype(BF16)
    for index in range(count):
        a_ref[index * row_count : (index + 1) * row_count, :] = waves[:, index * PAIR : (index + 1) * PAIR]
    step = 32 if row_count % 32 == 0 else 16
    e_ref[0] = dot(a_ref[...], to_columns[0]).astype(BF16)
    for group in range(GROUPS):
        now = group % 2
        if group + 1 < GROUPS:
            e_ref[1 - now] = dot(a_ref[...], to_columns[group + 1]).astype(BF16)
        for place in range(WIDE):
            first = (group * WIDE + place) * LANES
            halves = [slice((2 * place + half) * LANES, (2 * place + half + 1) * LANES) for half in range(2)]
            for r in range(0, row_count, step):
                total = None
                for index in range(count):
                    at = index * row_count + r
                    real, imag = (e_ref[now, at : at + step, half] for half in halves)
                    term = (real * real + imag * imag).astype(F32)
                    total = term if total is None else total + term
                wanted = target[r : r + step, first : first + LANES].astype(F32)
                decay = jnp.exp(4.0 - 2.0 * total)
                resist = pl.reciprocal(1.0 + decay, approx=True)
                slope = (resist - wanted) * (8.0 * decay) * (resist * resist)
                slope = slope.astype(BF16)
                for index in range(count):
                    at = index * row_count + r
                    for half in halves:
                        v_ref[now, at : at + step, half] = e_ref[now, at : at + step, half] * slope
        part = dot(v_ref[now], from_columns[group])
        if group == 0:
            u_ref[...] = part
        else:
            u_ref[...] += part
    wide = jnp.concatenate(
        [u_ref[i * row_count : (i + 1) * row_count, :].astype(BF16) for i in range(count)], 1
    )
    waves = lax.dot_general(rows, wide, (((0,), (0,)), ((), ())), preferred_element_type=F32)
    total = None
    for index, (real, imag) in enumerate(kernels):
        wave = waves[:, index * PAIR : (index + 1) * PAIR]
        top, bottom = wave[:KF], swap_halves(wave[KF:])
        wave = jnp.where(left, top + bottom, top - bottom)
        other = swap_halves(wave)
        other = jnp.where(left, other, -other)
        term = real * wave + imag * other
        total = term if total is None else total + term
    out[...] = total.astype(BF16)


def sum_body(count, *refs):
    total = refs[0][...].astype(F32)
    for one in refs[1:count]:
        total = total + one[...].astype(F32)
    refs[count][...] = total.astype(BF16)


def row_waves(rows, pair):
    pair = pair.astype(F32)
    other = swap_halves(pair)
    other = jnp.where(in_left_half(pair.shape), -other, other)
    return dot(rows, jnp.concatenate([pair, other], 0).astype(BF16)).astype(BF16)


def own_rows(mid, row_count):
    begin = pl.multiple_of(lax.axis_index("kern") * row_count, row_count)
    return mid[pl.ds(begin, row_count), :]


def inner_body(row_count, own, mid, back, out):
    out[...] = dot(row_waves(own_rows(mid, row_count), own[...]), back[...])


def outer_body(
    row_count, near, far, near_pack, far_edge, mid, margins, begun, out, held, sems
):
    inner = pltpu.make_async_copy(
        begun.at[:, LANES : N - LANES], out.at[:, LANES : N - LANES], sems.at[2]
    )
    inner.start()
    rows = own_rows(mid, row_count)
    near_wave, far_wave = row_waves(rows, near[...]), row_waves(rows, far[...])
    odd = lax.rem(lax.axis_index("tile"), 2) == 1
    below, above = jnp.where(odd, near_wave, far_wave), jnp.where(odd, far_wave, near_wave)
    near_marks = near_pack[2 * EDGE :, :].astype(F32)
    far_marks = far_edge[EDGE:, :].astype(F32)
    low_mark = jnp.where(odd, near_marks, far_marks)[1:2]
    high_mark = jnp.where(odd, far_marks, near_marks)[0:1]
    low = jnp.where(low_mark == 1.0, margins[1].astype(F32), margins[0].astype(F32)).astype(BF16)
    high = jnp.where(high_mark == 1.0, margins[3].astype(F32), margins[2].astype(F32)).astype(BF16)
    copies = []
    for side, first, wave, table in ((0, 0, below, low), (1, N - LANES, above, high)):
        columns = slice(first, first + LANES)
        held[side] = begun[:, columns] + dot(wave, table)
        copies.append(pltpu.make_async_copy(held.at[side], out.at[:, columns], sems.at[side]))
        copies[-1].start()
    for copy in (inner, *copies):
        copy.wait()


def far_off(array):
    return pltpu.with_memory_space_constraint(array, pltpu.HBM)


def per_device(mask_pixels, orientation, target_pattern, kernel_real, kernel_imag, eigen_weights):
    tables = tuple(jnp.asarray(one) for one in transform_tables())
    mid, mid_t, to_columns, from_columns, rims, back, margins = tables
    tiles, count = lax.axis_size("tile"), lax.axis_size("kern")
    row_count = target_pattern.shape[0]
    vmem = pl.BlockSpec(memory_space=pltpu.VMEM)
    smem = pl.BlockSpec(memory_space=pltpu.SMEM)
    hbm = pl.BlockSpec(memory_space=pltpu.HBM)
    small = jax.ShapeDtypeStruct((KF, PAIR), BF16)

    mate, other, side, held, mid, mid_t = call(
        edges_body,
        "edges",
        (
            pltpu.VMEM((2 * EDGE + MARKS, LANES), BF16),
            pltpu.VMEM((EDGE + MARKS, LANES), BF16),
            pltpu.VMEM((KF, PAIR), BF16),
            pltpu.VMEM((N, N), BF16),
            pltpu.VMEM((N, PAIR), BF16),
            pltpu.VMEM((PAIR, N), BF16),
        ),
        (
            *(far_off(one) for one in (mask_pixels, mid, mid_t, kernel_real, kernel_imag)),
            eigen_weights,
            far_off(orientation),
        ),
        [hbm] * 5 + [smem, hbm],
        scratch=[
            pltpu.VMEM((2, KF, KF), F32),
            pltpu.SMEM((1, 2), jnp.int32),
            pltpu.SemaphoreType.DMA((8,)),
        ],
        flops=2 * N * LANES * PAIR * 2,
        moved=N * LANES * 4,
    )

    def swapped(move_tile, step):
        pairs = []
        for t in range(tiles):
            for k in range(count):
                pairs.append((t * count + k, move_tile(t) * count + destination(k, step, count)))
        return pairs

    def chip_mate(t):
        return t ^ 1

    def other_side(t):
        return (t + 1 if t % 2 else t - 1) % tiles

    both = ("tile", "kern")
    far_edge = lax.ppermute(other, both, swapped(other_side, 0))
    near_pack = lax.ppermute(mate, both, swapped(chip_mate, 1))
    kernels = [lax.ppermute(side, both, swapped(lambda t: t, step)) for step in range(2, count)]

    middle = call(
        middle_body,
        "middle",
        jax.ShapeDtypeStruct((PAIR, PAIR), F32),
        (held, mid, mid_t),
        [vmem] * 3,
        flops=4 * N * N * PAIR,
        moved=N * N * 2,
    )

    part = call(
        functools.partial(fields_body, count, row_count),
        "fields",
        small,
        (orientation, middle, target_pattern, mid, to_columns, from_columns, rims, side, near_pack, *kernels, far_edge),
        [smem] + [vmem] * (7 + count),
        scratch=[
            pltpu.VMEM((count * row_count, PAIR), BF16),
            pltpu.VMEM((2, count * row_count, 2 * WIDE * LANES), BF16),
            pltpu.VMEM((2, count * row_count, 2 * WIDE * LANES), BF16),
            pltpu.VMEM((count * row_count, PAIR), F32),
        ],
        flops=8 * count * row_count * N * PAIR,
        moved=4 * row_count * N,
    )

    parts = [part]
    for step in range(1, count):
        pairs = [(k, destination(k, step, count)) for k in range(count)]
        parts.append(lax.ppermute(part, "kern", pairs))
    own = call(functools.partial(sum_body, count), "total", small, tuple(parts), [vmem] * count)
    near = lax.ppermute(own, "tile", [(t, chip_mate(t)) for t in range(tiles)])
    inner = [t for t in range(tiles) if 0 < t < tiles - 1]
    far = lax.ppermute(own, "tile", [(t, other_side(t)) for t in inner])
    begun = call(
        functools.partial(inner_body, row_count),
        "inner",
        pltpu.VMEM((row_count, N), F32),
        (own, mid, back),
        [vmem] * 3,
        flops=2 * row_count * PAIR * N,
        moved=4 * row_count * N,
    )
    return call(
        functools.partial(outer_body, row_count),
        "outer",
        jax.ShapeDtypeStruct((row_count, N), F32),
        (near, far, near_pack, far_edge, mid, margins, begun),
        [vmem] * 7,
        hbm,
        scratch=[
            pltpu.VMEM((2, row_count, LANES), F32),
            pltpu.SemaphoreType.DMA((3,)),
        ],
        flops=2 * row_count * PAIR * 6 * PAIR,
        moved=4 * row_count * 2 * LANES,
    )


def solution(mesh):
    in_specs = (
        P(None, "tile"),
        P("tile", None),
        P("kern", "tile"),
        P("kern", None, None),
        P("kern", None, None),
        P("kern"),
    )
    out_specs = P("kern", "tile")
    return jax.shard_map(
        per_device, mesh=mesh, in_specs=in_specs, out_specs=out_specs, check_vma=False
    )
```

```python
import functools
import math

import jax
import jax.numpy as jnp
import ml_dtypes
import numpy as np
from jax import lax
from jax.experimental import pallas as pl
from jax.experimental.pallas import tpu as pltpu
from jax.sharding import PartitionSpec as P

N = 1152
HALO = 64
KF = 64
NE = 1280
LANES = 128
PAIR = 2 * KF
BLOCKS = N // LANES
EDGE = KF
MARKS = 16
BF16 = jnp.bfloat16
F32 = jnp.float32
VMEM_LIMIT = 32 * 1024 * 1024


def wave_tables():
    position = np.arange(NE)[:, None]
    frequency = np.arange(KF)[None, :] - KF // 2
    phase = np.mod(position * frequency, NE).astype(np.float64) * (2.0 * math.pi / NE)
    return np.cos(phase).astype(np.float32), np.sin(phase).astype(np.float32)


def transform_tables():
    cos, sin = wave_tables()
    full = np.concatenate([cos, sin], 1)
    mid = full[HALO : HALO + N]
    ct, st = cos[HALO : HALO + N].T, sin[HALO : HALO + N].T
    columns = np.concatenate(
        [
            np.stack([ct.reshape(KF, BLOCKS, LANES), st.reshape(KF, BLOCKS, LANES)], 2),
            np.stack([-st.reshape(KF, BLOCKS, LANES), ct.reshape(KF, BLOCKS, LANES)], 2),
        ],
        0,
    )
    to_columns = columns.transpose(1, 0, 2, 3).reshape(BLOCKS, PAIR, 2 * LANES)
    from_columns = to_columns.transpose(0, 2, 1)
    low, high = full[:HALO], full[HALO + N :]
    blank = np.zeros((HALO, PAIR), np.float32)
    rims = np.stack(
        [
            np.concatenate([low[::-1], blank], 0),
            np.concatenate([low, blank], 0),
            np.concatenate([high[::-1], blank], 0),
            np.concatenate([high, blank], 0),
        ]
    )
    back = np.concatenate([cos.T, -sin.T], 0)
    back_low, back_high = back[:, :HALO], back[:, HALO + N :]
    blank = np.zeros((PAIR, HALO), np.float32)
    margins = np.stack(
        [
            np.concatenate([back_high[:, ::-1], blank], 1),
            np.concatenate([back_high, blank], 1),
            np.concatenate([blank, back_low[:, ::-1]], 1),
            np.concatenate([blank, back_low], 1),
        ]
    )
    tables = (mid, mid.T, to_columns, from_columns, rims, back[:, HALO : HALO + N], margins)
    return tuple(np.ascontiguousarray(one).astype(ml_dtypes.bfloat16) for one in tables)


def dot(a, b):
    return jnp.dot(a, b, preferred_element_type=F32)


def in_left_half(shape):
    return lax.broadcasted_iota(jnp.int32, shape, 1) < KF


def swap_halves(pair):
    return pltpu.roll(pair, KF, 1)


def destination(k, step, count):
    return k ^ step if count == 4 else (k - step) % count


def call(
    body, name, outs, args, specs, out_specs=None, scratch=(), flops=0, moved=0
):
    vmem = pl.BlockSpec(memory_space=pltpu.VMEM)
    if out_specs is None:
        out_specs = tuple(vmem for _ in outs) if isinstance(outs, tuple) else vmem
    return pl.pallas_call(
        body,
        name=name,
        out_shape=outs,
        in_specs=specs,
        out_specs=out_specs,
        scratch_shapes=list(scratch),
        compiler_params=pltpu.CompilerParams(vmem_limit_bytes=VMEM_LIMIT),
        cost_estimate=pl.CostEstimate(flops=flops, bytes_accessed=moved, transcendentals=0),
    )(*args)


def edges_body(
    mask, mid, mid_t, real, imag, weight, flags, mate, other, side, held, tall, table, pair, marks, sems
):
    odd = lax.rem(lax.axis_index("tile"), 2) == 1
    copies = [
        pltpu.make_async_copy(mid_t, table, sems.at[0]),
        pltpu.make_async_copy(mask.at[:, :LANES], held.at[:, :LANES], sems.at[1]),
        pltpu.make_async_copy(mask.at[:, N - LANES :], held.at[:, N - LANES :], sems.at[2]),
        pltpu.make_async_copy(real.at[0], pair.at[0], sems.at[3]),
        pltpu.make_async_copy(imag.at[0], pair.at[1], sems.at[4]),
        pltpu.make_async_copy(flags, marks, sems.at[5]),
    ]
    inner = pltpu.make_async_copy(
        mask.at[:, LANES : N - LANES], held.at[:, LANES : N - LANES], sems.at[6]
    )
    columns = pltpu.make_async_copy(mid, tall, sems.at[7])
    for copy in copies:
        copy.start()
    inner.start()
    columns.start()
    for copy in copies[3:]:
        copy.wait()
    scale = jnp.sqrt(jnp.full((KF, KF), 2.0 * weight[0], F32)) * (1.0 / (NE * KF))
    kernel = jnp.concatenate([pair[0] * scale, pair[1] * scale], 1).astype(BF16)
    row = lax.broadcasted_iota(jnp.int32, (16, LANES), 0)
    sides = jnp.where(row == 0, marks[0, 0].astype(F32), marks[0, 1].astype(F32)).astype(BF16)
    side[...] = kernel
    mate[EDGE : 2 * EDGE, :] = kernel
    mate[2 * EDGE :, :] = sides
    other[EDGE:, :] = sides
    for copy in copies[:3]:
        copy.wait()
    strips = jnp.concatenate([held[:, :LANES], held[:, N - LANES :]], 1)
    both = dot(table[...], strips)
    left = in_left_half((KF, LANES))
    first, last = both[:, :LANES], both[:, LANES:]
    first = jnp.where(left, first[:KF], swap_halves(first[KF:]))
    last = jnp.where(left, swap_halves(last[:KF]), last[KF:])
    mate[:EDGE, :] = jnp.where(odd, first, last).astype(BF16)
    other[:EDGE, :] = jnp.where(odd, last, first).astype(BF16)
    inner.wait()
    columns.wait()


def middle_body(mask, mid, mid_t, out):
    out[...] = dot(mid_t[...], dot(mask[...], mid[...]).astype(BF16))


def split_kernel(pair):
    left = in_left_half(pair.shape)
    other = swap_halves(pair)
    return jnp.where(left, pair, other), jnp.where(left, other, pair)


def fields_body(count, row_count, *refs):
    (flags, middle, target, mid, to_columns, from_columns, rims, own) = refs[:8]
    near_pack, *others, far_edge = refs[8 : 8 + count]
    out, a_ref, field_a, field_b, bent_a, bent_b, u_ref = refs[8 + count :]
    fields, bent = (field_a, field_b), (bent_a, bent_b)
    tile = lax.axis_index("tile")
    tiles = lax.axis_size("tile")
    left = in_left_half((KF, PAIR))
    blocks = middle[...]
    low = jnp.where(flags[0, 0] == 1, rims[1], rims[0])
    low = jnp.where(tile == 0, jnp.zeros_like(low), low)
    high = jnp.where(flags[0, 1] == 1, rims[3], rims[2])
    high = jnp.where(tile == tiles - 1, jnp.zeros_like(high), high)
    odd = lax.rem(tile, 2) == 1
    low, high = jnp.where(odd, low, high), jnp.where(odd, high, low)
    for pack, table in ((near_pack, low), (far_edge, high)):
        edge = pack[:EDGE, :].astype(F32)
        edge = jnp.concatenate([edge, swap_halves(edge)], 0).astype(BF16)
        blocks = blocks + dot(edge, table)
    top, bottom = blocks[:KF], swap_halves(blocks[KF:])
    spectrum = jnp.where(left, top - bottom, -(top + bottom))
    turned = swap_halves(spectrum)
    turned = jnp.where(left, -turned, turned)
    kernels = [own[...].astype(F32)]
    kernels.append(near_pack[EDGE : 2 * EDGE, :].astype(F32))
    kernels += [one[...].astype(F32) for one in others]
    kernels = [split_kernel(one) for one in kernels]
    begin = pl.multiple_of(lax.axis_index("kern") * row_count, row_count)
    rows = mid[pl.ds(begin, row_count), :]
    stacks = []
    for real, imag in kernels:
        product = real * spectrum + imag * turned
        other = swap_halves(product)
        other = jnp.where(left, -other, other)
        stacks.append(jnp.concatenate([product, other], 0).astype(BF16))
    waves = dot(rows, jnp.concatenate(stacks, 1)).astype(BF16)
    for index in range(count):
        a_ref[index * row_count : (index + 1) * row_count, :] = waves[:, index * PAIR : (index + 1) * PAIR]
    step = 32 if row_count % 32 == 0 else 16
    halves = (slice(0, LANES), slice(LANES, 2 * LANES))
    fields[0][...] = dot(a_ref[...], to_columns[0])
    for block in range(BLOCKS + 1):
        now = block % 2
        if block + 1 < BLOCKS:
            fields[1 - now][...] = dot(a_ref[...], to_columns[block + 1])
        if block > 0:
            part = dot(bent[1 - now][...], from_columns[block - 1])
            u_ref[...] = part if block == 1 else u_ref[...] + part
        if block == BLOCKS:
            continue
        for r in range(0, row_count, step):
            total = None
            for index in range(count):
                at = index * row_count + r
                real, imag = (fields[now][at : at + step, half] for half in halves)
                term = real * real + imag * imag
                total = term if total is None else total + term
            wanted = target[r : r + step, block * LANES : (block + 1) * LANES].astype(F32)
            decay = jnp.exp(4.0 - 2.0 * total)
            resist = pl.reciprocal(1.0 + decay, approx=True)
            slope = (resist - wanted) * (8.0 * decay) * (resist * resist)
            for index in range(count):
                at = index * row_count + r
                for half in halves:
                    field = fields[now][at : at + step, half] * slope
                    bent[now][at : at + step, half] = field.astype(BF16)
    wide = jnp.concatenate(
        [u_ref[i * row_count : (i + 1) * row_count, :].astype(BF16) for i in range(count)], 1
    )
    waves = lax.dot_general(rows, wide, (((0,), (0,)), ((), ())), preferred_element_type=F32)
    total = None
    for index, (real, imag) in enumerate(kernels):
        wave = waves[:, index * PAIR : (index + 1) * PAIR]
        top, bottom = wave[:KF], swap_halves(wave[KF:])
        wave = jnp.where(left, top + bottom, top - bottom)
        other = swap_halves(wave)
        other = jnp.where(left, other, -other)
        term = real * wave + imag * other
        total = term if total is None else total + term
    out[...] = total.astype(BF16)


def sum_body(count, *refs):
    total = refs[0][...].astype(F32)
    for one in refs[1:count]:
        total = total + one[...].astype(F32)
    refs[count][...] = total.astype(BF16)


def row_waves(rows, pair):
    pair = pair.astype(F32)
    other = swap_halves(pair)
    other = jnp.where(in_left_half(pair.shape), -other, other)
    return dot(rows, jnp.concatenate([pair, other], 0).astype(BF16)).astype(BF16)


def own_rows(mid, row_count):
    begin = pl.multiple_of(lax.axis_index("kern") * row_count, row_count)
    return mid[pl.ds(begin, row_count), :]


def inner_body(row_count, own, mid, back, out):
    out[...] = dot(row_waves(own_rows(mid, row_count), own[...]), back[...])


def outer_body(
    row_count, near, far, near_pack, far_edge, mid, margins, begun, out, held, sems
):
    inner = pltpu.make_async_copy(
        begun.at[:, LANES : N - LANES], out.at[:, LANES : N - LANES], sems.at[2]
    )
    inner.start()
    rows = own_rows(mid, row_count)
    near_wave, far_wave = row_waves(rows, near[...]), row_waves(rows, far[...])
    odd = lax.rem(lax.axis_index("tile"), 2) == 1
    below, above = jnp.where(odd, near_wave, far_wave), jnp.where(odd, far_wave, near_wave)
    near_marks = near_pack[2 * EDGE :, :].astype(F32)
    far_marks = far_edge[EDGE:, :].astype(F32)
    low_mark = jnp.where(odd, near_marks, far_marks)[1:2]
    high_mark = jnp.where(odd, far_marks, near_marks)[0:1]
    low = jnp.where(low_mark == 1.0, margins[1].astype(F32), margins[0].astype(F32)).astype(BF16)
    high = jnp.where(high_mark == 1.0, margins[3].astype(F32), margins[2].astype(F32)).astype(BF16)
    copies = []
    for side, first, wave, table in ((0, 0, below, low), (1, N - LANES, above, high)):
        columns = slice(first, first + LANES)
        held[side] = begun[:, columns] + dot(wave, table)
        copies.append(pltpu.make_async_copy(held.at[side], out.at[:, columns], sems.at[side]))
        copies[-1].start()
    for copy in (inner, *copies):
        copy.wait()


def far_off(array):
    return pltpu.with_memory_space_constraint(array, pltpu.HBM)


def per_device(mask_pixels, orientation, target_pattern, kernel_real, kernel_imag, eigen_weights):
    tables = tuple(jnp.asarray(one) for one in transform_tables())
    mid, mid_t, to_columns, from_columns, rims, back, margins = tables
    tiles, count = lax.axis_size("tile"), lax.axis_size("kern")
    row_count = target_pattern.shape[0]
    vmem = pl.BlockSpec(memory_space=pltpu.VMEM)
    smem = pl.BlockSpec(memory_space=pltpu.SMEM)
    hbm = pl.BlockSpec(memory_space=pltpu.HBM)
    small = jax.ShapeDtypeStruct((KF, PAIR), BF16)

    mate, other, side, held, mid, mid_t = call(
        edges_body,
        "edges",
        (
            pltpu.VMEM((2 * EDGE + MARKS, LANES), BF16),
            pltpu.VMEM((EDGE + MARKS, LANES), BF16),
            pltpu.VMEM((KF, PAIR), BF16),
            pltpu.VMEM((N, N), BF16),
            pltpu.VMEM((N, PAIR), BF16),
            pltpu.VMEM((PAIR, N), BF16),
        ),
        (
            *(far_off(one) for one in (mask_pixels, mid, mid_t, kernel_real, kernel_imag)),
            eigen_weights,
            far_off(orientation),
        ),
        [hbm] * 5 + [smem, hbm],
        scratch=[
            pltpu.VMEM((2, KF, KF), F32),
            pltpu.SMEM((1, 2), jnp.int32),
            pltpu.SemaphoreType.DMA((8,)),
        ],
        flops=2 * N * LANES * PAIR * 2,
        moved=N * LANES * 4,
    )

    def swapped(move_tile, step):
        pairs = []
        for t in range(tiles):
            for k in range(count):
                pairs.append((t * count + k, move_tile(t) * count + destination(k, step, count)))
        return pairs

    def chip_mate(t):
        return t ^ 1

    def other_side(t):
        return (t + 1 if t % 2 else t - 1) % tiles

    both = ("tile", "kern")
    far_edge = lax.ppermute(other, both, swapped(other_side, 0))
    near_pack = lax.ppermute(mate, both, swapped(chip_mate, 1))
    kernels = [lax.ppermute(side, both, swapped(lambda t: t, step)) for step in range(2, count)]

    middle = call(
        middle_body,
        "middle",
        jax.ShapeDtypeStruct((PAIR, PAIR), F32),
        (held, mid, mid_t),
        [vmem] * 3,
        flops=4 * N * N * PAIR,
        moved=N * N * 2,
    )

    part = call(
        functools.partial(fields_body, count, row_count),
        "fields",
        small,
        (orientation, middle, target_pattern, mid, to_columns, from_columns, rims, side, near_pack, *kernels, far_edge),
        [smem] + [vmem] * (7 + count),
        scratch=[
            pltpu.VMEM((count * row_count, PAIR), BF16),
            pltpu.VMEM((count * row_count, 2 * LANES), F32),
            pltpu.VMEM((count * row_count, 2 * LANES), F32),
            pltpu.VMEM((count * row_count, 2 * LANES), BF16),
            pltpu.VMEM((count * row_count, 2 * LANES), BF16),
            pltpu.VMEM((count * row_count, PAIR), F32),
        ],
        flops=8 * count * row_count * N * PAIR,
        moved=4 * row_count * N,
    )

    parts = [part]
    for step in range(1, count):
        pairs = [(k, destination(k, step, count)) for k in range(count)]
        parts.append(lax.ppermute(part, "kern", pairs))
    own = call(functools.partial(sum_body, count), "total", small, tuple(parts), [vmem] * count)
    near = lax.ppermute(own, "tile", [(t, chip_mate(t)) for t in range(tiles)])
    inner = [t for t in range(tiles) if 0 < t < tiles - 1]
    far = lax.ppermute(own, "tile", [(t, other_side(t)) for t in inner])
    begun = call(
        functools.partial(inner_body, row_count),
        "inner",
        pltpu.VMEM((row_count, N), F32),
        (own, mid, back),
        [vmem] * 3,
        flops=2 * row_count * PAIR * N,
        moved=4 * row_count * N,
    )
    return call(
        functools.partial(outer_body, row_count),
        "outer",
        jax.ShapeDtypeStruct((row_count, N), F32),
        (near, far, near_pack, far_edge, mid, margins, begun),
        [vmem] * 7,
        hbm,
        scratch=[
            pltpu.VMEM((2, row_count, LANES), F32),
            pltpu.SemaphoreType.DMA((3,)),
        ],
        flops=2 * row_count * PAIR * 6 * PAIR,
        moved=4 * row_count * 2 * LANES,
    )


def solution(mesh):
    in_specs = (
        P(None, "tile"),
        P("tile", None),
        P("kern", "tile"),
        P("kern", None, None),
        P("kern", None, None),
        P("kern"),
    )
    out_specs = P("kern", "tile")
    return jax.shard_map(
        per_device, mesh=mesh, in_specs=in_specs, out_specs=out_specs, check_vma=False
    )
```

```python
import functools
import math

import jax
import jax.numpy as jnp
import ml_dtypes
import numpy as np
from jax import lax
from jax.experimental import pallas as pl
from jax.experimental.pallas import tpu as pltpu
from jax.sharding import PartitionSpec as P

N = 1152
HALO = 64
KF = 64
NE = 1280
LANES = 128
PAIR = 2 * KF
BLOCKS = N // LANES
EDGE = KF
MARKS = 16
BF16 = jnp.bfloat16
F32 = jnp.float32
VMEM_LIMIT = 32 * 1024 * 1024


def wave_tables():
    position = np.arange(NE)[:, None]
    frequency = np.arange(KF)[None, :] - KF // 2
    phase = np.mod(position * frequency, NE).astype(np.float64) * (2.0 * math.pi / NE)
    return np.cos(phase).astype(np.float32), np.sin(phase).astype(np.float32)


def transform_tables():
    cos, sin = wave_tables()
    full = np.concatenate([cos, sin], 1)
    mid = full[HALO : HALO + N]
    ct, st = cos[HALO : HALO + N].T, sin[HALO : HALO + N].T
    columns = np.concatenate(
        [
            np.stack([ct.reshape(KF, BLOCKS, LANES), st.reshape(KF, BLOCKS, LANES)], 2),
            np.stack([-st.reshape(KF, BLOCKS, LANES), ct.reshape(KF, BLOCKS, LANES)], 2),
        ],
        0,
    )
    to_columns = columns.transpose(1, 0, 2, 3).reshape(BLOCKS, PAIR, 2 * LANES)
    from_columns = to_columns.transpose(0, 2, 1)
    low, high = full[:HALO], full[HALO + N :]
    blank = np.zeros((HALO, PAIR), np.float32)
    rims = np.stack(
        [
            np.concatenate([low[::-1], blank], 0),
            np.concatenate([low, blank], 0),
            np.concatenate([high[::-1], blank], 0),
            np.concatenate([high, blank], 0),
        ]
    )
    back = np.concatenate([cos.T, -sin.T], 0)
    back_low, back_high = back[:, :HALO], back[:, HALO + N :]
    blank = np.zeros((PAIR, HALO), np.float32)
    margins = np.stack(
        [
            np.concatenate([back_high[:, ::-1], blank], 1),
            np.concatenate([back_high, blank], 1),
            np.concatenate([blank, back_low[:, ::-1]], 1),
            np.concatenate([blank, back_low], 1),
        ]
    )
    tables = (mid, mid.T, to_columns, from_columns, rims, back[:, HALO : HALO + N], margins)
    return tuple(np.ascontiguousarray(one).astype(ml_dtypes.bfloat16) for one in tables)


def dot(a, b):
    return jnp.dot(a, b, preferred_element_type=F32)


def in_left_half(shape):
    return lax.broadcasted_iota(jnp.int32, shape, 1) < KF


def swap_halves(pair):
    return pltpu.roll(pair, KF, 1)


def destination(k, step, count):
    return k ^ step if count == 4 else (k - step) % count


def call(
    body, name, outs, args, specs, out_specs=None, scratch=(), flops=0, moved=0
):
    vmem = pl.BlockSpec(memory_space=pltpu.VMEM)
    if out_specs is None:
        out_specs = tuple(vmem for _ in outs) if isinstance(outs, tuple) else vmem
    return pl.pallas_call(
        body,
        name=name,
        out_shape=outs,
        in_specs=specs,
        out_specs=out_specs,
        scratch_shapes=list(scratch),
        compiler_params=pltpu.CompilerParams(vmem_limit_bytes=VMEM_LIMIT),
        cost_estimate=pl.CostEstimate(flops=flops, bytes_accessed=moved, transcendentals=0),
    )(*args)


def edges_body(
    mask, mid, mid_t, real, imag, weight, flags, mate, other, side, held, tall, table, sides_out, pair, marks, sems
):
    odd = lax.rem(lax.axis_index("tile"), 2) == 1
    copies = [
        pltpu.make_async_copy(mid_t, table, sems.at[0]),
        pltpu.make_async_copy(mask.at[:, :LANES], held.at[:, :LANES], sems.at[1]),
        pltpu.make_async_copy(mask.at[:, N - LANES :], held.at[:, N - LANES :], sems.at[2]),
        pltpu.make_async_copy(real.at[0], pair.at[0], sems.at[3]),
        pltpu.make_async_copy(imag.at[0], pair.at[1], sems.at[4]),
        pltpu.make_async_copy(flags, marks, sems.at[5]),
    ]
    inner = pltpu.make_async_copy(
        mask.at[:, LANES : N - LANES], held.at[:, LANES : N - LANES], sems.at[6]
    )
    columns = pltpu.make_async_copy(mid, tall, sems.at[7])
    for copy in copies:
        copy.start()
    inner.start()
    columns.start()
    for copy in copies[3:]:
        copy.wait()
    scale = jnp.sqrt(jnp.full((KF, KF), 2.0 * weight[0], F32)) * (1.0 / (NE * KF))
    kernel = jnp.concatenate([pair[0] * scale, pair[1] * scale], 1).astype(BF16)
    row = lax.broadcasted_iota(jnp.int32, (16, LANES), 0)
    sides = jnp.where(row == 0, marks[0, 0].astype(F32), marks[0, 1].astype(F32)).astype(BF16)
    side[...] = kernel
    mate[EDGE : 2 * EDGE, :] = kernel
    mate[2 * EDGE :, :] = sides
    other[EDGE:, :] = sides
    sides_out[...] = sides
    for copy in copies[:3]:
        copy.wait()
    strips = jnp.concatenate([held[:, :LANES], held[:, N - LANES :]], 1)
    both = dot(table[...], strips)
    left = in_left_half((KF, LANES))
    first, last = both[:, :LANES], both[:, LANES:]
    first = jnp.where(left, first[:KF], swap_halves(first[KF:]))
    last = jnp.where(left, swap_halves(last[:KF]), last[KF:])
    mate[:EDGE, :] = jnp.where(odd, first, last).astype(BF16)
    other[:EDGE, :] = jnp.where(odd, last, first).astype(BF16)
    inner.wait()
    columns.wait()


def middle_body(mask, mid, mid_t, marks, rims, out, tables):
    tile, tiles = lax.axis_index("tile"), lax.axis_size("tile")
    own = marks[...].astype(F32)
    low = jnp.where(own[0:1] == 1.0, rims[1].astype(F32), rims[0].astype(F32))
    high = jnp.where(own[1:2] == 1.0, rims[3].astype(F32), rims[2].astype(F32))
    low = jnp.where(tile == 0, 0.0, low).astype(BF16)
    high = jnp.where(tile == tiles - 1, 0.0, high).astype(BF16)
    odd = lax.rem(tile, 2) == 1
    tables[0] = jnp.where(odd, low, high)
    tables[1] = jnp.where(odd, high, low)
    out[...] = dot(mid_t[...], dot(mask[...], mid[...]).astype(BF16))


def split_kernel(pair):
    left = in_left_half(pair.shape)
    other = swap_halves(pair)
    return jnp.where(left, pair, other), jnp.where(left, other, pair)


def fields_body(count, row_count, *refs):
    (middle, target, mid, to_columns, from_columns, tables, own) = refs[:7]
    near_pack, *others, far_edge = refs[7 : 7 + count]
    out, a_ref, field_a, field_b, bent_a, bent_b, u_ref = refs[7 + count :]
    fields, bent = (field_a, field_b), (bent_a, bent_b)
    left = in_left_half((KF, PAIR))
    blocks = middle[...]
    for pack, table in ((near_pack, tables[0]), (far_edge, tables[1])):
        edge = pack[:EDGE, :].astype(F32)
        edge = jnp.concatenate([edge, swap_halves(edge)], 0).astype(BF16)
        blocks = blocks + dot(edge, table)
    top, bottom = blocks[:KF], swap_halves(blocks[KF:])
    spectrum = jnp.where(left, top - bottom, -(top + bottom))
    turned = swap_halves(spectrum)
    turned = jnp.where(left, -turned, turned)
    kernels = [own[...].astype(F32)]
    kernels.append(near_pack[EDGE : 2 * EDGE, :].astype(F32))
    kernels += [one[...].astype(F32) for one in others]
    kernels = [split_kernel(one) for one in kernels]
    begin = pl.multiple_of(lax.axis_index("kern") * row_count, row_count)
    rows = mid[pl.ds(begin, row_count), :]
    stacks = []
    for real, imag in kernels:
        product = real * spectrum + imag * turned
        other = swap_halves(product)
        other = jnp.where(left, -other, other)
        stacks.append(jnp.concatenate([product, other], 0).astype(BF16))
    waves = dot(rows, jnp.concatenate(stacks, 1)).astype(BF16)
    for index in range(count):
        a_ref[index * row_count : (index + 1) * row_count, :] = waves[:, index * PAIR : (index + 1) * PAIR]
    step = 32 if row_count % 32 == 0 else 16
    halves = (slice(0, LANES), slice(LANES, 2 * LANES))
    fields[0][...] = dot(a_ref[...], to_columns[0])
    for block in range(BLOCKS + 1):
        now = block % 2
        if block + 1 < BLOCKS:
            fields[1 - now][...] = dot(a_ref[...], to_columns[block + 1])
        if block > 0:
            part = dot(bent[1 - now][...], from_columns[block - 1])
            u_ref[...] = part if block == 1 else u_ref[...] + part
        if block == BLOCKS:
            continue
        for r in range(0, row_count, step):
            total = None
            for index in range(count):
                at = index * row_count + r
                real, imag = (fields[now][at : at + step, half] for half in halves)
                term = real * real + imag * imag
                total = term if total is None else total + term
            wanted = target[r : r + step, block * LANES : (block + 1) * LANES].astype(F32)
            decay = jnp.exp(4.0 - 2.0 * total)
            resist = pl.reciprocal(1.0 + decay, approx=True)
            slope = (resist - wanted) * (8.0 * decay) * (resist * resist)
            for index in range(count):
                at = index * row_count + r
                for half in halves:
                    field = fields[now][at : at + step, half] * slope
                    bent[now][at : at + step, half] = field.astype(BF16)
    wide = jnp.concatenate(
        [u_ref[i * row_count : (i + 1) * row_count, :].astype(BF16) for i in range(count)], 1
    )
    waves = lax.dot_general(rows, wide, (((0,), (0,)), ((), ())), preferred_element_type=F32)
    total = None
    for index, (real, imag) in enumerate(kernels):
        wave = waves[:, index * PAIR : (index + 1) * PAIR]
        top, bottom = wave[:KF], swap_halves(wave[KF:])
        wave = jnp.where(left, top + bottom, top - bottom)
        other = swap_halves(wave)
        other = jnp.where(left, other, -other)
        term = real * wave + imag * other
        total = term if total is None else total + term
    out[...] = total.astype(BF16)


def sum_body(count, *refs):
    total = refs[0][...].astype(F32)
    for one in refs[1:count]:
        total = total + one[...].astype(F32)
    refs[count][...] = total.astype(BF16)


def row_waves(rows, pair):
    pair = pair.astype(F32)
    other = swap_halves(pair)
    other = jnp.where(in_left_half(pair.shape), -other, other)
    return dot(rows, jnp.concatenate([pair, other], 0).astype(BF16)).astype(BF16)


def own_rows(mid, row_count):
    begin = pl.multiple_of(lax.axis_index("kern") * row_count, row_count)
    return mid[pl.ds(begin, row_count), :]


def inner_body(row_count, own, mid, back, out):
    out[...] = dot(row_waves(own_rows(mid, row_count), own[...]), back[...])


def outer_body(
    row_count, near, far, near_pack, far_edge, mid, margins, begun, out, held, sems
):
    inner = pltpu.make_async_copy(
        begun.at[:, LANES : N - LANES], out.at[:, LANES : N - LANES], sems.at[2]
    )
    inner.start()
    rows = own_rows(mid, row_count)
    near_wave, far_wave = row_waves(rows, near[...]), row_waves(rows, far[...])
    odd = lax.rem(lax.axis_index("tile"), 2) == 1
    below, above = jnp.where(odd, near_wave, far_wave), jnp.where(odd, far_wave, near_wave)
    near_marks = near_pack[2 * EDGE :, :].astype(F32)
    far_marks = far_edge[EDGE:, :].astype(F32)
    low_mark = jnp.where(odd, near_marks, far_marks)[1:2]
    high_mark = jnp.where(odd, far_marks, near_marks)[0:1]
    low = jnp.where(low_mark == 1.0, margins[1].astype(F32), margins[0].astype(F32)).astype(BF16)
    high = jnp.where(high_mark == 1.0, margins[3].astype(F32), margins[2].astype(F32)).astype(BF16)
    copies = []
    for side, first, wave, table in ((0, 0, below, low), (1, N - LANES, above, high)):
        columns = slice(first, first + LANES)
        held[side] = begun[:, columns] + dot(wave, table)
        copies.append(pltpu.make_async_copy(held.at[side], out.at[:, columns], sems.at[side]))
        copies[-1].start()
    for copy in (inner, *copies):
        copy.wait()


def far_off(array):
    return pltpu.with_memory_space_constraint(array, pltpu.HBM)


def per_device(mask_pixels, orientation, target_pattern, kernel_real, kernel_imag, eigen_weights):
    tables = tuple(jnp.asarray(one) for one in transform_tables())
    mid, mid_t, to_columns, from_columns, rims, back, margins = tables
    tiles, count = lax.axis_size("tile"), lax.axis_size("kern")
    row_count = target_pattern.shape[0]
    vmem = pl.BlockSpec(memory_space=pltpu.VMEM)
    smem = pl.BlockSpec(memory_space=pltpu.SMEM)
    hbm = pl.BlockSpec(memory_space=pltpu.HBM)
    small = jax.ShapeDtypeStruct((KF, PAIR), BF16)

    mate, other, side, held, mid, mid_t, marks = call(
        edges_body,
        "edges",
        (
            pltpu.VMEM((2 * EDGE + MARKS, LANES), BF16),
            pltpu.VMEM((EDGE + MARKS, LANES), BF16),
            pltpu.VMEM((KF, PAIR), BF16),
            pltpu.VMEM((N, N), BF16),
            pltpu.VMEM((N, PAIR), BF16),
            pltpu.VMEM((PAIR, N), BF16),
            pltpu.VMEM((MARKS, LANES), BF16),
        ),
        (
            *(far_off(one) for one in (mask_pixels, mid, mid_t, kernel_real, kernel_imag)),
            eigen_weights,
            far_off(orientation),
        ),
        [hbm] * 5 + [smem, hbm],
        scratch=[
            pltpu.VMEM((2, KF, KF), F32),
            pltpu.SMEM((1, 2), jnp.int32),
            pltpu.SemaphoreType.DMA((8,)),
        ],
        flops=2 * N * LANES * PAIR * 2,
        moved=N * LANES * 4,
    )

    def swapped(move_tile, step):
        pairs = []
        for t in range(tiles):
            for k in range(count):
                pairs.append((t * count + k, move_tile(t) * count + destination(k, step, count)))
        return pairs

    def chip_mate(t):
        return t ^ 1

    def other_side(t):
        return (t + 1 if t % 2 else t - 1) % tiles

    both = ("tile", "kern")
    far_edge = lax.ppermute(other, both, swapped(other_side, 0))
    near_pack = lax.ppermute(mate, both, swapped(chip_mate, 1))
    if count == 4:
        pairs = []
        for t in range(tiles):
            pairs += [(t * count + k, t * count + destination(k, 2 + t % 2, count)) for k in range(count)]
        kernels = [lax.ppermute(side, both, pairs)]
        kernels.append(lax.ppermute(kernels[0], both, swapped(chip_mate, 0)))
    else:
        kernels = [lax.ppermute(side, both, swapped(lambda t: t, step)) for step in range(2, count)]

    middle, edge_tables = call(
        middle_body,
        "middle",
        (pltpu.VMEM((PAIR, PAIR), F32), pltpu.VMEM((2, PAIR, PAIR), BF16)),
        (held, mid, mid_t, marks, rims),
        [vmem] * 5,
        flops=4 * N * N * PAIR,
        moved=N * N * 2,
    )

    part = call(
        functools.partial(fields_body, count, row_count),
        "fields",
        small,
        (middle, target_pattern, mid, to_columns, from_columns, edge_tables, side, near_pack, *kernels, far_edge),
        [vmem] * (7 + count),
        scratch=[
            pltpu.VMEM((count * row_count, PAIR), BF16),
            pltpu.VMEM((count * row_count, 2 * LANES), F32),
            pltpu.VMEM((count * row_count, 2 * LANES), F32),
            pltpu.VMEM((count * row_count, 2 * LANES), BF16),
            pltpu.VMEM((count * row_count, 2 * LANES), BF16),
            pltpu.VMEM((count * row_count, PAIR), F32),
        ],
        flops=8 * count * row_count * N * PAIR,
        moved=4 * row_count * N,
    )

    parts = [part]
    for step in range(1, count):
        pairs = [(k, destination(k, step, count)) for k in range(count)]
        parts.append(lax.ppermute(part, "kern", pairs))
    own = call(functools.partial(sum_body, count), "total", small, tuple(parts), [vmem] * count)
    near = lax.ppermute(own, "tile", [(t, chip_mate(t)) for t in range(tiles)])
    inner = [t for t in range(tiles) if 0 < t < tiles - 1]
    far = lax.ppermute(own, "tile", [(t, other_side(t)) for t in inner])
    begun = call(
        functools.partial(inner_body, row_count),
        "inner",
        pltpu.VMEM((row_count, N), F32),
        (own, mid, back),
        [vmem] * 3,
        flops=2 * row_count * PAIR * N,
        moved=4 * row_count * N,
    )
    return call(
        functools.partial(outer_body, row_count),
        "outer",
        jax.ShapeDtypeStruct((row_count, N), F32),
        (near, far, near_pack, far_edge, mid, margins, begun),
        [vmem] * 7,
        hbm,
        scratch=[
            pltpu.VMEM((2, row_count, LANES), F32),
            pltpu.SemaphoreType.DMA((3,)),
        ],
        flops=2 * row_count * PAIR * 6 * PAIR,
        moved=4 * row_count * 2 * LANES,
    )


def solution(mesh):
    in_specs = (
        P(None, "tile"),
        P("tile", None),
        P("kern", "tile"),
        P("kern", None, None),
        P("kern", None, None),
        P("kern"),
    )
    out_specs = P("kern", "tile")
    return jax.shard_map(
        per_device, mesh=mesh, in_specs=in_specs, out_specs=out_specs, check_vma=False
    )
```

```python
import functools
import math

import jax
import jax.numpy as jnp
import ml_dtypes
import numpy as np
from jax import lax
from jax.experimental import pallas as pl
from jax.experimental.pallas import tpu as pltpu
from jax.sharding import PartitionSpec as P

N = 1152
HALO = 64
KF = 64
NE = 1280
LANES = 128
PAIR = 2 * KF
BLOCKS = N // LANES
EDGE = KF
MARKS = 16
BF16 = jnp.bfloat16
F32 = jnp.float32
VMEM_LIMIT = 32 * 1024 * 1024


def wave_tables():
    position = np.arange(NE)[:, None]
    frequency = np.arange(KF)[None, :] - KF // 2
    phase = np.mod(position * frequency, NE).astype(np.float64) * (2.0 * math.pi / NE)
    return np.cos(phase).astype(np.float32), np.sin(phase).astype(np.float32)


def transform_tables():
    cos, sin = wave_tables()
    full = np.concatenate([cos, sin], 1)
    mid = full[HALO : HALO + N]
    ct, st = cos[HALO : HALO + N].T, sin[HALO : HALO + N].T
    columns = np.concatenate(
        [
            np.stack([ct.reshape(KF, BLOCKS, LANES), st.reshape(KF, BLOCKS, LANES)], 2),
            np.stack([-st.reshape(KF, BLOCKS, LANES), ct.reshape(KF, BLOCKS, LANES)], 2),
        ],
        0,
    )
    to_columns = columns.transpose(1, 0, 2, 3).reshape(BLOCKS, PAIR, 2 * LANES)
    from_columns = to_columns.transpose(0, 2, 1)
    low, high = full[:HALO], full[HALO + N :]
    blank = np.zeros((HALO, PAIR), np.float32)
    rims = np.stack(
        [
            np.concatenate([low[::-1], blank], 0),
            np.concatenate([low, blank], 0),
            np.concatenate([high[::-1], blank], 0),
            np.concatenate([high, blank], 0),
        ]
    )
    back = np.concatenate([cos.T, -sin.T], 0)
    back_low, back_high = back[:, :HALO], back[:, HALO + N :]
    blank = np.zeros((PAIR, HALO), np.float32)
    margins = np.stack(
        [
            np.concatenate([back_high[:, ::-1], blank], 1),
            np.concatenate([back_high, blank], 1),
            np.concatenate([blank, back_low[:, ::-1]], 1),
            np.concatenate([blank, back_low], 1),
        ]
    )
    tables = (mid, mid.T, to_columns, from_columns, rims, back[:, HALO : HALO + N], margins)
    return tuple(np.ascontiguousarray(one).astype(ml_dtypes.bfloat16) for one in tables)


def dot(a, b):
    return jnp.dot(a, b, preferred_element_type=F32)


def in_left_half(shape):
    return lax.broadcasted_iota(jnp.int32, shape, 1) < KF


def swap_halves(pair):
    return pltpu.roll(pair, KF, 1)


def destination(k, step, count):
    return k ^ step if count == 4 else (k - step) % count


def call(
    body, name, outs, args, specs, out_specs=None, scratch=(), flops=0, moved=0
):
    vmem = pl.BlockSpec(memory_space=pltpu.VMEM)
    if out_specs is None:
        out_specs = tuple(vmem for _ in outs) if isinstance(outs, tuple) else vmem
    return pl.pallas_call(
        body,
        name=name,
        out_shape=outs,
        in_specs=specs,
        out_specs=out_specs,
        scratch_shapes=list(scratch),
        compiler_params=pltpu.CompilerParams(vmem_limit_bytes=VMEM_LIMIT),
        cost_estimate=pl.CostEstimate(flops=flops, bytes_accessed=moved, transcendentals=0),
    )(*args)


def edges_body(
    mask, mid, mid_t, real, imag, weight, flags, mate, other, side, held, tall, table, sides_out, pair, marks, sems
):
    odd = lax.rem(lax.axis_index("tile"), 2) == 1
    copies = [
        pltpu.make_async_copy(mid_t, table, sems.at[0]),
        pltpu.make_async_copy(mask.at[:, :LANES], held.at[:, :LANES], sems.at[1]),
        pltpu.make_async_copy(mask.at[:, N - LANES :], held.at[:, N - LANES :], sems.at[2]),
        pltpu.make_async_copy(real.at[0], pair.at[0], sems.at[3]),
        pltpu.make_async_copy(imag.at[0], pair.at[1], sems.at[4]),
        pltpu.make_async_copy(flags, marks, sems.at[5]),
    ]
    inner = pltpu.make_async_copy(
        mask.at[:, LANES : N - LANES], held.at[:, LANES : N - LANES], sems.at[6]
    )
    columns = pltpu.make_async_copy(mid, tall, sems.at[7])
    for copy in copies:
        copy.start()
    inner.start()
    columns.start()
    for copy in copies[3:]:
        copy.wait()
    scale = jnp.sqrt(jnp.full((KF, KF), 2.0 * weight[0], F32)) * (1.0 / (NE * KF))
    kernel = jnp.concatenate([pair[0] * scale, pair[1] * scale], 1).astype(BF16)
    row = lax.broadcasted_iota(jnp.int32, (16, LANES), 0)
    sides = jnp.where(row == 0, marks[0, 0].astype(F32), marks[0, 1].astype(F32)).astype(BF16)
    side[...] = kernel
    mate[EDGE : 2 * EDGE, :] = kernel
    mate[2 * EDGE :, :] = sides
    other[EDGE:, :] = sides
    sides_out[...] = sides
    for copy in copies[:3]:
        copy.wait()
    strips = jnp.concatenate([held[:, :LANES], held[:, N - LANES :]], 1)
    both = dot(table[...], strips)
    left = in_left_half((KF, LANES))
    first, last = both[:, :LANES], both[:, LANES:]
    first = jnp.where(left, first[:KF], swap_halves(first[KF:]))
    last = jnp.where(left, swap_halves(last[:KF]), last[KF:])
    mate[:EDGE, :] = jnp.where(odd, first, last).astype(BF16)
    other[:EDGE, :] = jnp.where(odd, last, first).astype(BF16)
    inner.wait()
    columns.wait()


def middle_body(row_count, mask, mid, mid_t, marks, rims, out, tables, rows_t):
    rows_t[...] = own_rows(mid, row_count).astype(F32).T.astype(BF16)
    tile, tiles = lax.axis_index("tile"), lax.axis_size("tile")
    own = marks[...].astype(F32)
    low = jnp.where(own[0:1] == 1.0, rims[1].astype(F32), rims[0].astype(F32))
    high = jnp.where(own[1:2] == 1.0, rims[3].astype(F32), rims[2].astype(F32))
    low = jnp.where(tile == 0, 0.0, low).astype(BF16)
    high = jnp.where(tile == tiles - 1, 0.0, high).astype(BF16)
    odd = lax.rem(tile, 2) == 1
    tables[0] = jnp.where(odd, low, high)
    tables[1] = jnp.where(odd, high, low)
    out[...] = dot(mid_t[...], dot(mask[...], mid[...]).astype(BF16))


def relay_body(value, ready, out):
    out[...] = value[...]


def split_kernel(pair):
    left = in_left_half(pair.shape)
    other = swap_halves(pair)
    return jnp.where(left, pair, other), jnp.where(left, other, pair)


def fields_body(count, row_count, *refs):
    (middle, target, mid, rows_t, to_columns, from_columns, tables, own) = refs[:8]
    near_pack, *others, far_edge = refs[8 : 8 + count]
    out, a_ref, field_a, field_b, bent_a, bent_b, u_ref = refs[8 + count :]
    fields, bent = (field_a, field_b), (bent_a, bent_b)
    left = in_left_half((KF, PAIR))
    blocks = middle[...]
    for pack, table in ((near_pack, tables[0]), (far_edge, tables[1])):
        edge = pack[:EDGE, :].astype(F32)
        edge = jnp.concatenate([edge, swap_halves(edge)], 0).astype(BF16)
        blocks = blocks + dot(edge, table)
    top, bottom = blocks[:KF], swap_halves(blocks[KF:])
    spectrum = jnp.where(left, top - bottom, -(top + bottom))
    turned = swap_halves(spectrum)
    turned = jnp.where(left, -turned, turned)
    kernels = [own[...].astype(F32)]
    kernels.append(near_pack[EDGE : 2 * EDGE, :].astype(F32))
    kernels += [one[...].astype(F32) for one in others]
    kernels = [split_kernel(one) for one in kernels]
    begin = pl.multiple_of(lax.axis_index("kern") * row_count, row_count)
    rows = mid[pl.ds(begin, row_count), :]
    stacks = []
    for real, imag in kernels:
        product = real * spectrum + imag * turned
        other = swap_halves(product)
        other = jnp.where(left, -other, other)
        stacks.append(jnp.concatenate([product, other], 0).astype(BF16))
    waves = dot(rows, jnp.concatenate(stacks, 1)).astype(BF16)
    for index in range(count):
        a_ref[index * row_count : (index + 1) * row_count, :] = waves[:, index * PAIR : (index + 1) * PAIR]
    step = 32 if row_count % 32 == 0 else 16
    halves = (slice(0, LANES), slice(LANES, 2 * LANES))
    fields[0][...] = dot(a_ref[...], to_columns[0])
    for block in range(BLOCKS + 1):
        now = block % 2
        if block + 1 < BLOCKS:
            fields[1 - now][...] = dot(a_ref[...], to_columns[block + 1])
        if block > 0:
            part = dot(bent[1 - now][...], from_columns[block - 1])
            u_ref[...] = part if block == 1 else u_ref[...] + part
        if block == BLOCKS:
            continue
        for r in range(0, row_count, step):
            total = None
            for index in range(count):
                at = index * row_count + r
                real, imag = (fields[now][at : at + step, half] for half in halves)
                term = real * real + imag * imag
                total = term if total is None else total + term
            wanted = target[r : r + step, block * LANES : (block + 1) * LANES].astype(F32)
            decay = jnp.exp(4.0 - 2.0 * total)
            resist = pl.reciprocal(1.0 + decay, approx=True)
            slope = (resist - wanted) * (8.0 * decay) * (resist * resist)
            for index in range(count):
                at = index * row_count + r
                for half in halves:
                    field = fields[now][at : at + step, half] * slope
                    bent[now][at : at + step, half] = field.astype(BF16)
    wide = jnp.concatenate(
        [u_ref[i * row_count : (i + 1) * row_count, :].astype(BF16) for i in range(count)], 1
    )
    waves = dot(rows_t[...], wide)
    total = None
    for index, (real, imag) in enumerate(kernels):
        wave = waves[:, index * PAIR : (index + 1) * PAIR]
        top, bottom = wave[:KF], swap_halves(wave[KF:])
        wave = jnp.where(left, top + bottom, top - bottom)
        other = swap_halves(wave)
        other = jnp.where(left, other, -other)
        term = real * wave + imag * other
        total = term if total is None else total + term
    out[...] = total.astype(BF16)


def sum_body(count, *refs):
    total = refs[0][...].astype(F32)
    for one in refs[1:count]:
        total = total + one[...].astype(F32)
    refs[count][...] = total.astype(BF16)


def row_waves(rows, pair):
    pair = pair.astype(F32)
    other = swap_halves(pair)
    other = jnp.where(in_left_half(pair.shape), -other, other)
    return dot(rows, jnp.concatenate([pair, other], 0).astype(BF16)).astype(BF16)


def own_rows(mid, row_count):
    begin = pl.multiple_of(lax.axis_index("kern") * row_count, row_count)
    return mid[pl.ds(begin, row_count), :]


def inner_body(row_count, own, mid, back, out):
    out[...] = dot(row_waves(own_rows(mid, row_count), own[...]), back[...])


def outer_body(
    row_count, near, far, near_pack, far_edge, mid, margins, begun, out, held, sems
):
    inner = pltpu.make_async_copy(
        begun.at[:, LANES : N - LANES], out.at[:, LANES : N - LANES], sems.at[2]
    )
    inner.start()
    rows = own_rows(mid, row_count)
    near_wave, far_wave = row_waves(rows, near[...]), row_waves(rows, far[...])
    odd = lax.rem(lax.axis_index("tile"), 2) == 1
    below, above = jnp.where(odd, near_wave, far_wave), jnp.where(odd, far_wave, near_wave)
    near_marks = near_pack[2 * EDGE :, :].astype(F32)
    far_marks = far_edge[EDGE:, :].astype(F32)
    low_mark = jnp.where(odd, near_marks, far_marks)[1:2]
    high_mark = jnp.where(odd, far_marks, near_marks)[0:1]
    low = jnp.where(low_mark == 1.0, margins[1].astype(F32), margins[0].astype(F32)).astype(BF16)
    high = jnp.where(high_mark == 1.0, margins[3].astype(F32), margins[2].astype(F32)).astype(BF16)
    copies = []
    for side, first, wave, table in ((0, 0, below, low), (1, N - LANES, above, high)):
        columns = slice(first, first + LANES)
        held[side] = begun[:, columns] + dot(wave, table)
        copies.append(pltpu.make_async_copy(held.at[side], out.at[:, columns], sems.at[side]))
        copies[-1].start()
    for copy in (inner, *copies):
        copy.wait()


def far_off(array):
    return pltpu.with_memory_space_constraint(array, pltpu.HBM)


def per_device(mask_pixels, orientation, target_pattern, kernel_real, kernel_imag, eigen_weights):
    tables = tuple(jnp.asarray(one) for one in transform_tables())
    mid, mid_t, to_columns, from_columns, rims, back, margins = tables
    tiles, count = lax.axis_size("tile"), lax.axis_size("kern")
    row_count = target_pattern.shape[0]
    vmem = pl.BlockSpec(memory_space=pltpu.VMEM)
    smem = pl.BlockSpec(memory_space=pltpu.SMEM)
    hbm = pl.BlockSpec(memory_space=pltpu.HBM)
    small = jax.ShapeDtypeStruct((KF, PAIR), BF16)

    mate, other, side, held, mid, mid_t, marks = call(
        edges_body,
        "edges",
        (
            pltpu.VMEM((2 * EDGE + MARKS, LANES), BF16),
            pltpu.VMEM((EDGE + MARKS, LANES), BF16),
            pltpu.VMEM((KF, PAIR), BF16),
            pltpu.VMEM((N, N), BF16),
            pltpu.VMEM((N, PAIR), BF16),
            pltpu.VMEM((PAIR, N), BF16),
            pltpu.VMEM((MARKS, LANES), BF16),
        ),
        (
            *(far_off(one) for one in (mask_pixels, mid, mid_t, kernel_real, kernel_imag)),
            eigen_weights,
            far_off(orientation),
        ),
        [hbm] * 5 + [smem, hbm],
        scratch=[
            pltpu.VMEM((2, KF, KF), F32),
            pltpu.SMEM((1, 2), jnp.int32),
            pltpu.SemaphoreType.DMA((8,)),
        ],
        flops=2 * N * LANES * PAIR * 2,
        moved=N * LANES * 4,
    )

    def swapped(move_tile, step):
        pairs = []
        for t in range(tiles):
            for k in range(count):
                pairs.append((t * count + k, move_tile(t) * count + destination(k, step, count)))
        return pairs

    def chip_mate(t):
        return t ^ 1

    def other_side(t):
        return (t + 1 if t % 2 else t - 1) % tiles

    both = ("tile", "kern")
    far_edge = lax.ppermute(other, both, swapped(other_side, 0))
    near_pack = lax.ppermute(mate, both, swapped(chip_mate, 1))
    if count == 4:
        pairs = []
        for t in range(tiles):
            pairs += [(t * count + k, t * count + destination(k, 2 + t % 2, count)) for k in range(count)]
        kernels = [lax.ppermute(side, both, pairs)]
    else:
        kernels = [lax.ppermute(side, both, swapped(lambda t: t, step)) for step in range(2, count)]

    middle, edge_tables, rows_t = call(
        functools.partial(middle_body, row_count),
        "middle",
        (
            pltpu.VMEM((PAIR, PAIR), F32),
            pltpu.VMEM((2, PAIR, PAIR), BF16),
            pltpu.VMEM((PAIR, row_count), BF16),
        ),
        (held, mid, mid_t, marks, rims),
        [vmem] * 5,
        flops=4 * N * N * PAIR,
        moved=N * N * 2,
    )

    if count == 4:
        relayed = call(relay_body, "relay", small, (kernels[0], middle), [vmem] * 2)
        kernels.append(lax.ppermute(relayed, both, swapped(chip_mate, 0)))

    part = call(
        functools.partial(fields_body, count, row_count),
        "fields",
        small,
        (middle, target_pattern, mid, rows_t, to_columns, from_columns, edge_tables, side, near_pack, *kernels, far_edge),
        [vmem] * (8 + count),
        scratch=[
            pltpu.VMEM((count * row_count, PAIR), BF16),
            pltpu.VMEM((count * row_count, 2 * LANES), F32),
            pltpu.VMEM((count * row_count, 2 * LANES), F32),
            pltpu.VMEM((count * row_count, 2 * LANES), BF16),
            pltpu.VMEM((count * row_count, 2 * LANES), BF16),
            pltpu.VMEM((count * row_count, PAIR), F32),
        ],
        flops=8 * count * row_count * N * PAIR,
        moved=4 * row_count * N,
    )

    parts = [part]
    for step in range(1, count):
        pairs = []
        for t in range(tiles):
            own_step = step if t % 2 else count - step
            pairs += [(t * count + k, t * count + destination(k, own_step, count)) for k in range(count)]
        parts.append(lax.ppermute(part, both, pairs))
    own = call(functools.partial(sum_body, count), "total", small, tuple(parts), [vmem] * count)
    near = lax.ppermute(own, "tile", [(t, chip_mate(t)) for t in range(tiles)])
    inner = [t for t in range(tiles) if 0 < t < tiles - 1]
    far = lax.ppermute(own, "tile", [(t, other_side(t)) for t in inner])
    begun = call(
        functools.partial(inner_body, row_count),
        "inner",
        pltpu.VMEM((row_count, N), F32),
        (own, mid, back),
        [vmem] * 3,
        flops=2 * row_count * PAIR * N,
        moved=4 * row_count * N,
    )
    return call(
        functools.partial(outer_body, row_count),
        "outer",
        jax.ShapeDtypeStruct((row_count, N), F32),
        (near, far, near_pack, far_edge, mid, margins, begun),
        [vmem] * 7,
        hbm,
        scratch=[
            pltpu.VMEM((2, row_count, LANES), F32),
            pltpu.SemaphoreType.DMA((3,)),
        ],
        flops=2 * row_count * PAIR * 6 * PAIR,
        moved=4 * row_count * 2 * LANES,
    )


def solution(mesh):
    in_specs = (
        P(None, "tile"),
        P("tile", None),
        P("kern", "tile"),
        P("kern", None, None),
        P("kern", None, None),
        P("kern"),
    )
    out_specs = P("kern", "tile")
    return jax.shard_map(
        per_device, mesh=mesh, in_specs=in_specs, out_specs=out_specs, check_vma=False
    )
```

```python
import functools
import math

import jax
import jax.numpy as jnp
import ml_dtypes
import numpy as np
from jax import lax
from jax.experimental import pallas as pl
from jax.experimental.pallas import tpu as pltpu
from jax.sharding import PartitionSpec as P

N = 1152
HALO = 64
KF = 64
NE = 1280
LANES = 128
PAIR = 2 * KF
BLOCKS = N // LANES
EDGE = KF
MARKS = 16
BF16 = jnp.bfloat16
F32 = jnp.float32
VMEM_LIMIT = 32 * 1024 * 1024


def wave_tables():
    position = np.arange(NE)[:, None]
    frequency = np.arange(KF)[None, :] - KF // 2
    phase = np.mod(position * frequency, NE).astype(np.float64) * (2.0 * math.pi / NE)
    return np.cos(phase).astype(np.float32), np.sin(phase).astype(np.float32)


def transform_tables():
    cos, sin = wave_tables()
    full = np.concatenate([cos, sin], 1)
    mid = full[HALO : HALO + N]
    ct, st = cos[HALO : HALO + N].T, sin[HALO : HALO + N].T
    columns = np.concatenate(
        [
            np.stack([ct.reshape(KF, BLOCKS, LANES), st.reshape(KF, BLOCKS, LANES)], 2),
            np.stack([-st.reshape(KF, BLOCKS, LANES), ct.reshape(KF, BLOCKS, LANES)], 2),
        ],
        0,
    )
    to_columns = columns.transpose(1, 0, 2, 3).reshape(BLOCKS, PAIR, 2 * LANES)
    from_columns = to_columns.transpose(0, 2, 1)
    low, high = full[:HALO], full[HALO + N :]
    blank = np.zeros((HALO, PAIR), np.float32)
    rims = np.stack(
        [
            np.concatenate([low[::-1], blank], 0),
            np.concatenate([low, blank], 0),
            np.concatenate([high[::-1], blank], 0),
            np.concatenate([high, blank], 0),
        ]
    )
    back = np.concatenate([cos.T, -sin.T], 0)
    back_low, back_high = back[:, :HALO], back[:, HALO + N :]
    blank = np.zeros((PAIR, HALO), np.float32)
    margins = np.stack(
        [
            np.concatenate([back_high[:, ::-1], blank], 1),
            np.concatenate([back_high, blank], 1),
            np.concatenate([blank, back_low[:, ::-1]], 1),
            np.concatenate([blank, back_low], 1),
        ]
    )
    tables = (mid, mid.T, to_columns, from_columns, rims, back[:, HALO : HALO + N], margins)
    return tuple(np.ascontiguousarray(one).astype(ml_dtypes.bfloat16) for one in tables)


def dot(a, b):
    return jnp.dot(a, b, preferred_element_type=F32)


def in_left_half(shape):
    return lax.broadcasted_iota(jnp.int32, shape, 1) < KF


def swap_halves(pair):
    return pltpu.roll(pair, KF, 1)


def sum_step(step, tile, count):
    return (step, (2, 3, 1)[step - 1])[tile % 2] if count == 4 else step


def destination(k, step, count):
    return k ^ step if count == 4 else (k - step) % count


def call(
    body, name, outs, args, specs, out_specs=None, scratch=(), flops=0, moved=0
):
    vmem = pl.BlockSpec(memory_space=pltpu.VMEM)
    if out_specs is None:
        out_specs = tuple(vmem for _ in outs) if isinstance(outs, tuple) else vmem
    return pl.pallas_call(
        body,
        name=name,
        out_shape=outs,
        in_specs=specs,
        out_specs=out_specs,
        scratch_shapes=list(scratch),
        compiler_params=pltpu.CompilerParams(vmem_limit_bytes=VMEM_LIMIT),
        cost_estimate=pl.CostEstimate(flops=flops, bytes_accessed=moved, transcendentals=0),
    )(*args)


def edges_body(
    mask, mid, mid_t, real, imag, weight, flags, mate, other, side, held, tall, table, sides_out, pair, marks, sems
):
    odd = lax.rem(lax.axis_index("tile"), 2) == 1
    copies = [
        pltpu.make_async_copy(mid_t, table, sems.at[0]),
        pltpu.make_async_copy(mask.at[:, :LANES], held.at[:, :LANES], sems.at[1]),
        pltpu.make_async_copy(mask.at[:, N - LANES :], held.at[:, N - LANES :], sems.at[2]),
        pltpu.make_async_copy(real.at[0], pair.at[0], sems.at[3]),
        pltpu.make_async_copy(imag.at[0], pair.at[1], sems.at[4]),
        pltpu.make_async_copy(flags, marks, sems.at[5]),
    ]
    inner = pltpu.make_async_copy(
        mask.at[:, LANES : N - LANES], held.at[:, LANES : N - LANES], sems.at[6]
    )
    columns = pltpu.make_async_copy(mid, tall, sems.at[7])
    for copy in copies:
        copy.start()
    inner.start()
    columns.start()
    for copy in copies[3:]:
        copy.wait()
    scale = jnp.sqrt(jnp.full((KF, KF), 2.0 * weight[0], F32)) * (1.0 / (NE * KF))
    kernel = jnp.concatenate([pair[0] * scale, pair[1] * scale], 1).astype(BF16)
    row = lax.broadcasted_iota(jnp.int32, (16, LANES), 0)
    sides = jnp.where(row == 0, marks[0, 0].astype(F32), marks[0, 1].astype(F32)).astype(BF16)
    side[...] = kernel
    mate[EDGE : 2 * EDGE, :] = kernel
    mate[2 * EDGE :, :] = sides
    other[EDGE:, :] = sides
    sides_out[...] = sides
    for copy in copies[:3]:
        copy.wait()
    strips = jnp.concatenate([held[:, :LANES], held[:, N - LANES :]], 1)
    both = dot(table[...], strips)
    left = in_left_half((KF, LANES))
    first, last = both[:, :LANES], both[:, LANES:]
    first = jnp.where(left, first[:KF], swap_halves(first[KF:]))
    last = jnp.where(left, swap_halves(last[:KF]), last[KF:])
    mate[:EDGE, :] = jnp.where(odd, first, last).astype(BF16)
    other[:EDGE, :] = jnp.where(odd, last, first).astype(BF16)
    inner.wait()
    columns.wait()


def middle_body(row_count, mask, mid, mid_t, marks, rims, out, tables, rows_t):
    rows_t[...] = own_rows(mid, row_count).astype(F32).T.astype(BF16)
    tile, tiles = lax.axis_index("tile"), lax.axis_size("tile")
    own = marks[...].astype(F32)
    low = jnp.where(own[0:1] == 1.0, rims[1].astype(F32), rims[0].astype(F32))
    high = jnp.where(own[1:2] == 1.0, rims[3].astype(F32), rims[2].astype(F32))
    low = jnp.where(tile == 0, 0.0, low).astype(BF16)
    high = jnp.where(tile == tiles - 1, 0.0, high).astype(BF16)
    odd = lax.rem(tile, 2) == 1
    tables[0] = jnp.where(odd, low, high)
    tables[1] = jnp.where(odd, high, low)
    out[...] = dot(mid_t[...], dot(mask[...], mid[...]).astype(BF16))


def relay_body(value, ready, out):
    out[...] = value[...]


def split_kernel(pair):
    left = in_left_half(pair.shape)
    other = swap_halves(pair)
    return jnp.where(left, pair, other), jnp.where(left, other, pair)


def fields_body(count, row_count, *refs):
    (middle, target, mid, rows_t, to_columns, from_columns, tables, own) = refs[:8]
    near_pack, *others, far_edge = refs[8 : 8 + count]
    out, a_ref, field_a, field_b, bent_a, bent_b, u_ref = refs[8 + count :]
    fields, bent = (field_a, field_b), (bent_a, bent_b)
    left = in_left_half((KF, PAIR))
    blocks = middle[...]
    for pack, table in ((near_pack, tables[0]), (far_edge, tables[1])):
        edge = pack[:EDGE, :].astype(F32)
        edge = jnp.concatenate([edge, swap_halves(edge)], 0).astype(BF16)
        blocks = blocks + dot(edge, table)
    top, bottom = blocks[:KF], swap_halves(blocks[KF:])
    spectrum = jnp.where(left, top - bottom, -(top + bottom))
    turned = swap_halves(spectrum)
    turned = jnp.where(left, -turned, turned)
    kernels = [own[...].astype(F32)]
    kernels.append(near_pack[EDGE : 2 * EDGE, :].astype(F32))
    kernels += [one[...].astype(F32) for one in others]
    kernels = [split_kernel(one) for one in kernels]
    begin = pl.multiple_of(lax.axis_index("kern") * row_count, row_count)
    rows = mid[pl.ds(begin, row_count), :]
    stacks = []
    for real, imag in kernels:
        product = real * spectrum + imag * turned
        other = swap_halves(product)
        other = jnp.where(left, -other, other)
        stacks.append(jnp.concatenate([product, other], 0).astype(BF16))
    waves = dot(rows, jnp.concatenate(stacks, 1)).astype(BF16)
    for index in range(count):
        a_ref[index * row_count : (index + 1) * row_count, :] = waves[:, index * PAIR : (index + 1) * PAIR]
    step = 32 if row_count % 32 == 0 else 16
    halves = (slice(0, LANES), slice(LANES, 2 * LANES))
    fields[0][...] = dot(a_ref[...], to_columns[0])
    for block in range(BLOCKS + 1):
        now = block % 2
        if block + 1 < BLOCKS:
            fields[1 - now][...] = dot(a_ref[...], to_columns[block + 1])
        if block > 0:
            part = dot(bent[1 - now][...], from_columns[block - 1])
            u_ref[...] = part if block == 1 else u_ref[...] + part
        if block == BLOCKS:
            continue
        for r in range(0, row_count, step):
            total = None
            for index in range(count):
                at = index * row_count + r
                real, imag = (fields[now][at : at + step, half] for half in halves)
                term = real * real + imag * imag
                total = term if total is None else total + term
            wanted = target[r : r + step, block * LANES : (block + 1) * LANES].astype(F32)
            decay = jnp.exp(4.0 - 2.0 * total)
            resist = pl.reciprocal(1.0 + decay, approx=True)
            slope = (resist - wanted) * (8.0 * decay) * (resist * resist)
            for index in range(count):
                at = index * row_count + r
                for half in halves:
                    field = fields[now][at : at + step, half] * slope
                    bent[now][at : at + step, half] = field.astype(BF16)
    wide = jnp.concatenate(
        [u_ref[i * row_count : (i + 1) * row_count, :].astype(BF16) for i in range(count)], 1
    )
    waves = dot(rows_t[...], wide)
    total = None
    for index, (real, imag) in enumerate(kernels):
        wave = waves[:, index * PAIR : (index + 1) * PAIR]
        top, bottom = wave[:KF], swap_halves(wave[KF:])
        wave = jnp.where(left, top + bottom, top - bottom)
        other = swap_halves(wave)
        other = jnp.where(left, other, -other)
        term = real * wave + imag * other
        total = term if total is None else total + term
    out[...] = total.astype(BF16)


def sum_body(count, *refs):
    total = refs[0][...].astype(F32)
    for one in refs[1:count]:
        total = total + one[...].astype(F32)
    refs[count][...] = total.astype(BF16)


def row_waves(rows, pair):
    pair = pair.astype(F32)
    other = swap_halves(pair)
    other = jnp.where(in_left_half(pair.shape), -other, other)
    return dot(rows, jnp.concatenate([pair, other], 0).astype(BF16)).astype(BF16)


def own_rows(mid, row_count):
    begin = pl.multiple_of(lax.axis_index("kern") * row_count, row_count)
    return mid[pl.ds(begin, row_count), :]


def inner_body(row_count, own, mid, back, out):
    out[...] = dot(row_waves(own_rows(mid, row_count), own[...]), back[...])


def outer_body(
    row_count, near, far, near_pack, far_edge, mid, margins, begun, out, held, sems
):
    inner = pltpu.make_async_copy(
        begun.at[:, LANES : N - LANES], out.at[:, LANES : N - LANES], sems.at[2]
    )
    inner.start()
    rows = own_rows(mid, row_count)
    near_wave, far_wave = row_waves(rows, near[...]), row_waves(rows, far[...])
    odd = lax.rem(lax.axis_index("tile"), 2) == 1
    below, above = jnp.where(odd, near_wave, far_wave), jnp.where(odd, far_wave, near_wave)
    near_marks = near_pack[2 * EDGE :, :].astype(F32)
    far_marks = far_edge[EDGE:, :].astype(F32)
    low_mark = jnp.where(odd, near_marks, far_marks)[1:2]
    high_mark = jnp.where(odd, far_marks, near_marks)[0:1]
    low = jnp.where(low_mark == 1.0, margins[1].astype(F32), margins[0].astype(F32)).astype(BF16)
    high = jnp.where(high_mark == 1.0, margins[3].astype(F32), margins[2].astype(F32)).astype(BF16)
    copies = []
    for side, first, wave, table in ((0, 0, below, low), (1, N - LANES, above, high)):
        columns = slice(first, first + LANES)
        held[side] = begun[:, columns] + dot(wave, table)
        copies.append(pltpu.make_async_copy(held.at[side], out.at[:, columns], sems.at[side]))
        copies[-1].start()
    for copy in (inner, *copies):
        copy.wait()


def far_off(array):
    return pltpu.with_memory_space_constraint(array, pltpu.HBM)


def per_device(mask_pixels, orientation, target_pattern, kernel_real, kernel_imag, eigen_weights):
    tables = tuple(jnp.asarray(one) for one in transform_tables())
    mid, mid_t, to_columns, from_columns, rims, back, margins = tables
    tiles, count = lax.axis_size("tile"), lax.axis_size("kern")
    row_count = target_pattern.shape[0]
    vmem = pl.BlockSpec(memory_space=pltpu.VMEM)
    smem = pl.BlockSpec(memory_space=pltpu.SMEM)
    hbm = pl.BlockSpec(memory_space=pltpu.HBM)
    small = jax.ShapeDtypeStruct((KF, PAIR), BF16)

    mate, other, side, held, mid, mid_t, marks = call(
        edges_body,
        "edges",
        (
            pltpu.VMEM((2 * EDGE + MARKS, LANES), BF16),
            pltpu.VMEM((EDGE + MARKS, LANES), BF16),
            pltpu.VMEM((KF, PAIR), BF16),
            pltpu.VMEM((N, N), BF16),
            pltpu.VMEM((N, PAIR), BF16),
            pltpu.VMEM((PAIR, N), BF16),
            pltpu.VMEM((MARKS, LANES), BF16),
        ),
        (
            *(far_off(one) for one in (mask_pixels, mid, mid_t, kernel_real, kernel_imag)),
            eigen_weights,
            far_off(orientation),
        ),
        [hbm] * 5 + [smem, hbm],
        scratch=[
            pltpu.VMEM((2, KF, KF), F32),
            pltpu.SMEM((1, 2), jnp.int32),
            pltpu.SemaphoreType.DMA((8,)),
        ],
        flops=2 * N * LANES * PAIR * 2,
        moved=N * LANES * 4,
    )

    def swapped(move_tile, step):
        pairs = []
        for t in range(tiles):
            for k in range(count):
                pairs.append((t * count + k, move_tile(t) * count + destination(k, step, count)))
        return pairs

    def chip_mate(t):
        return t ^ 1

    def other_side(t):
        return (t + 1 if t % 2 else t - 1) % tiles

    both = ("tile", "kern")
    far_edge = lax.ppermute(other, both, swapped(other_side, 0))
    near_pack = lax.ppermute(mate, both, swapped(chip_mate, 1))
    if count == 4:
        pairs = []
        for t in range(tiles):
            pairs += [(t * count + k, t * count + destination(k, 2 + t % 2, count)) for k in range(count)]
        kernels = [lax.ppermute(side, both, pairs)]
    else:
        kernels = [lax.ppermute(side, both, swapped(lambda t: t, step)) for step in range(2, count)]

    middle, edge_tables, rows_t = call(
        functools.partial(middle_body, row_count),
        "middle",
        (
            pltpu.VMEM((PAIR, PAIR), F32),
            pltpu.VMEM((2, PAIR, PAIR), BF16),
            pltpu.VMEM((PAIR, row_count), BF16),
        ),
        (held, mid, mid_t, marks, rims),
        [vmem] * 5,
        flops=4 * N * N * PAIR,
        moved=N * N * 2,
    )

    if count == 4:
        relayed = call(relay_body, "relay", small, (kernels[0], middle), [vmem] * 2)
        kernels.append(lax.ppermute(relayed, both, swapped(chip_mate, 0)))

    part = call(
        functools.partial(fields_body, count, row_count),
        "fields",
        small,
        (middle, target_pattern, mid, rows_t, to_columns, from_columns, edge_tables, side, near_pack, *kernels, far_edge),
        [vmem] * (8 + count),
        scratch=[
            pltpu.VMEM((count * row_count, PAIR), BF16),
            pltpu.VMEM((count * row_count, 2 * LANES), F32),
            pltpu.VMEM((count * row_count, 2 * LANES), F32),
            pltpu.VMEM((count * row_count, 2 * LANES), BF16),
            pltpu.VMEM((count * row_count, 2 * LANES), BF16),
            pltpu.VMEM((count * row_count, PAIR), F32),
        ],
        flops=8 * count * row_count * N * PAIR,
        moved=4 * row_count * N,
    )

    parts = [part]
    for step in range(1, count):
        pairs = []
        for t in range(tiles):
            own_step = sum_step(step, t, count)
            pairs += [(t * count + k, t * count + destination(k, own_step, count)) for k in range(count)]
        parts.append(lax.ppermute(part, both, pairs))
    own = call(functools.partial(sum_body, count), "total", small, tuple(parts), [vmem] * count)
    near = lax.ppermute(own, "tile", [(t, chip_mate(t)) for t in range(tiles)])
    inner = [t for t in range(tiles) if 0 < t < tiles - 1]
    far = lax.ppermute(own, "tile", [(t, other_side(t)) for t in inner])
    begun = call(
        functools.partial(inner_body, row_count),
        "inner",
        pltpu.VMEM((row_count, N), F32),
        (own, mid, back),
        [vmem] * 3,
        flops=2 * row_count * PAIR * N,
        moved=4 * row_count * N,
    )
    return call(
        functools.partial(outer_body, row_count),
        "outer",
        jax.ShapeDtypeStruct((row_count, N), F32),
        (near, far, near_pack, far_edge, mid, margins, begun),
        [vmem] * 7,
        hbm,
        scratch=[
            pltpu.VMEM((2, row_count, LANES), F32),
            pltpu.SemaphoreType.DMA((3,)),
        ],
        flops=2 * row_count * PAIR * 6 * PAIR,
        moved=4 * row_count * 2 * LANES,
    )


def solution(mesh):
    in_specs = (
        P(None, "tile"),
        P("tile", None),
        P("kern", "tile"),
        P("kern", None, None),
        P("kern", None, None),
        P("kern"),
    )
    out_specs = P("kern", "tile")
    return jax.shard_map(
        per_device, mesh=mesh, in_specs=in_specs, out_specs=out_specs, check_vma=False
    )
```

```python
import functools
import math

import jax
import jax.numpy as jnp
import ml_dtypes
import numpy as np
from jax import lax
from jax.experimental import pallas as pl
from jax.experimental.pallas import tpu as pltpu
from jax.sharding import PartitionSpec as P

N = 1152
HALO = 64
KF = 64
NE = 1280
LANES = 128
PAIR = 2 * KF
BLOCKS = N // LANES
EDGE = KF
MARKS = 16
BF16 = jnp.bfloat16
F32 = jnp.float32
VMEM_LIMIT = 32 * 1024 * 1024


def wave_tables():
    position = np.arange(NE)[:, None]
    frequency = np.arange(KF)[None, :] - KF // 2
    phase = np.mod(position * frequency, NE).astype(np.float64) * (2.0 * math.pi / NE)
    return np.cos(phase).astype(np.float32), np.sin(phase).astype(np.float32)


def transform_tables():
    cos, sin = wave_tables()
    full = np.concatenate([cos, sin], 1)
    mid = full[HALO : HALO + N]
    ct, st = cos[HALO : HALO + N].T, sin[HALO : HALO + N].T
    columns = np.concatenate(
        [
            np.stack([ct.reshape(KF, BLOCKS, LANES), st.reshape(KF, BLOCKS, LANES)], 2),
            np.stack([-st.reshape(KF, BLOCKS, LANES), ct.reshape(KF, BLOCKS, LANES)], 2),
        ],
        0,
    )
    to_columns = columns.transpose(1, 0, 2, 3).reshape(BLOCKS, PAIR, 2 * LANES)
    from_columns = to_columns.transpose(0, 2, 1)
    low, high = full[:HALO], full[HALO + N :]
    blank = np.zeros((HALO, PAIR), np.float32)
    rims = np.stack(
        [
            np.concatenate([low[::-1], blank], 0),
            np.concatenate([low, blank], 0),
            np.concatenate([high[::-1], blank], 0),
            np.concatenate([high, blank], 0),
        ]
    )
    back = np.concatenate([cos.T, -sin.T], 0)
    back_low, back_high = back[:, :HALO], back[:, HALO + N :]
    blank = np.zeros((PAIR, HALO), np.float32)
    margins = np.stack(
        [
            np.concatenate([back_high[:, ::-1], blank], 1),
            np.concatenate([back_high, blank], 1),
            np.concatenate([blank, back_low[:, ::-1]], 1),
            np.concatenate([blank, back_low], 1),
        ]
    )
    tables = (mid, mid.T, to_columns, from_columns, rims, back[:, HALO : HALO + N], margins)
    return tuple(np.ascontiguousarray(one).astype(ml_dtypes.bfloat16) for one in tables)


def dot(a, b):
    return jnp.dot(a, b, preferred_element_type=F32)


def in_left_half(shape):
    return lax.broadcasted_iota(jnp.int32, shape, 1) < KF


def swap_halves(pair):
    return pltpu.roll(pair, KF, 1)


def sum_step(step, tile, count):
    return ((2, 3, 1)[step - 1], step)[tile % 2] if count == 4 else step


def destination(k, step, count):
    return k ^ step if count == 4 else (k - step) % count


def call(
    body, name, outs, args, specs, out_specs=None, scratch=(), flops=0, moved=0
):
    vmem = pl.BlockSpec(memory_space=pltpu.VMEM)
    if out_specs is None:
        out_specs = tuple(vmem for _ in outs) if isinstance(outs, tuple) else vmem
    return pl.pallas_call(
        body,
        name=name,
        out_shape=outs,
        in_specs=specs,
        out_specs=out_specs,
        scratch_shapes=list(scratch),
        compiler_params=pltpu.CompilerParams(vmem_limit_bytes=VMEM_LIMIT),
        cost_estimate=pl.CostEstimate(flops=flops, bytes_accessed=moved, transcendentals=0),
    )(*args)


def edges_body(
    mask, mid, mid_t, real, imag, weight, flags, mate, other, side, held, tall, table, sides_out, pair, marks, sems
):
    odd = lax.rem(lax.axis_index("tile"), 2) == 1
    copies = [
        pltpu.make_async_copy(mid_t, table, sems.at[0]),
        pltpu.make_async_copy(mask.at[:, :LANES], held.at[:, :LANES], sems.at[1]),
        pltpu.make_async_copy(mask.at[:, N - LANES :], held.at[:, N - LANES :], sems.at[2]),
        pltpu.make_async_copy(real.at[0], pair.at[0], sems.at[3]),
        pltpu.make_async_copy(imag.at[0], pair.at[1], sems.at[4]),
        pltpu.make_async_copy(flags, marks, sems.at[5]),
    ]
    inner = pltpu.make_async_copy(
        mask.at[:, LANES : N - LANES], held.at[:, LANES : N - LANES], sems.at[6]
    )
    columns = pltpu.make_async_copy(mid, tall, sems.at[7])
    for copy in copies:
        copy.start()
    inner.start()
    columns.start()
    for copy in copies[3:]:
        copy.wait()
    scale = jnp.sqrt(jnp.full((KF, KF), 2.0 * weight[0], F32)) * (1.0 / (NE * KF))
    kernel = jnp.concatenate([pair[0] * scale, pair[1] * scale], 1).astype(BF16)
    row = lax.broadcasted_iota(jnp.int32, (16, LANES), 0)
    sides = jnp.where(row == 0, marks[0, 0].astype(F32), marks[0, 1].astype(F32)).astype(BF16)
    side[...] = kernel
    mate[EDGE : 2 * EDGE, :] = kernel
    mate[2 * EDGE :, :] = sides
    other[EDGE:, :] = sides
    sides_out[...] = sides
    for copy in copies[:3]:
        copy.wait()
    strips = jnp.concatenate([held[:, :LANES], held[:, N - LANES :]], 1)
    both = dot(table[...], strips)
    left = in_left_half((KF, LANES))
    first, last = both[:, :LANES], both[:, LANES:]
    first = jnp.where(left, first[:KF], swap_halves(first[KF:]))
    last = jnp.where(left, swap_halves(last[:KF]), last[KF:])
    mate[:EDGE, :] = jnp.where(odd, first, last).astype(BF16)
    other[:EDGE, :] = jnp.where(odd, last, first).astype(BF16)
    inner.wait()
    columns.wait()


def middle_body(row_count, mask, mid, mid_t, marks, rims, out, tables, rows_t):
    rows_t[...] = own_rows(mid, row_count).astype(F32).T.astype(BF16)
    tile, tiles = lax.axis_index("tile"), lax.axis_size("tile")
    own = marks[...].astype(F32)
    low = jnp.where(own[0:1] == 1.0, rims[1].astype(F32), rims[0].astype(F32))
    high = jnp.where(own[1:2] == 1.0, rims[3].astype(F32), rims[2].astype(F32))
    low = jnp.where(tile == 0, 0.0, low).astype(BF16)
    high = jnp.where(tile == tiles - 1, 0.0, high).astype(BF16)
    odd = lax.rem(tile, 2) == 1
    tables[0] = jnp.where(odd, low, high)
    tables[1] = jnp.where(odd, high, low)
    out[...] = dot(mid_t[...], dot(mask[...], mid[...]).astype(BF16))


def relay_body(value, ready, out):
    out[...] = value[...]


def split_kernel(pair):
    left = in_left_half(pair.shape)
    other = swap_halves(pair)
    return jnp.where(left, pair, other), jnp.where(left, other, pair)


def fields_body(count, row_count, *refs):
    (middle, target, mid, rows_t, to_columns, from_columns, tables, own) = refs[:8]
    near_pack, *others, far_edge = refs[8 : 8 + count]
    out, a_ref, field_a, field_b, bent_a, bent_b, u_ref = refs[8 + count :]
    fields, bent = (field_a, field_b), (bent_a, bent_b)
    left = in_left_half((KF, PAIR))
    blocks = middle[...]
    for pack, table in ((near_pack, tables[0]), (far_edge, tables[1])):
        edge = pack[:EDGE, :].astype(F32)
        edge = jnp.concatenate([edge, swap_halves(edge)], 0).astype(BF16)
        blocks = blocks + dot(edge, table)
    top, bottom = blocks[:KF], swap_halves(blocks[KF:])
    spectrum = jnp.where(left, top - bottom, -(top + bottom))
    turned = swap_halves(spectrum)
    turned = jnp.where(left, -turned, turned)
    kernels = [own[...].astype(F32)]
    kernels.append(near_pack[EDGE : 2 * EDGE, :].astype(F32))
    kernels += [one[...].astype(F32) for one in others]
    kernels = [split_kernel(one) for one in kernels]
    begin = pl.multiple_of(lax.axis_index("kern") * row_count, row_count)
    rows = mid[pl.ds(begin, row_count), :]
    stacks = []
    for real, imag in kernels:
        product = real * spectrum + imag * turned
        other = swap_halves(product)
        other = jnp.where(left, -other, other)
        stacks.append(jnp.concatenate([product, other], 0).astype(BF16))
    waves = dot(rows, jnp.concatenate(stacks, 1)).astype(BF16)
    for index in range(count):
        a_ref[index * row_count : (index + 1) * row_count, :] = waves[:, index * PAIR : (index + 1) * PAIR]
    step = 32 if row_count % 32 == 0 else 16
    halves = (slice(0, LANES), slice(LANES, 2 * LANES))
    fields[0][...] = dot(a_ref[...], to_columns[0])
    for block in range(BLOCKS + 1):
        now = block % 2
        if block + 1 < BLOCKS:
            fields[1 - now][...] = dot(a_ref[...], to_columns[block + 1])
        if block > 0:
            part = dot(bent[1 - now][...], from_columns[block - 1])
            u_ref[...] = part if block == 1 else u_ref[...] + part
        if block == BLOCKS:
            continue
        for r in range(0, row_count, step):
            total = None
            for index in range(count):
                at = index * row_count + r
                real, imag = (fields[now][at : at + step, half] for half in halves)
                term = real * real + imag * imag
                total = term if total is None else total + term
            wanted = target[r : r + step, block * LANES : (block + 1) * LANES].astype(F32)
            decay = jnp.exp(4.0 - 2.0 * total)
            resist = pl.reciprocal(1.0 + decay, approx=True)
            slope = (resist - wanted) * (8.0 * decay) * (resist * resist)
            for index in range(count):
                at = index * row_count + r
                for half in halves:
                    field = fields[now][at : at + step, half] * slope
                    bent[now][at : at + step, half] = field.astype(BF16)
    wide = jnp.concatenate(
        [u_ref[i * row_count : (i + 1) * row_count, :].astype(BF16) for i in range(count)], 1
    )
    waves = dot(rows_t[...], wide)
    total = None
    for index, (real, imag) in enumerate(kernels):
        wave = waves[:, index * PAIR : (index + 1) * PAIR]
        top, bottom = wave[:KF], swap_halves(wave[KF:])
        wave = jnp.where(left, top + bottom, top - bottom)
        other = swap_halves(wave)
        other = jnp.where(left, other, -other)
        term = real * wave + imag * other
        total = term if total is None else total + term
    out[...] = total.astype(BF16)


def sum_body(count, *refs):
    total = refs[0][...].astype(F32)
    for one in refs[1:count]:
        total = total + one[...].astype(F32)
    refs[count][...] = total.astype(BF16)


def row_waves(rows, pair):
    pair = pair.astype(F32)
    other = swap_halves(pair)
    other = jnp.where(in_left_half(pair.shape), -other, other)
    return dot(rows, jnp.concatenate([pair, other], 0).astype(BF16)).astype(BF16)


def own_rows(mid, row_count):
    begin = pl.multiple_of(lax.axis_index("kern") * row_count, row_count)
    return mid[pl.ds(begin, row_count), :]


def inner_body(row_count, own, mid, back, out):
    out[...] = dot(row_waves(own_rows(mid, row_count), own[...]), back[...])


def outer_body(
    row_count, near, far, near_pack, far_edge, mid, margins, begun, out, held, sems
):
    inner = pltpu.make_async_copy(
        begun.at[:, LANES : N - LANES], out.at[:, LANES : N - LANES], sems.at[2]
    )
    inner.start()
    rows = own_rows(mid, row_count)
    near_wave, far_wave = row_waves(rows, near[...]), row_waves(rows, far[...])
    odd = lax.rem(lax.axis_index("tile"), 2) == 1
    below, above = jnp.where(odd, near_wave, far_wave), jnp.where(odd, far_wave, near_wave)
    near_marks = near_pack[2 * EDGE :, :].astype(F32)
    far_marks = far_edge[EDGE:, :].astype(F32)
    low_mark = jnp.where(odd, near_marks, far_marks)[1:2]
    high_mark = jnp.where(odd, far_marks, near_marks)[0:1]
    low = jnp.where(low_mark == 1.0, margins[1].astype(F32), margins[0].astype(F32)).astype(BF16)
    high = jnp.where(high_mark == 1.0, margins[3].astype(F32), margins[2].astype(F32)).astype(BF16)
    copies = []
    for side, first, wave, table in ((0, 0, below, low), (1, N - LANES, above, high)):
        columns = slice(first, first + LANES)
        held[side] = begun[:, columns] + dot(wave, table)
        copies.append(pltpu.make_async_copy(held.at[side], out.at[:, columns], sems.at[side]))
        copies[-1].start()
    for copy in (inner, *copies):
        copy.wait()


def far_off(array):
    return pltpu.with_memory_space_constraint(array, pltpu.HBM)


def per_device(mask_pixels, orientation, target_pattern, kernel_real, kernel_imag, eigen_weights):
    tables = tuple(jnp.asarray(one) for one in transform_tables())
    mid, mid_t, to_columns, from_columns, rims, back, margins = tables
    tiles, count = lax.axis_size("tile"), lax.axis_size("kern")
    row_count = target_pattern.shape[0]
    vmem = pl.BlockSpec(memory_space=pltpu.VMEM)
    smem = pl.BlockSpec(memory_space=pltpu.SMEM)
    hbm = pl.BlockSpec(memory_space=pltpu.HBM)
    small = jax.ShapeDtypeStruct((KF, PAIR), BF16)

    mate, other, side, held, mid, mid_t, marks = call(
        edges_body,
        "edges",
        (
            pltpu.VMEM((2 * EDGE + MARKS, LANES), BF16),
            pltpu.VMEM((EDGE + MARKS, LANES), BF16),
            pltpu.VMEM((KF, PAIR), BF16),
            pltpu.VMEM((N, N), BF16),
            pltpu.VMEM((N, PAIR), BF16),
            pltpu.VMEM((PAIR, N), BF16),
            pltpu.VMEM((MARKS, LANES), BF16),
        ),
        (
            *(far_off(one) for one in (mask_pixels, mid, mid_t, kernel_real, kernel_imag)),
            eigen_weights,
            far_off(orientation),
        ),
        [hbm] * 5 + [smem, hbm],
        scratch=[
            pltpu.VMEM((2, KF, KF), F32),
            pltpu.SMEM((1, 2), jnp.int32),
            pltpu.SemaphoreType.DMA((8,)),
        ],
        flops=2 * N * LANES * PAIR * 2,
        moved=N * LANES * 4,
    )

    def swapped(move_tile, step):
        pairs = []
        for t in range(tiles):
            for k in range(count):
                pairs.append((t * count + k, move_tile(t) * count + destination(k, step, count)))
        return pairs

    def chip_mate(t):
        return t ^ 1

    def other_side(t):
        return (t + 1 if t % 2 else t - 1) % tiles

    both = ("tile", "kern")
    far_edge = lax.ppermute(other, both, swapped(other_side, 0))
    near_pack = lax.ppermute(mate, both, swapped(chip_mate, 1))
    if count == 4:
        pairs = []
        for t in range(tiles):
            pairs += [(t * count + k, t * count + destination(k, 2 + t % 2, count)) for k in range(count)]
        kernels = [lax.ppermute(side, both, pairs)]
    else:
        kernels = [lax.ppermute(side, both, swapped(lambda t: t, step)) for step in range(2, count)]

    middle, edge_tables, rows_t = call(
        functools.partial(middle_body, row_count),
        "middle",
        (
            pltpu.VMEM((PAIR, PAIR), F32),
            pltpu.VMEM((2, PAIR, PAIR), BF16),
            pltpu.VMEM((PAIR, row_count), BF16),
        ),
        (held, mid, mid_t, marks, rims),
        [vmem] * 5,
        flops=4 * N * N * PAIR,
        moved=N * N * 2,
    )

    if count == 4:
        relayed = call(relay_body, "relay", small, (kernels[0], middle), [vmem] * 2)
        kernels.append(lax.ppermute(relayed, both, swapped(chip_mate, 0)))

    part = call(
        functools.partial(fields_body, count, row_count),
        "fields",
        small,
        (middle, target_pattern, mid, rows_t, to_columns, from_columns, edge_tables, side, near_pack, *kernels, far_edge),
        [vmem] * (8 + count),
        scratch=[
            pltpu.VMEM((count * row_count, PAIR), BF16),
            pltpu.VMEM((count * row_count, 2 * LANES), F32),
            pltpu.VMEM((count * row_count, 2 * LANES), F32),
            pltpu.VMEM((count * row_count, 2 * LANES), BF16),
            pltpu.VMEM((count * row_count, 2 * LANES), BF16),
            pltpu.VMEM((count * row_count, PAIR), F32),
        ],
        flops=8 * count * row_count * N * PAIR,
        moved=4 * row_count * N,
    )

    parts = [part]
    for step in range(1, count):
        pairs = []
        for t in range(tiles):
            own_step = sum_step(step, t, count)
            pairs += [(t * count + k, t * count + destination(k, own_step, count)) for k in range(count)]
        parts.append(lax.ppermute(part, both, pairs))
    own = call(functools.partial(sum_body, count), "total", small, tuple(parts), [vmem] * count)
    near = lax.ppermute(own, "tile", [(t, chip_mate(t)) for t in range(tiles)])
    inner = [t for t in range(tiles) if 0 < t < tiles - 1]
    far = lax.ppermute(own, "tile", [(t, other_side(t)) for t in inner])
    begun = call(
        functools.partial(inner_body, row_count),
        "inner",
        pltpu.VMEM((row_count, N), F32),
        (own, mid, back),
        [vmem] * 3,
        flops=2 * row_count * PAIR * N,
        moved=4 * row_count * N,
    )
    return call(
        functools.partial(outer_body, row_count),
        "outer",
        jax.ShapeDtypeStruct((row_count, N), F32),
        (near, far, near_pack, far_edge, mid, margins, begun),
        [vmem] * 7,
        hbm,
        scratch=[
            pltpu.VMEM((2, row_count, LANES), F32),
            pltpu.SemaphoreType.DMA((3,)),
        ],
        flops=2 * row_count * PAIR * 6 * PAIR,
        moved=4 * row_count * 2 * LANES,
    )


def solution(mesh):
    in_specs = (
        P(None, "tile"),
        P("tile", None),
        P("kern", "tile"),
        P("kern", None, None),
        P("kern", None, None),
        P("kern"),
    )
    out_specs = P("kern", "tile")
    return jax.shard_map(
        per_device, mesh=mesh, in_specs=in_specs, out_specs=out_specs, check_vma=False
    )
```

```python
import functools
import math

import jax
import jax.numpy as jnp
import ml_dtypes
import numpy as np
from jax import lax
from jax.experimental import pallas as pl
from jax.experimental.pallas import tpu as pltpu
from jax.sharding import PartitionSpec as P

N = 1152
HALO = 64
KF = 64
NE = 1280
LANES = 128
PAIR = 2 * KF
BLOCKS = N // LANES
EDGE = KF
MARKS = 16
BF16 = jnp.bfloat16
F32 = jnp.float32
VMEM_LIMIT = 32 * 1024 * 1024


def wave_tables():
    position = np.arange(NE)[:, None]
    frequency = np.arange(KF)[None, :] - KF // 2
    phase = np.mod(position * frequency, NE).astype(np.float64) * (2.0 * math.pi / NE)
    return np.cos(phase).astype(np.float32), np.sin(phase).astype(np.float32)


def transform_tables():
    cos, sin = wave_tables()
    full = np.concatenate([cos, sin], 1)
    mid = full[HALO : HALO + N]
    ct, st = cos[HALO : HALO + N].T, sin[HALO : HALO + N].T
    columns = np.concatenate(
        [
            np.stack([ct.reshape(KF, BLOCKS, LANES), st.reshape(KF, BLOCKS, LANES)], 2),
            np.stack([-st.reshape(KF, BLOCKS, LANES), ct.reshape(KF, BLOCKS, LANES)], 2),
        ],
        0,
    )
    to_columns = columns.transpose(1, 0, 2, 3).reshape(BLOCKS, PAIR, 2 * LANES)
    from_columns = to_columns.transpose(0, 2, 1)
    low, high = full[:HALO], full[HALO + N :]
    blank = np.zeros((HALO, PAIR), np.float32)
    rims = np.stack(
        [
            np.concatenate([low[::-1], blank], 0),
            np.concatenate([low, blank], 0),
            np.concatenate([high[::-1], blank], 0),
            np.concatenate([high, blank], 0),
        ]
    )
    back = np.concatenate([cos.T, -sin.T], 0)
    back_low, back_high = back[:, :HALO], back[:, HALO + N :]
    blank = np.zeros((PAIR, HALO), np.float32)
    margins = np.stack(
        [
            np.concatenate([back_high[:, ::-1], blank], 1),
            np.concatenate([back_high, blank], 1),
            np.concatenate([blank, back_low[:, ::-1]], 1),
            np.concatenate([blank, back_low], 1),
        ]
    )
    tables = (mid, mid.T, to_columns, from_columns, rims, back[:, HALO : HALO + N], margins)
    return tuple(np.ascontiguousarray(one).astype(ml_dtypes.bfloat16) for one in tables)


def dot(a, b):
    return jnp.dot(a, b, preferred_element_type=F32)


def in_left_half(shape):
    return lax.broadcasted_iota(jnp.int32, shape, 1) < KF


def swap_halves(pair):
    return pltpu.roll(pair, KF, 1)


def sum_step(step, tile, count):
    return (step, (2, 3, 1)[step - 1])[tile % 2] if count == 4 else step


def destination(k, step, count):
    return k ^ step if count == 4 else (k - step) % count


def call(
    body, name, outs, args, specs, out_specs=None, scratch=(), flops=0, moved=0
):
    vmem = pl.BlockSpec(memory_space=pltpu.VMEM)
    if out_specs is None:
        out_specs = tuple(vmem for _ in outs) if isinstance(outs, tuple) else vmem
    return pl.pallas_call(
        body,
        name=name,
        out_shape=outs,
        in_specs=specs,
        out_specs=out_specs,
        scratch_shapes=list(scratch),
        compiler_params=pltpu.CompilerParams(vmem_limit_bytes=VMEM_LIMIT),
        cost_estimate=pl.CostEstimate(flops=flops, bytes_accessed=moved, transcendentals=0),
    )(*args)


def pack_body(real, imag, weight, flags, side, sides, pair, marks, sems):
    copies = [
        pltpu.make_async_copy(real.at[0], pair.at[0], sems.at[0]),
        pltpu.make_async_copy(imag.at[0], pair.at[1], sems.at[1]),
        pltpu.make_async_copy(flags, marks, sems.at[2]),
    ]
    for copy in copies:
        copy.start()
    for copy in copies:
        copy.wait()
    scale = jnp.sqrt(jnp.full((KF, KF), 2.0 * weight[0], F32)) * (1.0 / (NE * KF))
    side[...] = jnp.concatenate([pair[0] * scale, pair[1] * scale], 1).astype(BF16)
    row = lax.broadcasted_iota(jnp.int32, (MARKS, LANES), 0)
    sides[...] = jnp.where(row == 0, marks[0, 0].astype(F32), marks[0, 1].astype(F32)).astype(BF16)


def edges_body(mask, mid_t, side, sides, mate, other, table, strips, sems):
    copies = [
        pltpu.make_async_copy(mid_t, table, sems.at[0]),
        pltpu.make_async_copy(mask.at[:, :LANES], strips.at[:, :LANES], sems.at[1]),
        pltpu.make_async_copy(mask.at[:, N - LANES :], strips.at[:, LANES:], sems.at[2]),
    ]
    for copy in copies:
        copy.start()
    odd = lax.rem(lax.axis_index("tile"), 2) == 1
    mate[EDGE : 2 * EDGE, :] = side[...]
    mate[2 * EDGE :, :] = sides[...]
    other[EDGE:, :] = sides[...]
    for copy in copies:
        copy.wait()
    both = dot(table[...], strips[...])
    left = in_left_half((KF, LANES))
    first, last = both[:, :LANES], both[:, LANES:]
    first = jnp.where(left, first[:KF], swap_halves(first[KF:]))
    last = jnp.where(left, swap_halves(last[:KF]), last[KF:])
    mate[:EDGE, :] = jnp.where(odd, first, last).astype(BF16)
    other[:EDGE, :] = jnp.where(odd, last, first).astype(BF16)


def middle_body(row_count, mask, mid, mid_t, marks, rims, out, tables, rows_t):
    rows_t[...] = own_rows(mid, row_count).astype(F32).T.astype(BF16)
    tile, tiles = lax.axis_index("tile"), lax.axis_size("tile")
    own = marks[...].astype(F32)
    low = jnp.where(own[0:1] == 1.0, rims[1].astype(F32), rims[0].astype(F32))
    high = jnp.where(own[1:2] == 1.0, rims[3].astype(F32), rims[2].astype(F32))
    low = jnp.where(tile == 0, 0.0, low).astype(BF16)
    high = jnp.where(tile == tiles - 1, 0.0, high).astype(BF16)
    odd = lax.rem(tile, 2) == 1
    tables[0] = jnp.where(odd, low, high)
    tables[1] = jnp.where(odd, high, low)
    out[...] = dot(mid_t[...], dot(mask[...], mid[...]).astype(BF16))


def relay_body(value, ready, out):
    out[...] = value[...]


def split_kernel(pair):
    left = in_left_half(pair.shape)
    other = swap_halves(pair)
    return jnp.where(left, pair, other), jnp.where(left, other, pair)


def fields_body(count, row_count, *refs):
    (middle, target, mid, rows_t, to_columns, from_columns, tables, own) = refs[:8]
    near_pack, *others, far_edge = refs[8 : 8 + count]
    out, a_ref, field_a, field_b, bent_a, bent_b, u_ref = refs[8 + count :]
    fields, bent = (field_a, field_b), (bent_a, bent_b)
    left = in_left_half((KF, PAIR))
    blocks = middle[...]
    for pack, table in ((near_pack, tables[0]), (far_edge, tables[1])):
        edge = pack[:EDGE, :].astype(F32)
        edge = jnp.concatenate([edge, swap_halves(edge)], 0).astype(BF16)
        blocks = blocks + dot(edge, table)
    top, bottom = blocks[:KF], swap_halves(blocks[KF:])
    spectrum = jnp.where(left, top - bottom, -(top + bottom))
    turned = swap_halves(spectrum)
    turned = jnp.where(left, -turned, turned)
    kernels = [own[...].astype(F32)]
    kernels.append(near_pack[EDGE : 2 * EDGE, :].astype(F32))
    kernels += [one[...].astype(F32) for one in others]
    kernels = [split_kernel(one) for one in kernels]
    begin = pl.multiple_of(lax.axis_index("kern") * row_count, row_count)
    rows = mid[pl.ds(begin, row_count), :]
    stacks = []
    for real, imag in kernels:
        product = real * spectrum + imag * turned
        other = swap_halves(product)
        other = jnp.where(left, -other, other)
        stacks.append(jnp.concatenate([product, other], 0).astype(BF16))
    waves = dot(rows, jnp.concatenate(stacks, 1)).astype(BF16)
    for index in range(count):
        a_ref[index * row_count : (index + 1) * row_count, :] = waves[:, index * PAIR : (index + 1) * PAIR]
    step = 32 if row_count % 32 == 0 else 16
    halves = (slice(0, LANES), slice(LANES, 2 * LANES))
    fields[0][...] = dot(a_ref[...], to_columns[0])
    for block in range(BLOCKS + 1):
        now = block % 2
        if block + 1 < BLOCKS:
            fields[1 - now][...] = dot(a_ref[...], to_columns[block + 1])
        if block > 0:
            part = dot(bent[1 - now][...], from_columns[block - 1])
            u_ref[...] = part if block == 1 else u_ref[...] + part
        if block == BLOCKS:
            continue
        for r in range(0, row_count, step):
            total = None
            for index in range(count):
                at = index * row_count + r
                real, imag = (fields[now][at : at + step, half] for half in halves)
                term = real * real + imag * imag
                total = term if total is None else total + term
            wanted = target[r : r + step, block * LANES : (block + 1) * LANES].astype(F32)
            decay = jnp.exp(4.0 - 2.0 * total)
            resist = pl.reciprocal(1.0 + decay, approx=True)
            slope = (resist - wanted) * (8.0 * decay) * (resist * resist)
            for index in range(count):
                at = index * row_count + r
                for half in halves:
                    field = fields[now][at : at + step, half] * slope
                    bent[now][at : at + step, half] = field.astype(BF16)
    wide = jnp.concatenate(
        [u_ref[i * row_count : (i + 1) * row_count, :].astype(BF16) for i in range(count)], 1
    )
    waves = dot(rows_t[...], wide)
    total = None
    for index, (real, imag) in enumerate(kernels):
        wave = waves[:, index * PAIR : (index + 1) * PAIR]
        top, bottom = wave[:KF], swap_halves(wave[KF:])
        wave = jnp.where(left, top + bottom, top - bottom)
        other = swap_halves(wave)
        other = jnp.where(left, other, -other)
        term = real * wave + imag * other
        total = term if total is None else total + term
    out[...] = total.astype(BF16)


def sum_body(count, *refs):
    total = refs[0][...].astype(F32)
    for one in refs[1:count]:
        total = total + one[...].astype(F32)
    refs[count][...] = total.astype(BF16)


def row_waves(rows, pair):
    pair = pair.astype(F32)
    other = swap_halves(pair)
    other = jnp.where(in_left_half(pair.shape), -other, other)
    return dot(rows, jnp.concatenate([pair, other], 0).astype(BF16)).astype(BF16)


def own_rows(mid, row_count):
    begin = pl.multiple_of(lax.axis_index("kern") * row_count, row_count)
    return mid[pl.ds(begin, row_count), :]


def inner_body(row_count, own, mid, back, out):
    out[...] = dot(row_waves(own_rows(mid, row_count), own[...]), back[...])


def outer_body(
    row_count, near, far, near_pack, far_edge, mid, margins, begun, out, held, sems
):
    inner = pltpu.make_async_copy(
        begun.at[:, LANES : N - LANES], out.at[:, LANES : N - LANES], sems.at[2]
    )
    inner.start()
    rows = own_rows(mid, row_count)
    near_wave, far_wave = row_waves(rows, near[...]), row_waves(rows, far[...])
    odd = lax.rem(lax.axis_index("tile"), 2) == 1
    below, above = jnp.where(odd, near_wave, far_wave), jnp.where(odd, far_wave, near_wave)
    near_marks = near_pack[2 * EDGE :, :].astype(F32)
    far_marks = far_edge[EDGE:, :].astype(F32)
    low_mark = jnp.where(odd, near_marks, far_marks)[1:2]
    high_mark = jnp.where(odd, far_marks, near_marks)[0:1]
    low = jnp.where(low_mark == 1.0, margins[1].astype(F32), margins[0].astype(F32)).astype(BF16)
    high = jnp.where(high_mark == 1.0, margins[3].astype(F32), margins[2].astype(F32)).astype(BF16)
    copies = []
    for side, first, wave, table in ((0, 0, below, low), (1, N - LANES, above, high)):
        columns = slice(first, first + LANES)
        held[side] = begun[:, columns] + dot(wave, table)
        copies.append(pltpu.make_async_copy(held.at[side], out.at[:, columns], sems.at[side]))
        copies[-1].start()
    for copy in (inner, *copies):
        copy.wait()


def far_off(array):
    return pltpu.with_memory_space_constraint(array, pltpu.HBM)


def per_device(mask_pixels, orientation, target_pattern, kernel_real, kernel_imag, eigen_weights):
    tables = tuple(jnp.asarray(one) for one in transform_tables())
    mid, mid_t, to_columns, from_columns, rims, back, margins = tables
    tiles, count = lax.axis_size("tile"), lax.axis_size("kern")
    row_count = target_pattern.shape[0]
    vmem = pl.BlockSpec(memory_space=pltpu.VMEM)
    smem = pl.BlockSpec(memory_space=pltpu.SMEM)
    hbm = pl.BlockSpec(memory_space=pltpu.HBM)
    small = jax.ShapeDtypeStruct((KF, PAIR), BF16)

    side, marks = call(
        pack_body,
        "pack",
        (pltpu.VMEM((KF, PAIR), BF16), pltpu.VMEM((MARKS, LANES), BF16)),
        (far_off(kernel_real), far_off(kernel_imag), eigen_weights, far_off(orientation)),
        [hbm, hbm, smem, hbm],
        scratch=[
            pltpu.VMEM((2, KF, KF), F32),
            pltpu.SMEM((1, 2), jnp.int32),
            pltpu.SemaphoreType.DMA((3,)),
        ],
        flops=8 * KF * KF,
        moved=8 * KF * KF,
    )
    held = pltpu.with_memory_space_constraint(mask_pixels, pltpu.VMEM)
    mate, other, mid_t = call(
        edges_body,
        "edges",
        (
            pltpu.VMEM((2 * EDGE + MARKS, LANES), BF16),
            pltpu.VMEM((EDGE + MARKS, LANES), BF16),
            pltpu.VMEM((PAIR, N), BF16),
        ),
        (far_off(mask_pixels), far_off(mid_t), side, marks),
        [hbm, hbm, vmem, vmem],
        scratch=[pltpu.VMEM((N, 2 * LANES), BF16), pltpu.SemaphoreType.DMA((3,))],
        flops=2 * N * LANES * PAIR * 2,
        moved=N * LANES * 4,
    )

    def swapped(move_tile, step):
        pairs = []
        for t in range(tiles):
            for k in range(count):
                pairs.append((t * count + k, move_tile(t) * count + destination(k, step, count)))
        return pairs

    def chip_mate(t):
        return t ^ 1

    def other_side(t):
        return (t + 1 if t % 2 else t - 1) % tiles

    both = ("tile", "kern")
    far_edge = lax.ppermute(other, both, swapped(other_side, 0))
    near_pack = lax.ppermute(mate, both, swapped(chip_mate, 1))
    if count == 4:
        pairs = []
        for t in range(tiles):
            pairs += [(t * count + k, t * count + destination(k, 2 + t % 2, count)) for k in range(count)]
        kernels = [lax.ppermute(side, both, pairs)]
    else:
        kernels = [lax.ppermute(side, both, swapped(lambda t: t, step)) for step in range(2, count)]

    middle, edge_tables, rows_t = call(
        functools.partial(middle_body, row_count),
        "middle",
        (
            pltpu.VMEM((PAIR, PAIR), F32),
            pltpu.VMEM((2, PAIR, PAIR), BF16),
            pltpu.VMEM((PAIR, row_count), BF16),
        ),
        (held, mid, mid_t, marks, rims),
        [vmem] * 5,
        flops=4 * N * N * PAIR,
        moved=N * N * 2,
    )

    if count == 4:
        relayed = call(relay_body, "relay", small, (kernels[0], middle), [vmem] * 2)
        kernels.append(lax.ppermute(relayed, both, swapped(chip_mate, 0)))

    part = call(
        functools.partial(fields_body, count, row_count),
        "fields",
        small,
        (middle, target_pattern, mid, rows_t, to_columns, from_columns, edge_tables, side, near_pack, *kernels, far_edge),
        [vmem] * (8 + count),
        scratch=[
            pltpu.VMEM((count * row_count, PAIR), BF16),
            pltpu.VMEM((count * row_count, 2 * LANES), F32),
            pltpu.VMEM((count * row_count, 2 * LANES), F32),
            pltpu.VMEM((count * row_count, 2 * LANES), BF16),
            pltpu.VMEM((count * row_count, 2 * LANES), BF16),
            pltpu.VMEM((count * row_count, PAIR), F32),
        ],
        flops=8 * count * row_count * N * PAIR,
        moved=4 * row_count * N,
    )

    parts = [part]
    for step in range(1, count):
        pairs = []
        for t in range(tiles):
            own_step = sum_step(step, t, count)
            pairs += [(t * count + k, t * count + destination(k, own_step, count)) for k in range(count)]
        parts.append(lax.ppermute(part, both, pairs))
    own = call(functools.partial(sum_body, count), "total", small, tuple(parts), [vmem] * count)
    near = lax.ppermute(own, "tile", [(t, chip_mate(t)) for t in range(tiles)])
    inner = [t for t in range(tiles) if 0 < t < tiles - 1]
    far = lax.ppermute(own, "tile", [(t, other_side(t)) for t in inner])
    begun = call(
        functools.partial(inner_body, row_count),
        "inner",
        pltpu.VMEM((row_count, N), F32),
        (own, mid, back),
        [vmem] * 3,
        flops=2 * row_count * PAIR * N,
        moved=4 * row_count * N,
    )
    return call(
        functools.partial(outer_body, row_count),
        "outer",
        jax.ShapeDtypeStruct((row_count, N), F32),
        (near, far, near_pack, far_edge, mid, margins, begun),
        [vmem] * 7,
        hbm,
        scratch=[
            pltpu.VMEM((2, row_count, LANES), F32),
            pltpu.SemaphoreType.DMA((3,)),
        ],
        flops=2 * row_count * PAIR * 6 * PAIR,
        moved=4 * row_count * 2 * LANES,
    )


def solution(mesh):
    in_specs = (
        P(None, "tile"),
        P("tile", None),
        P("kern", "tile"),
        P("kern", None, None),
        P("kern", None, None),
        P("kern"),
    )
    out_specs = P("kern", "tile")
    return jax.shard_map(
        per_device, mesh=mesh, in_specs=in_specs, out_specs=out_specs, check_vma=False
    )
```

```python
import functools
import math

import jax
import jax.numpy as jnp
import ml_dtypes
import numpy as np
from jax import lax
from jax.experimental import pallas as pl
from jax.experimental.pallas import tpu as pltpu
from jax.sharding import PartitionSpec as P

N = 1152
HALO = 64
KF = 64
NE = 1280
LANES = 128
PAIR = 2 * KF
BLOCKS = N // LANES
EDGE = KF
MARKS = 16
BF16 = jnp.bfloat16
F32 = jnp.float32
VMEM_LIMIT = 32 * 1024 * 1024


def wave_tables():
    position = np.arange(NE)[:, None]
    frequency = np.arange(KF)[None, :] - KF // 2
    phase = np.mod(position * frequency, NE).astype(np.float64) * (2.0 * math.pi / NE)
    return np.cos(phase).astype(np.float32), np.sin(phase).astype(np.float32)


def transform_tables():
    cos, sin = wave_tables()
    full = np.concatenate([cos, sin], 1)
    mid = full[HALO : HALO + N]
    ct, st = cos[HALO : HALO + N].T, sin[HALO : HALO + N].T
    columns = np.concatenate(
        [
            np.stack([ct.reshape(KF, BLOCKS, LANES), st.reshape(KF, BLOCKS, LANES)], 2),
            np.stack([-st.reshape(KF, BLOCKS, LANES), ct.reshape(KF, BLOCKS, LANES)], 2),
        ],
        0,
    )
    to_columns = columns.transpose(1, 0, 2, 3).reshape(BLOCKS, PAIR, 2 * LANES)
    from_columns = to_columns.transpose(0, 2, 1)
    low, high = full[:HALO], full[HALO + N :]
    blank = np.zeros((HALO, PAIR), np.float32)
    rims = np.stack(
        [
            np.concatenate([low[::-1], blank], 0),
            np.concatenate([low, blank], 0),
            np.concatenate([high[::-1], blank], 0),
            np.concatenate([high, blank], 0),
        ]
    )
    back = np.concatenate([cos.T, -sin.T], 0)
    back_low, back_high = back[:, :HALO], back[:, HALO + N :]
    blank = np.zeros((PAIR, HALO), np.float32)
    margins = np.stack(
        [
            np.concatenate([back_high[:, ::-1], blank], 1),
            np.concatenate([back_high, blank], 1),
            np.concatenate([blank, back_low[:, ::-1]], 1),
            np.concatenate([blank, back_low], 1),
        ]
    )
    tables = (mid, mid.T, to_columns, from_columns, rims, back[:, HALO : HALO + N], margins)
    return tuple(np.ascontiguousarray(one).astype(ml_dtypes.bfloat16) for one in tables)


def dot(a, b):
    return jnp.dot(a, b, preferred_element_type=F32)


def in_left_half(shape):
    return lax.broadcasted_iota(jnp.int32, shape, 1) < KF


def swap_halves(pair):
    return pltpu.roll(pair, KF, 1)


def sum_step(step, tile, count):
    return (step, (2, 3, 1)[step - 1])[tile % 2] if count == 4 else step


def destination(k, step, count):
    return k ^ step if count == 4 else (k - step) % count


def call(
    body, name, outs, args, specs, out_specs=None, scratch=(), flops=0, moved=0
):
    vmem = pl.BlockSpec(memory_space=pltpu.VMEM)
    if out_specs is None:
        out_specs = tuple(vmem for _ in outs) if isinstance(outs, tuple) else vmem
    return pl.pallas_call(
        body,
        name=name,
        out_shape=outs,
        in_specs=specs,
        out_specs=out_specs,
        scratch_shapes=list(scratch),
        compiler_params=pltpu.CompilerParams(vmem_limit_bytes=VMEM_LIMIT),
        cost_estimate=pl.CostEstimate(flops=flops, bytes_accessed=moved, transcendentals=0),
    )(*args)


def edges_body(
    mask, mid, mid_t, rims, real, imag, weight, flags, mate, other, side, tall, table, sides_out, rims_out, strips, pair, marks, sems
):
    odd = lax.rem(lax.axis_index("tile"), 2) == 1
    copies = [
        pltpu.make_async_copy(mid_t, table, sems.at[0]),
        pltpu.make_async_copy(mask.at[:, :LANES], strips.at[:, :LANES], sems.at[1]),
        pltpu.make_async_copy(mask.at[:, N - LANES :], strips.at[:, LANES:], sems.at[2]),
        pltpu.make_async_copy(real.at[0], pair.at[0], sems.at[3]),
        pltpu.make_async_copy(imag.at[0], pair.at[1], sems.at[4]),
        pltpu.make_async_copy(flags, marks, sems.at[5]),
    ]
    turned = pltpu.make_async_copy(rims, rims_out, sems.at[6])
    columns = pltpu.make_async_copy(mid, tall, sems.at[7])
    for copy in copies:
        copy.start()
    turned.start()
    columns.start()
    for copy in copies[3:]:
        copy.wait()
    scale = jnp.sqrt(jnp.full((KF, KF), 2.0 * weight[0], F32)) * (1.0 / (NE * KF))
    kernel = jnp.concatenate([pair[0] * scale, pair[1] * scale], 1).astype(BF16)
    row = lax.broadcasted_iota(jnp.int32, (16, LANES), 0)
    sides = jnp.where(row == 0, marks[0, 0].astype(F32), marks[0, 1].astype(F32)).astype(BF16)
    side[...] = kernel
    mate[EDGE : 2 * EDGE, :] = kernel
    mate[2 * EDGE :, :] = sides
    other[EDGE:, :] = sides
    sides_out[...] = sides
    for copy in copies[:3]:
        copy.wait()
    both = dot(table[...], strips[...])
    left = in_left_half((KF, LANES))
    first, last = both[:, :LANES], both[:, LANES:]
    first = jnp.where(left, first[:KF], swap_halves(first[KF:]))
    last = jnp.where(left, swap_halves(last[:KF]), last[KF:])
    mate[:EDGE, :] = jnp.where(odd, first, last).astype(BF16)
    other[:EDGE, :] = jnp.where(odd, last, first).astype(BF16)
    turned.wait()
    columns.wait()


def middle_body(row_count, mask, mid, mid_t, marks, rims, out, tables, rows_t):
    rows_t[...] = own_rows(mid, row_count).astype(F32).T.astype(BF16)
    tile, tiles = lax.axis_index("tile"), lax.axis_size("tile")
    own = marks[...].astype(F32)
    low = jnp.where(own[0:1] == 1.0, rims[1].astype(F32), rims[0].astype(F32))
    high = jnp.where(own[1:2] == 1.0, rims[3].astype(F32), rims[2].astype(F32))
    low = jnp.where(tile == 0, 0.0, low).astype(BF16)
    high = jnp.where(tile == tiles - 1, 0.0, high).astype(BF16)
    odd = lax.rem(tile, 2) == 1
    tables[0] = jnp.where(odd, low, high)
    tables[1] = jnp.where(odd, high, low)
    out[...] = dot(mid_t[...], dot(mask[...], mid[...]).astype(BF16))


def relay_body(value, ready, out):
    out[...] = value[...]


def split_kernel(pair):
    left = in_left_half(pair.shape)
    other = swap_halves(pair)
    return jnp.where(left, pair, other), jnp.where(left, other, pair)


def fields_body(count, row_count, *refs):
    (middle, target, mid, rows_t, to_columns, from_columns, tables, own) = refs[:8]
    near_pack, *others, far_edge = refs[8 : 8 + count]
    out, a_ref, field_a, field_b, bent_a, bent_b, u_ref = refs[8 + count :]
    fields, bent = (field_a, field_b), (bent_a, bent_b)
    left = in_left_half((KF, PAIR))
    blocks = middle[...]
    for pack, table in ((near_pack, tables[0]), (far_edge, tables[1])):
        edge = pack[:EDGE, :].astype(F32)
        edge = jnp.concatenate([edge, swap_halves(edge)], 0).astype(BF16)
        blocks = blocks + dot(edge, table)
    top, bottom = blocks[:KF], swap_halves(blocks[KF:])
    spectrum = jnp.where(left, top - bottom, -(top + bottom))
    turned = swap_halves(spectrum)
    turned = jnp.where(left, -turned, turned)
    kernels = [own[...].astype(F32)]
    kernels.append(near_pack[EDGE : 2 * EDGE, :].astype(F32))
    kernels += [one[...].astype(F32) for one in others]
    kernels = [split_kernel(one) for one in kernels]
    begin = pl.multiple_of(lax.axis_index("kern") * row_count, row_count)
    rows = mid[pl.ds(begin, row_count), :]
    stacks = []
    for real, imag in kernels:
        product = real * spectrum + imag * turned
        other = swap_halves(product)
        other = jnp.where(left, -other, other)
        stacks.append(jnp.concatenate([product, other], 0).astype(BF16))
    waves = dot(rows, jnp.concatenate(stacks, 1)).astype(BF16)
    for index in range(count):
        a_ref[index * row_count : (index + 1) * row_count, :] = waves[:, index * PAIR : (index + 1) * PAIR]
    step = 32 if row_count % 32 == 0 else 16
    halves = (slice(0, LANES), slice(LANES, 2 * LANES))
    fields[0][...] = dot(a_ref[...], to_columns[0])
    for block in range(BLOCKS + 1):
        now = block % 2
        if block + 1 < BLOCKS:
            fields[1 - now][...] = dot(a_ref[...], to_columns[block + 1])
        if block > 0:
            part = dot(bent[1 - now][...], from_columns[block - 1])
            u_ref[...] = part if block == 1 else u_ref[...] + part
        if block == BLOCKS:
            continue
        for r in range(0, row_count, step):
            total = None
            for index in range(count):
                at = index * row_count + r
                real, imag = (fields[now][at : at + step, half] for half in halves)
                term = real * real + imag * imag
                total = term if total is None else total + term
            wanted = target[r : r + step, block * LANES : (block + 1) * LANES].astype(F32)
            decay = jnp.exp(4.0 - 2.0 * total)
            resist = pl.reciprocal(1.0 + decay, approx=True)
            slope = (resist - wanted) * (8.0 * decay) * (resist * resist)
            for index in range(count):
                at = index * row_count + r
                for half in halves:
                    field = fields[now][at : at + step, half] * slope
                    bent[now][at : at + step, half] = field.astype(BF16)
    wide = jnp.concatenate(
        [u_ref[i * row_count : (i + 1) * row_count, :].astype(BF16) for i in range(count)], 1
    )
    waves = dot(rows_t[...], wide)
    total = None
    for index, (real, imag) in enumerate(kernels):
        wave = waves[:, index * PAIR : (index + 1) * PAIR]
        top, bottom = wave[:KF], swap_halves(wave[KF:])
        wave = jnp.where(left, top + bottom, top - bottom)
        other = swap_halves(wave)
        other = jnp.where(left, other, -other)
        term = real * wave + imag * other
        total = term if total is None else total + term
    out[...] = total.astype(BF16)


def sum_body(count, *refs):
    total = refs[0][...].astype(F32)
    for one in refs[1:count]:
        total = total + one[...].astype(F32)
    refs[count][...] = total.astype(BF16)


def row_waves(rows, pair):
    pair = pair.astype(F32)
    other = swap_halves(pair)
    other = jnp.where(in_left_half(pair.shape), -other, other)
    return dot(rows, jnp.concatenate([pair, other], 0).astype(BF16)).astype(BF16)


def own_rows(mid, row_count):
    begin = pl.multiple_of(lax.axis_index("kern") * row_count, row_count)
    return mid[pl.ds(begin, row_count), :]


def inner_body(row_count, own, mid, back, out):
    out[...] = dot(row_waves(own_rows(mid, row_count), own[...]), back[...])


def outer_body(
    row_count, near, far, near_pack, far_edge, mid, margins, begun, out, held, sems
):
    inner = pltpu.make_async_copy(
        begun.at[:, LANES : N - LANES], out.at[:, LANES : N - LANES], sems.at[2]
    )
    inner.start()
    rows = own_rows(mid, row_count)
    near_wave, far_wave = row_waves(rows, near[...]), row_waves(rows, far[...])
    odd = lax.rem(lax.axis_index("tile"), 2) == 1
    below, above = jnp.where(odd, near_wave, far_wave), jnp.where(odd, far_wave, near_wave)
    near_marks = near_pack[2 * EDGE :, :].astype(F32)
    far_marks = far_edge[EDGE:, :].astype(F32)
    low_mark = jnp.where(odd, near_marks, far_marks)[1:2]
    high_mark = jnp.where(odd, far_marks, near_marks)[0:1]
    low = jnp.where(low_mark == 1.0, margins[1].astype(F32), margins[0].astype(F32)).astype(BF16)
    high = jnp.where(high_mark == 1.0, margins[3].astype(F32), margins[2].astype(F32)).astype(BF16)
    copies = []
    for side, first, wave, table in ((0, 0, below, low), (1, N - LANES, above, high)):
        columns = slice(first, first + LANES)
        held[side] = begun[:, columns] + dot(wave, table)
        copies.append(pltpu.make_async_copy(held.at[side], out.at[:, columns], sems.at[side]))
        copies[-1].start()
    for copy in (inner, *copies):
        copy.wait()


def far_off(array):
    return pltpu.with_memory_space_constraint(array, pltpu.HBM)


def per_device(mask_pixels, orientation, target_pattern, kernel_real, kernel_imag, eigen_weights):
    tables = tuple(jnp.asarray(one) for one in transform_tables())
    mid, mid_t, to_columns, from_columns, rims, back, margins = tables
    tiles, count = lax.axis_size("tile"), lax.axis_size("kern")
    row_count = target_pattern.shape[0]
    vmem = pl.BlockSpec(memory_space=pltpu.VMEM)
    smem = pl.BlockSpec(memory_space=pltpu.SMEM)
    hbm = pl.BlockSpec(memory_space=pltpu.HBM)
    small = jax.ShapeDtypeStruct((KF, PAIR), BF16)

    mate, other, side, mid, mid_t, marks, rims = call(
        edges_body,
        "edges",
        (
            pltpu.VMEM((2 * EDGE + MARKS, LANES), BF16),
            pltpu.VMEM((EDGE + MARKS, LANES), BF16),
            pltpu.VMEM((KF, PAIR), BF16),
            pltpu.VMEM((N, PAIR), BF16),
            pltpu.VMEM((PAIR, N), BF16),
            pltpu.VMEM((MARKS, LANES), BF16),
            pltpu.VMEM((4, LANES, PAIR), BF16),
        ),
        (
            *(far_off(one) for one in (mask_pixels, mid, mid_t, rims, kernel_real, kernel_imag)),
            eigen_weights,
            far_off(orientation),
        ),
        [hbm] * 6 + [smem, hbm],
        scratch=[
            pltpu.VMEM((N, 2 * LANES), BF16),
            pltpu.VMEM((2, KF, KF), F32),
            pltpu.SMEM((1, 2), jnp.int32),
            pltpu.SemaphoreType.DMA((8,)),
        ],
        flops=2 * N * LANES * PAIR * 2,
        moved=N * LANES * 4,
    )

    def swapped(move_tile, step):
        pairs = []
        for t in range(tiles):
            for k in range(count):
                pairs.append((t * count + k, move_tile(t) * count + destination(k, step, count)))
        return pairs

    def chip_mate(t):
        return t ^ 1

    def other_side(t):
        return (t + 1 if t % 2 else t - 1) % tiles

    both = ("tile", "kern")
    far_edge = lax.ppermute(other, both, swapped(other_side, 0))
    near_pack = lax.ppermute(mate, both, swapped(chip_mate, 1))
    if count == 4:
        pairs = []
        for t in range(tiles):
            pairs += [(t * count + k, t * count + destination(k, 2 + t % 2, count)) for k in range(count)]
        kernels = [lax.ppermute(side, both, pairs)]
    else:
        kernels = [lax.ppermute(side, both, swapped(lambda t: t, step)) for step in range(2, count)]

    middle, edge_tables, rows_t = call(
        functools.partial(middle_body, row_count),
        "middle",
        (
            pltpu.VMEM((PAIR, PAIR), F32),
            pltpu.VMEM((2, PAIR, PAIR), BF16),
            pltpu.VMEM((PAIR, row_count), BF16),
        ),
        (pltpu.with_memory_space_constraint(mask_pixels, pltpu.VMEM), mid, mid_t, marks, rims),
        [vmem] * 5,
        flops=4 * N * N * PAIR,
        moved=N * N * 2,
    )

    if count == 4:
        relayed = call(relay_body, "relay", small, (kernels[0], middle), [vmem] * 2)
        kernels.append(lax.ppermute(relayed, both, swapped(chip_mate, 0)))

    part = call(
        functools.partial(fields_body, count, row_count),
        "fields",
        small,
        (middle, target_pattern, mid, rows_t, to_columns, from_columns, edge_tables, side, near_pack, *kernels, far_edge),
        [vmem] * (8 + count),
        scratch=[
            pltpu.VMEM((count * row_count, PAIR), BF16),
            pltpu.VMEM((count * row_count, 2 * LANES), F32),
            pltpu.VMEM((count * row_count, 2 * LANES), F32),
            pltpu.VMEM((count * row_count, 2 * LANES), BF16),
            pltpu.VMEM((count * row_count, 2 * LANES), BF16),
            pltpu.VMEM((count * row_count, PAIR), F32),
        ],
        flops=8 * count * row_count * N * PAIR,
        moved=4 * row_count * N,
    )

    parts = [part]
    for step in range(1, count):
        pairs = []
        for t in range(tiles):
            own_step = sum_step(step, t, count)
            pairs += [(t * count + k, t * count + destination(k, own_step, count)) for k in range(count)]
        parts.append(lax.ppermute(part, both, pairs))
    own = call(functools.partial(sum_body, count), "total", small, tuple(parts), [vmem] * count)
    near = lax.ppermute(own, "tile", [(t, chip_mate(t)) for t in range(tiles)])
    inner = [t for t in range(tiles) if 0 < t < tiles - 1]
    far = lax.ppermute(own, "tile", [(t, other_side(t)) for t in inner])
    begun = call(
        functools.partial(inner_body, row_count),
        "inner",
        pltpu.VMEM((row_count, N), F32),
        (own, mid, back),
        [vmem] * 3,
        flops=2 * row_count * PAIR * N,
        moved=4 * row_count * N,
    )
    return call(
        functools.partial(outer_body, row_count),
        "outer",
        jax.ShapeDtypeStruct((row_count, N), F32),
        (near, far, near_pack, far_edge, mid, margins, begun),
        [vmem] * 7,
        hbm,
        scratch=[
            pltpu.VMEM((2, row_count, LANES), F32),
            pltpu.SemaphoreType.DMA((3,)),
        ],
        flops=2 * row_count * PAIR * 6 * PAIR,
        moved=4 * row_count * 2 * LANES,
    )


def solution(mesh):
    in_specs = (
        P(None, "tile"),
        P("tile", None),
        P("kern", "tile"),
        P("kern", None, None),
        P("kern", None, None),
        P("kern"),
    )
    out_specs = P("kern", "tile")
    return jax.shard_map(
        per_device, mesh=mesh, in_specs=in_specs, out_specs=out_specs, check_vma=False
    )
```

```python
import functools
import math

import jax
import jax.numpy as jnp
import ml_dtypes
import numpy as np
from jax import lax
from jax.experimental import pallas as pl
from jax.experimental.pallas import tpu as pltpu
from jax.sharding import PartitionSpec as P

N = 1152
HALO = 64
KF = 64
NE = 1280
LANES = 128
PAIR = 2 * KF
BLOCKS = N // LANES
EDGE = KF
MARKS = 16
BF16 = jnp.bfloat16
F32 = jnp.float32
VMEM_LIMIT = 32 * 1024 * 1024


def wave_tables():
    position = np.arange(NE)[:, None]
    frequency = np.arange(KF)[None, :] - KF // 2
    phase = np.mod(position * frequency, NE).astype(np.float64) * (2.0 * math.pi / NE)
    return np.cos(phase).astype(np.float32), np.sin(phase).astype(np.float32)


def transform_tables():
    cos, sin = wave_tables()
    full = np.concatenate([cos, sin], 1)
    mid = full[HALO : HALO + N]
    ct, st = cos[HALO : HALO + N].T, sin[HALO : HALO + N].T
    columns = np.concatenate(
        [
            np.stack([ct.reshape(KF, BLOCKS, LANES), st.reshape(KF, BLOCKS, LANES)], 2),
            np.stack([-st.reshape(KF, BLOCKS, LANES), ct.reshape(KF, BLOCKS, LANES)], 2),
        ],
        0,
    )
    to_columns = columns.transpose(1, 0, 2, 3).reshape(BLOCKS, PAIR, 2 * LANES)
    from_columns = to_columns.transpose(0, 2, 1)
    low, high = full[:HALO], full[HALO + N :]
    blank = np.zeros((HALO, PAIR), np.float32)
    rims = np.stack(
        [
            np.concatenate([low[::-1], blank], 0),
            np.concatenate([low, blank], 0),
            np.concatenate([high[::-1], blank], 0),
            np.concatenate([high, blank], 0),
        ]
    )
    back = np.concatenate([cos.T, -sin.T], 0)
    back_low, back_high = back[:, :HALO], back[:, HALO + N :]
    blank = np.zeros((PAIR, HALO), np.float32)
    margins = np.stack(
        [
            np.concatenate([back_high[:, ::-1], blank], 1),
            np.concatenate([back_high, blank], 1),
            np.concatenate([blank, back_low[:, ::-1]], 1),
            np.concatenate([blank, back_low], 1),
        ]
    )
    tables = (mid, mid.T, to_columns, from_columns, rims, back[:, HALO : HALO + N], margins)
    return tuple(np.ascontiguousarray(one).astype(ml_dtypes.bfloat16) for one in tables)


def dot(a, b):
    return jnp.dot(a, b, preferred_element_type=F32)


def in_left_half(shape):
    return lax.broadcasted_iota(jnp.int32, shape, 1) < KF


def swap_halves(pair):
    return pltpu.roll(pair, KF, 1)


def sum_step(step, tile, count):
    return (step, (2, 3, 1)[step - 1])[tile % 2] if count == 4 else step


def destination(k, step, count):
    return k ^ step if count == 4 else (k - step) % count


def call(
    body, name, outs, args, specs, out_specs=None, scratch=(), flops=0, moved=0
):
    vmem = pl.BlockSpec(memory_space=pltpu.VMEM)
    if out_specs is None:
        out_specs = tuple(vmem for _ in outs) if isinstance(outs, tuple) else vmem
    return pl.pallas_call(
        body,
        name=name,
        out_shape=outs,
        in_specs=specs,
        out_specs=out_specs,
        scratch_shapes=list(scratch),
        compiler_params=pltpu.CompilerParams(vmem_limit_bytes=VMEM_LIMIT),
        cost_estimate=pl.CostEstimate(flops=flops, bytes_accessed=moved, transcendentals=0),
    )(*args)


def edges_body(
    mask, mid, mid_t, rims, real, imag, weight, flags, mate, other, side, tall, table, sides_out, rims_out, strips, pair, marks, sems
):
    odd = lax.rem(lax.axis_index("tile"), 2) == 1
    copies = [
        pltpu.make_async_copy(mid_t, table, sems.at[0]),
        pltpu.make_async_copy(mask.at[:, :LANES], strips.at[:, :LANES], sems.at[1]),
        pltpu.make_async_copy(mask.at[:, N - LANES :], strips.at[:, LANES:], sems.at[2]),
        pltpu.make_async_copy(real.at[0], pair.at[0], sems.at[3]),
        pltpu.make_async_copy(imag.at[0], pair.at[1], sems.at[4]),
        pltpu.make_async_copy(flags, marks, sems.at[5]),
    ]
    turned = pltpu.make_async_copy(rims, rims_out, sems.at[6])
    columns = pltpu.make_async_copy(mid, tall, sems.at[7])
    for copy in copies:
        copy.start()
    turned.start()
    columns.start()
    for copy in copies[3:]:
        copy.wait()
    scale = jnp.sqrt(jnp.full((KF, KF), 2.0 * weight[0], F32)) * (1.0 / (NE * KF))
    kernel = jnp.concatenate([pair[0] * scale, pair[1] * scale], 1).astype(BF16)
    row = lax.broadcasted_iota(jnp.int32, (16, LANES), 0)
    sides = jnp.where(row == 0, marks[0, 0].astype(F32), marks[0, 1].astype(F32)).astype(BF16)
    side[...] = kernel
    mate[EDGE : 2 * EDGE, :] = kernel
    mate[2 * EDGE :, :] = sides
    other[EDGE:, :] = sides
    sides_out[...] = sides
    for copy in copies[:3]:
        copy.wait()
    both = dot(table[...], strips[...])
    left = in_left_half((KF, LANES))
    first, last = both[:, :LANES], both[:, LANES:]
    first = jnp.where(left, first[:KF], swap_halves(first[KF:]))
    last = jnp.where(left, swap_halves(last[:KF]), last[KF:])
    mate[:EDGE, :] = jnp.where(odd, first, last).astype(BF16)
    other[:EDGE, :] = jnp.where(odd, last, first).astype(BF16)
    turned.wait()
    columns.wait()


def middle_body(row_count, mask, mid, mid_t, marks, rims, out, tables, rows_t):
    rows_t[...] = own_rows(mid, row_count).astype(F32).T.astype(BF16)
    tile, tiles = lax.axis_index("tile"), lax.axis_size("tile")
    own = marks[...].astype(F32)
    low = jnp.where(own[0:1] == 1.0, rims[1].astype(F32), rims[0].astype(F32))
    high = jnp.where(own[1:2] == 1.0, rims[3].astype(F32), rims[2].astype(F32))
    low = jnp.where(tile == 0, 0.0, low).astype(BF16)
    high = jnp.where(tile == tiles - 1, 0.0, high).astype(BF16)
    odd = lax.rem(tile, 2) == 1
    tables[0] = jnp.where(odd, low, high)
    tables[1] = jnp.where(odd, high, low)
    out[...] = dot(mid_t[...], dot(mask[...], mid[...]).astype(BF16))


def relay_body(value, ready, out):
    out[...] = value[...]


def split_kernel(pair):
    left = in_left_half(pair.shape)
    other = swap_halves(pair)
    return jnp.where(left, pair, other), jnp.where(left, other, pair)


def spectrum_body(middle, tables, near_pack, far_edge, out):
    left = in_left_half((KF, PAIR))
    blocks = middle[...]
    for pack, table in ((near_pack, tables[0]), (far_edge, tables[1])):
        edge = pack[:EDGE, :].astype(F32)
        edge = jnp.concatenate([edge, swap_halves(edge)], 0).astype(BF16)
        blocks = blocks + dot(edge, table)
    top, bottom = blocks[:KF], swap_halves(blocks[KF:])
    spectrum = jnp.where(left, top - bottom, -(top + bottom))
    turned = swap_halves(spectrum)
    turned = jnp.where(left, -turned, turned)
    out[0], out[1] = spectrum, turned


def fields_body(count, row_count, *refs):
    (spectra, target, mid, rows_t, to_columns, from_columns, own) = refs[:7]
    near_pack, *others = refs[7 : 6 + count]
    out, a_ref, field_a, field_b, bent_a, bent_b, u_ref = refs[6 + count :]
    fields, bent = (field_a, field_b), (bent_a, bent_b)
    left = in_left_half((KF, PAIR))
    spectrum, turned = spectra[0], spectra[1]
    kernels = [own[...].astype(F32)]
    kernels.append(near_pack[EDGE : 2 * EDGE, :].astype(F32))
    kernels += [one[...].astype(F32) for one in others]
    kernels = [split_kernel(one) for one in kernels]
    begin = pl.multiple_of(lax.axis_index("kern") * row_count, row_count)
    rows = mid[pl.ds(begin, row_count), :]
    stacks = []
    for real, imag in kernels:
        product = real * spectrum + imag * turned
        other = swap_halves(product)
        other = jnp.where(left, -other, other)
        stacks.append(jnp.concatenate([product, other], 0).astype(BF16))
    waves = dot(rows, jnp.concatenate(stacks, 1)).astype(BF16)
    for index in range(count):
        a_ref[index * row_count : (index + 1) * row_count, :] = waves[:, index * PAIR : (index + 1) * PAIR]
    step = 32 if row_count % 32 == 0 else 16
    halves = (slice(0, LANES), slice(LANES, 2 * LANES))
    fields[0][...] = dot(a_ref[...], to_columns[0])
    for block in range(BLOCKS + 1):
        now = block % 2
        if block + 1 < BLOCKS:
            fields[1 - now][...] = dot(a_ref[...], to_columns[block + 1])
        if block > 0:
            part = dot(bent[1 - now][...], from_columns[block - 1])
            u_ref[...] = part if block == 1 else u_ref[...] + part
        if block == BLOCKS:
            continue
        for r in range(0, row_count, step):
            total = None
            for index in range(count):
                at = index * row_count + r
                real, imag = (fields[now][at : at + step, half] for half in halves)
                term = real * real + imag * imag
                total = term if total is None else total + term
            wanted = target[r : r + step, block * LANES : (block + 1) * LANES].astype(F32)
            decay = jnp.exp(4.0 - 2.0 * total)
            resist = pl.reciprocal(1.0 + decay, approx=True)
            slope = (resist - wanted) * (8.0 * decay) * (resist * resist)
            for index in range(count):
                at = index * row_count + r
                for half in halves:
                    field = fields[now][at : at + step, half] * slope
                    bent[now][at : at + step, half] = field.astype(BF16)
    wide = jnp.concatenate(
        [u_ref[i * row_count : (i + 1) * row_count, :].astype(BF16) for i in range(count)], 1
    )
    waves = dot(rows_t[...], wide)
    total = None
    for index, (real, imag) in enumerate(kernels):
        wave = waves[:, index * PAIR : (index + 1) * PAIR]
        top, bottom = wave[:KF], swap_halves(wave[KF:])
        wave = jnp.where(left, top + bottom, top - bottom)
        other = swap_halves(wave)
        other = jnp.where(left, other, -other)
        term = real * wave + imag * other
        total = term if total is None else total + term
    out[...] = total.astype(BF16)


def sum_body(count, *refs):
    total = refs[0][...].astype(F32)
    for one in refs[1:count]:
        total = total + one[...].astype(F32)
    refs[count][...] = total.astype(BF16)


def row_waves(rows, pair):
    pair = pair.astype(F32)
    other = swap_halves(pair)
    other = jnp.where(in_left_half(pair.shape), -other, other)
    return dot(rows, jnp.concatenate([pair, other], 0).astype(BF16)).astype(BF16)


def own_rows(mid, row_count):
    begin = pl.multiple_of(lax.axis_index("kern") * row_count, row_count)
    return mid[pl.ds(begin, row_count), :]


def inner_body(row_count, own, mid, back, out):
    out[...] = dot(row_waves(own_rows(mid, row_count), own[...]), back[...])


def outer_body(
    row_count, near, far, near_pack, far_edge, mid, margins, begun, out, held, sems
):
    inner = pltpu.make_async_copy(
        begun.at[:, LANES : N - LANES], out.at[:, LANES : N - LANES], sems.at[2]
    )
    inner.start()
    rows = own_rows(mid, row_count)
    near_wave, far_wave = row_waves(rows, near[...]), row_waves(rows, far[...])
    odd = lax.rem(lax.axis_index("tile"), 2) == 1
    below, above = jnp.where(odd, near_wave, far_wave), jnp.where(odd, far_wave, near_wave)
    near_marks = near_pack[2 * EDGE :, :].astype(F32)
    far_marks = far_edge[EDGE:, :].astype(F32)
    low_mark = jnp.where(odd, near_marks, far_marks)[1:2]
    high_mark = jnp.where(odd, far_marks, near_marks)[0:1]
    low = jnp.where(low_mark == 1.0, margins[1].astype(F32), margins[0].astype(F32)).astype(BF16)
    high = jnp.where(high_mark == 1.0, margins[3].astype(F32), margins[2].astype(F32)).astype(BF16)
    copies = []
    for side, first, wave, table in ((0, 0, below, low), (1, N - LANES, above, high)):
        columns = slice(first, first + LANES)
        held[side] = begun[:, columns] + dot(wave, table)
        copies.append(pltpu.make_async_copy(held.at[side], out.at[:, columns], sems.at[side]))
        copies[-1].start()
    for copy in (inner, *copies):
        copy.wait()


def far_off(array):
    return pltpu.with_memory_space_constraint(array, pltpu.HBM)


def per_device(mask_pixels, orientation, target_pattern, kernel_real, kernel_imag, eigen_weights):
    tables = tuple(jnp.asarray(one) for one in transform_tables())
    mid, mid_t, to_columns, from_columns, rims, back, margins = tables
    tiles, count = lax.axis_size("tile"), lax.axis_size("kern")
    row_count = target_pattern.shape[0]
    vmem = pl.BlockSpec(memory_space=pltpu.VMEM)
    smem = pl.BlockSpec(memory_space=pltpu.SMEM)
    hbm = pl.BlockSpec(memory_space=pltpu.HBM)
    small = jax.ShapeDtypeStruct((KF, PAIR), BF16)

    mate, other, side, mid, mid_t, marks, rims = call(
        edges_body,
        "edges",
        (
            pltpu.VMEM((2 * EDGE + MARKS, LANES), BF16),
            pltpu.VMEM((EDGE + MARKS, LANES), BF16),
            pltpu.VMEM((KF, PAIR), BF16),
            pltpu.VMEM((N, PAIR), BF16),
            pltpu.VMEM((PAIR, N), BF16),
            pltpu.VMEM((MARKS, LANES), BF16),
            pltpu.VMEM((4, LANES, PAIR), BF16),
        ),
        (
            *(far_off(one) for one in (mask_pixels, mid, mid_t, rims, kernel_real, kernel_imag)),
            eigen_weights,
            far_off(orientation),
        ),
        [hbm] * 6 + [smem, hbm],
        scratch=[
            pltpu.VMEM((N, 2 * LANES), BF16),
            pltpu.VMEM((2, KF, KF), F32),
            pltpu.SMEM((1, 2), jnp.int32),
            pltpu.SemaphoreType.DMA((8,)),
        ],
        flops=2 * N * LANES * PAIR * 2,
        moved=N * LANES * 4,
    )

    def swapped(move_tile, step):
        pairs = []
        for t in range(tiles):
            for k in range(count):
                pairs.append((t * count + k, move_tile(t) * count + destination(k, step, count)))
        return pairs

    def chip_mate(t):
        return t ^ 1

    def other_side(t):
        return (t + 1 if t % 2 else t - 1) % tiles

    both = ("tile", "kern")
    far_edge = lax.ppermute(other, both, swapped(other_side, 0))
    near_pack = lax.ppermute(mate, both, swapped(chip_mate, 1))
    if count == 4:
        pairs = []
        for t in range(tiles):
            pairs += [(t * count + k, t * count + destination(k, 2 + t % 2, count)) for k in range(count)]
        kernels = [lax.ppermute(side, both, pairs)]
    else:
        kernels = [lax.ppermute(side, both, swapped(lambda t: t, step)) for step in range(2, count)]

    middle, edge_tables, rows_t = call(
        functools.partial(middle_body, row_count),
        "middle",
        (
            pltpu.VMEM((PAIR, PAIR), F32),
            pltpu.VMEM((2, PAIR, PAIR), BF16),
            pltpu.VMEM((PAIR, row_count), BF16),
        ),
        (pltpu.with_memory_space_constraint(mask_pixels, pltpu.VMEM), mid, mid_t, marks, rims),
        [vmem] * 5,
        flops=4 * N * N * PAIR,
        moved=N * N * 2,
    )

    if count == 4:
        relayed = call(relay_body, "relay", small, (kernels[0], middle), [vmem] * 2)
        kernels.append(lax.ppermute(relayed, both, swapped(chip_mate, 0)))

    spectra = call(
        spectrum_body,
        "spectrum",
        pltpu.VMEM((2, KF, PAIR), F32),
        (middle, edge_tables, near_pack, far_edge),
        [vmem] * 4,
    )
    part = call(
        functools.partial(fields_body, count, row_count),
        "fields",
        small,
        (spectra, target_pattern, mid, rows_t, to_columns, from_columns, side, near_pack, *kernels),
        [vmem] * (6 + count),
        scratch=[
            pltpu.VMEM((count * row_count, PAIR), BF16),
            pltpu.VMEM((count * row_count, 2 * LANES), F32),
            pltpu.VMEM((count * row_count, 2 * LANES), F32),
            pltpu.VMEM((count * row_count, 2 * LANES), BF16),
            pltpu.VMEM((count * row_count, 2 * LANES), BF16),
            pltpu.VMEM((count * row_count, PAIR), F32),
        ],
        flops=8 * count * row_count * N * PAIR,
        moved=4 * row_count * N,
    )

    parts = [part]
    for step in range(1, count):
        pairs = []
        for t in range(tiles):
            own_step = sum_step(step, t, count)
            pairs += [(t * count + k, t * count + destination(k, own_step, count)) for k in range(count)]
        parts.append(lax.ppermute(part, both, pairs))
    own = call(functools.partial(sum_body, count), "total", small, tuple(parts), [vmem] * count)
    near = lax.ppermute(own, "tile", [(t, chip_mate(t)) for t in range(tiles)])
    inner = [t for t in range(tiles) if 0 < t < tiles - 1]
    far = lax.ppermute(own, "tile", [(t, other_side(t)) for t in inner])
    begun = call(
        functools.partial(inner_body, row_count),
        "inner",
        pltpu.VMEM((row_count, N), F32),
        (own, mid, back),
        [vmem] * 3,
        flops=2 * row_count * PAIR * N,
        moved=4 * row_count * N,
    )
    return call(
        functools.partial(outer_body, row_count),
        "outer",
        jax.ShapeDtypeStruct((row_count, N), F32),
        (near, far, near_pack, far_edge, mid, margins, begun),
        [vmem] * 7,
        hbm,
        scratch=[
            pltpu.VMEM((2, row_count, LANES), F32),
            pltpu.SemaphoreType.DMA((3,)),
        ],
        flops=2 * row_count * PAIR * 6 * PAIR,
        moved=4 * row_count * 2 * LANES,
    )


def solution(mesh):
    in_specs = (
        P(None, "tile"),
        P("tile", None),
        P("kern", "tile"),
        P("kern", None, None),
        P("kern", None, None),
        P("kern"),
    )
    out_specs = P("kern", "tile")
    return jax.shard_map(
        per_device, mesh=mesh, in_specs=in_specs, out_specs=out_specs, check_vma=False
    )
```

```python
import functools
import math

import jax
import jax.numpy as jnp
import ml_dtypes
import numpy as np
from jax import lax
from jax.experimental import pallas as pl
from jax.experimental.pallas import tpu as pltpu
from jax.sharding import PartitionSpec as P

N = 1152
HALO = 64
KF = 64
NE = 1280
LANES = 128
PAIR = 2 * KF
BLOCKS = N // LANES
EDGE = KF
MARKS = 16
BF16 = jnp.bfloat16
F32 = jnp.float32
VMEM_LIMIT = 32 * 1024 * 1024


def wave_tables():
    position = np.arange(NE)[:, None]
    frequency = np.arange(KF)[None, :] - KF // 2
    phase = np.mod(position * frequency, NE).astype(np.float64) * (2.0 * math.pi / NE)
    return np.cos(phase).astype(np.float32), np.sin(phase).astype(np.float32)


def transform_tables():
    cos, sin = wave_tables()
    full = np.concatenate([cos, sin], 1)
    mid = full[HALO : HALO + N]
    ct, st = cos[HALO : HALO + N].T, sin[HALO : HALO + N].T
    columns = np.concatenate(
        [
            np.stack([ct.reshape(KF, BLOCKS, LANES), st.reshape(KF, BLOCKS, LANES)], 2),
            np.stack([-st.reshape(KF, BLOCKS, LANES), ct.reshape(KF, BLOCKS, LANES)], 2),
        ],
        0,
    )
    to_columns = columns.transpose(1, 0, 2, 3).reshape(BLOCKS, PAIR, 2 * LANES)
    from_columns = to_columns.transpose(0, 2, 1)
    low, high = full[:HALO], full[HALO + N :]
    blank = np.zeros((HALO, PAIR), np.float32)
    rims = np.stack(
        [
            np.concatenate([low[::-1], blank], 0),
            np.concatenate([low, blank], 0),
            np.concatenate([high[::-1], blank], 0),
            np.concatenate([high, blank], 0),
        ]
    )
    back = np.concatenate([cos.T, -sin.T], 0)
    back_low, back_high = back[:, :HALO], back[:, HALO + N :]
    blank = np.zeros((PAIR, HALO), np.float32)
    margins = np.stack(
        [
            np.concatenate([back_high[:, ::-1], blank], 1),
            np.concatenate([back_high, blank], 1),
            np.concatenate([blank, back_low[:, ::-1]], 1),
            np.concatenate([blank, back_low], 1),
        ]
    )
    tables = (mid, mid.T, to_columns, from_columns, rims, back[:, HALO : HALO + N], margins)
    return tuple(np.ascontiguousarray(one).astype(ml_dtypes.bfloat16) for one in tables)


def dot(a, b):
    return jnp.dot(a, b, preferred_element_type=F32)


def in_left_half(shape):
    return lax.broadcasted_iota(jnp.int32, shape, 1) < KF


def swap_halves(pair):
    return pltpu.roll(pair, KF, 1)


def sum_step(step, tile, count):
    return (step, (2, 3, 1)[step - 1])[tile % 2] if count == 4 else step


def destination(k, step, count):
    return k ^ step if count == 4 else (k - step) % count


def call(
    body, name, outs, args, specs, out_specs=None, scratch=(), flops=0, moved=0
):
    vmem = pl.BlockSpec(memory_space=pltpu.VMEM)
    if out_specs is None:
        out_specs = tuple(vmem for _ in outs) if isinstance(outs, tuple) else vmem
    return pl.pallas_call(
        body,
        name=name,
        out_shape=outs,
        in_specs=specs,
        out_specs=out_specs,
        scratch_shapes=list(scratch),
        compiler_params=pltpu.CompilerParams(vmem_limit_bytes=VMEM_LIMIT),
        cost_estimate=pl.CostEstimate(flops=flops, bytes_accessed=moved, transcendentals=0),
    )(*args)


def edges_body(
    mask, mid, mid_t, rims, real, imag, weight, flags, mate, other, side, tall, table, sides_out, rims_out, strips, pair, marks, sems
):
    odd = lax.rem(lax.axis_index("tile"), 2) == 1
    copies = [
        pltpu.make_async_copy(mid_t, table, sems.at[0]),
        pltpu.make_async_copy(mask.at[:, :LANES], strips.at[:, :LANES], sems.at[1]),
        pltpu.make_async_copy(mask.at[:, N - LANES :], strips.at[:, LANES:], sems.at[2]),
        pltpu.make_async_copy(real.at[0], pair.at[0], sems.at[3]),
        pltpu.make_async_copy(imag.at[0], pair.at[1], sems.at[4]),
        pltpu.make_async_copy(flags, marks, sems.at[5]),
    ]
    turned = pltpu.make_async_copy(rims, rims_out, sems.at[6])
    columns = pltpu.make_async_copy(mid, tall, sems.at[7])
    for copy in copies:
        copy.start()
    turned.start()
    columns.start()
    for copy in copies[3:]:
        copy.wait()
    scale = jnp.sqrt(jnp.full((KF, KF), 2.0 * weight[0], F32)) * (1.0 / (NE * KF))
    kernel = jnp.concatenate([pair[0] * scale, pair[1] * scale], 1).astype(BF16)
    row = lax.broadcasted_iota(jnp.int32, (16, LANES), 0)
    sides = jnp.where(row == 0, marks[0, 0].astype(F32), marks[0, 1].astype(F32)).astype(BF16)
    side[...] = kernel
    mate[EDGE : 2 * EDGE, :] = kernel
    mate[2 * EDGE :, :] = sides
    other[EDGE:, :] = sides
    sides_out[...] = sides
    for copy in copies[:3]:
        copy.wait()
    both = dot(table[...], strips[...])
    left = in_left_half((KF, LANES))
    first, last = both[:, :LANES], both[:, LANES:]
    first = jnp.where(left, first[:KF], swap_halves(first[KF:]))
    last = jnp.where(left, swap_halves(last[:KF]), last[KF:])
    mate[:EDGE, :] = jnp.where(odd, first, last).astype(BF16)
    other[:EDGE, :] = jnp.where(odd, last, first).astype(BF16)
    turned.wait()
    columns.wait()


def middle_body(row_count, mask, mid, mid_t, marks, rims, out, tables, rows_t):
    rows_t[...] = own_rows(mid, row_count).astype(F32).T.astype(BF16)
    tile, tiles = lax.axis_index("tile"), lax.axis_size("tile")
    own = marks[...].astype(F32)
    low = jnp.where(own[0:1] == 1.0, rims[1].astype(F32), rims[0].astype(F32))
    high = jnp.where(own[1:2] == 1.0, rims[3].astype(F32), rims[2].astype(F32))
    low = jnp.where(tile == 0, 0.0, low).astype(BF16)
    high = jnp.where(tile == tiles - 1, 0.0, high).astype(BF16)
    odd = lax.rem(tile, 2) == 1
    tables[0] = jnp.where(odd, low, high)
    tables[1] = jnp.where(odd, high, low)
    out[...] = dot(mid_t[...], dot(mask[...], mid[...]).astype(BF16))


def relay_body(value, ready, out):
    out[...] = value[...]


def split_kernel(pair):
    left = in_left_half(pair.shape)
    other = swap_halves(pair)
    return jnp.where(left, pair, other), jnp.where(left, other, pair)


def fields_body(count, row_count, *refs):
    (middle, target, mid, rows_t, to_columns, from_columns, tables, own) = refs[:8]
    near_pack, *others, far_edge = refs[8 : 8 + count]
    out, a_ref, field_a, field_b, bent_a, bent_b, u_ref = refs[8 + count :]
    fields, bent = (field_a, field_b), (bent_a, bent_b)
    left = in_left_half((KF, PAIR))
    blocks = middle[...]
    for pack, table in ((near_pack, tables[0]), (far_edge, tables[1])):
        edge = pack[:EDGE, :].astype(F32)
        edge = jnp.concatenate([edge, swap_halves(edge)], 0).astype(BF16)
        blocks = blocks + dot(edge, table)
    top, bottom = blocks[:KF], swap_halves(blocks[KF:])
    spectrum = jnp.where(left, top - bottom, -(top + bottom))
    turned = swap_halves(spectrum)
    turned = jnp.where(left, -turned, turned)
    kernels = [own[...].astype(F32)]
    kernels.append(near_pack[EDGE : 2 * EDGE, :].astype(F32))
    kernels += [one[...].astype(F32) for one in others]
    kernels = [split_kernel(one) for one in kernels]
    begin = pl.multiple_of(lax.axis_index("kern") * row_count, row_count)
    rows = mid[pl.ds(begin, row_count), :]
    stacks = []
    for real, imag in kernels:
        product = real * spectrum + imag * turned
        other = swap_halves(product)
        other = jnp.where(left, -other, other)
        stacks.append(jnp.concatenate([product, other], 0).astype(BF16))
    waves = dot(rows, jnp.concatenate(stacks, 1)).astype(BF16)
    for index in range(count):
        a_ref[index * row_count : (index + 1) * row_count, :] = waves[:, index * PAIR : (index + 1) * PAIR]
    step = 16
    halves = (slice(0, LANES), slice(LANES, 2 * LANES))
    fields[0][...] = dot(a_ref[...], to_columns[0])
    for block in range(BLOCKS + 1):
        now = block % 2
        if block + 1 < BLOCKS:
            fields[1 - now][...] = dot(a_ref[...], to_columns[block + 1])
        if block > 0:
            part = dot(bent[1 - now][...], from_columns[block - 1])
            u_ref[...] = part if block == 1 else u_ref[...] + part
        if block == BLOCKS:
            continue
        for r in range(0, row_count, step):
            total = None
            for index in range(count):
                at = index * row_count + r
                real, imag = (fields[now][at : at + step, half] for half in halves)
                term = real * real + imag * imag
                total = term if total is None else total + term
            wanted = target[r : r + step, block * LANES : (block + 1) * LANES].astype(F32)
            decay = jnp.exp(4.0 - 2.0 * total)
            resist = pl.reciprocal(1.0 + decay, approx=True)
            slope = (resist - wanted) * (8.0 * decay) * (resist * resist)
            for index in range(count):
                at = index * row_count + r
                for half in halves:
                    field = fields[now][at : at + step, half] * slope
                    bent[now][at : at + step, half] = field.astype(BF16)
    wide = jnp.concatenate(
        [u_ref[i * row_count : (i + 1) * row_count, :].astype(BF16) for i in range(count)], 1
    )
    waves = dot(rows_t[...], wide)
    total = None
    for index, (real, imag) in enumerate(kernels):
        wave = waves[:, index * PAIR : (index + 1) * PAIR]
        top, bottom = wave[:KF], swap_halves(wave[KF:])
        wave = jnp.where(left, top + bottom, top - bottom)
        other = swap_halves(wave)
        other = jnp.where(left, other, -other)
        term = real * wave + imag * other
        total = term if total is None else total + term
    out[...] = total.astype(BF16)


def sum_body(count, *refs):
    total = refs[0][...].astype(F32)
    for one in refs[1:count]:
        total = total + one[...].astype(F32)
    refs[count][...] = total.astype(BF16)


def row_waves(rows, pair):
    pair = pair.astype(F32)
    other = swap_halves(pair)
    other = jnp.where(in_left_half(pair.shape), -other, other)
    return dot(rows, jnp.concatenate([pair, other], 0).astype(BF16)).astype(BF16)


def own_rows(mid, row_count):
    begin = pl.multiple_of(lax.axis_index("kern") * row_count, row_count)
    return mid[pl.ds(begin, row_count), :]


def inner_body(row_count, own, mid, back, out):
    out[...] = dot(row_waves(own_rows(mid, row_count), own[...]), back[...])


def outer_body(
    row_count, near, far, near_pack, far_edge, mid, margins, begun, out, held, sems
):
    inner = pltpu.make_async_copy(
        begun.at[:, LANES : N - LANES], out.at[:, LANES : N - LANES], sems.at[2]
    )
    inner.start()
    rows = own_rows(mid, row_count)
    near_wave, far_wave = row_waves(rows, near[...]), row_waves(rows, far[...])
    odd = lax.rem(lax.axis_index("tile"), 2) == 1
    below, above = jnp.where(odd, near_wave, far_wave), jnp.where(odd, far_wave, near_wave)
    near_marks = near_pack[2 * EDGE :, :].astype(F32)
    far_marks = far_edge[EDGE:, :].astype(F32)
    low_mark = jnp.where(odd, near_marks, far_marks)[1:2]
    high_mark = jnp.where(odd, far_marks, near_marks)[0:1]
    low = jnp.where(low_mark == 1.0, margins[1].astype(F32), margins[0].astype(F32)).astype(BF16)
    high = jnp.where(high_mark == 1.0, margins[3].astype(F32), margins[2].astype(F32)).astype(BF16)
    copies = []
    for side, first, wave, table in ((0, 0, below, low), (1, N - LANES, above, high)):
        columns = slice(first, first + LANES)
        held[side] = begun[:, columns] + dot(wave, table)
        copies.append(pltpu.make_async_copy(held.at[side], out.at[:, columns], sems.at[side]))
        copies[-1].start()
    for copy in (inner, *copies):
        copy.wait()


def far_off(array):
    return pltpu.with_memory_space_constraint(array, pltpu.HBM)


def per_device(mask_pixels, orientation, target_pattern, kernel_real, kernel_imag, eigen_weights):
    tables = tuple(jnp.asarray(one) for one in transform_tables())
    mid, mid_t, to_columns, from_columns, rims, back, margins = tables
    tiles, count = lax.axis_size("tile"), lax.axis_size("kern")
    row_count = target_pattern.shape[0]
    vmem = pl.BlockSpec(memory_space=pltpu.VMEM)
    smem = pl.BlockSpec(memory_space=pltpu.SMEM)
    hbm = pl.BlockSpec(memory_space=pltpu.HBM)
    small = jax.ShapeDtypeStruct((KF, PAIR), BF16)

    mate, other, side, mid, mid_t, marks, rims = call(
        edges_body,
        "edges",
        (
            pltpu.VMEM((2 * EDGE + MARKS, LANES), BF16),
            pltpu.VMEM((EDGE + MARKS, LANES), BF16),
            pltpu.VMEM((KF, PAIR), BF16),
            pltpu.VMEM((N, PAIR), BF16),
            pltpu.VMEM((PAIR, N), BF16),
            pltpu.VMEM((MARKS, LANES), BF16),
            pltpu.VMEM((4, LANES, PAIR), BF16),
        ),
        (
            *(far_off(one) for one in (mask_pixels, mid, mid_t, rims, kernel_real, kernel_imag)),
            eigen_weights,
            far_off(orientation),
        ),
        [hbm] * 6 + [smem, hbm],
        scratch=[
            pltpu.VMEM((N, 2 * LANES), BF16),
            pltpu.VMEM((2, KF, KF), F32),
            pltpu.SMEM((1, 2), jnp.int32),
            pltpu.SemaphoreType.DMA((8,)),
        ],
        flops=2 * N * LANES * PAIR * 2,
        moved=N * LANES * 4,
    )

    def swapped(move_tile, step):
        pairs = []
        for t in range(tiles):
            for k in range(count):
                pairs.append((t * count + k, move_tile(t) * count + destination(k, step, count)))
        return pairs

    def chip_mate(t):
        return t ^ 1

    def other_side(t):
        return (t + 1 if t % 2 else t - 1) % tiles

    both = ("tile", "kern")
    far_edge = lax.ppermute(other, both, swapped(other_side, 0))
    near_pack = lax.ppermute(mate, both, swapped(chip_mate, 1))
    if count == 4:
        pairs = []
        for t in range(tiles):
            pairs += [(t * count + k, t * count + destination(k, 2 + t % 2, count)) for k in range(count)]
        kernels = [lax.ppermute(side, both, pairs)]
    else:
        kernels = [lax.ppermute(side, both, swapped(lambda t: t, step)) for step in range(2, count)]

    middle, edge_tables, rows_t = call(
        functools.partial(middle_body, row_count),
        "middle",
        (
            pltpu.VMEM((PAIR, PAIR), F32),
            pltpu.VMEM((2, PAIR, PAIR), BF16),
            pltpu.VMEM((PAIR, row_count), BF16),
        ),
        (pltpu.with_memory_space_constraint(mask_pixels, pltpu.VMEM), mid, mid_t, marks, rims),
        [vmem] * 5,
        flops=4 * N * N * PAIR,
        moved=N * N * 2,
    )

    if count == 4:
        relayed = call(relay_body, "relay", small, (kernels[0], middle), [vmem] * 2)
        kernels.append(lax.ppermute(relayed, both, swapped(chip_mate, 0)))

    part = call(
        functools.partial(fields_body, count, row_count),
        "fields",
        small,
        (middle, target_pattern, mid, rows_t, to_columns, from_columns, edge_tables, side, near_pack, *kernels, far_edge),
        [vmem] * (8 + count),
        scratch=[
            pltpu.VMEM((count * row_count, PAIR), BF16),
            pltpu.VMEM((count * row_count, 2 * LANES), F32),
            pltpu.VMEM((count * row_count, 2 * LANES), F32),
            pltpu.VMEM((count * row_count, 2 * LANES), BF16),
            pltpu.VMEM((count * row_count, 2 * LANES), BF16),
            pltpu.VMEM((count * row_count, PAIR), F32),
        ],
        flops=8 * count * row_count * N * PAIR,
        moved=4 * row_count * N,
    )

    parts = [part]
    for step in range(1, count):
        pairs = []
        for t in range(tiles):
            own_step = sum_step(step, t, count)
            pairs += [(t * count + k, t * count + destination(k, own_step, count)) for k in range(count)]
        parts.append(lax.ppermute(part, both, pairs))
    own = call(functools.partial(sum_body, count), "total", small, tuple(parts), [vmem] * count)
    near = lax.ppermute(own, "tile", [(t, chip_mate(t)) for t in range(tiles)])
    inner = [t for t in range(tiles) if 0 < t < tiles - 1]
    far = lax.ppermute(own, "tile", [(t, other_side(t)) for t in inner])
    begun = call(
        functools.partial(inner_body, row_count),
        "inner",
        pltpu.VMEM((row_count, N), F32),
        (own, mid, back),
        [vmem] * 3,
        flops=2 * row_count * PAIR * N,
        moved=4 * row_count * N,
    )
    return call(
        functools.partial(outer_body, row_count),
        "outer",
        jax.ShapeDtypeStruct((row_count, N), F32),
        (near, far, near_pack, far_edge, mid, margins, begun),
        [vmem] * 7,
        hbm,
        scratch=[
            pltpu.VMEM((2, row_count, LANES), F32),
            pltpu.SemaphoreType.DMA((3,)),
        ],
        flops=2 * row_count * PAIR * 6 * PAIR,
        moved=4 * row_count * 2 * LANES,
    )


def solution(mesh):
    in_specs = (
        P(None, "tile"),
        P("tile", None),
        P("kern", "tile"),
        P("kern", None, None),
        P("kern", None, None),
        P("kern"),
    )
    out_specs = P("kern", "tile")
    return jax.shard_map(
        per_device, mesh=mesh, in_specs=in_specs, out_specs=out_specs, check_vma=False
    )
```

```python
import functools
import math

import jax
import jax.numpy as jnp
import ml_dtypes
import numpy as np
from jax import lax
from jax.experimental import pallas as pl
from jax.experimental.pallas import tpu as pltpu
from jax.sharding import PartitionSpec as P

N = 1152
HALO = 64
KF = 64
NE = 1280
LANES = 128
PAIR = 2 * KF
BLOCKS = N // LANES
EDGE = KF
MARKS = 16
BF16 = jnp.bfloat16
F32 = jnp.float32
VMEM_LIMIT = 32 * 1024 * 1024


def wave_tables():
    position = np.arange(NE)[:, None]
    frequency = np.arange(KF)[None, :] - KF // 2
    phase = np.mod(position * frequency, NE).astype(np.float64) * (2.0 * math.pi / NE)
    return np.cos(phase).astype(np.float32), np.sin(phase).astype(np.float32)


def transform_tables():
    cos, sin = wave_tables()
    full = np.concatenate([cos, sin], 1)
    mid = full[HALO : HALO + N]
    ct, st = cos[HALO : HALO + N].T, sin[HALO : HALO + N].T
    columns = np.concatenate(
        [
            np.stack([ct.reshape(KF, BLOCKS, LANES), st.reshape(KF, BLOCKS, LANES)], 2),
            np.stack([-st.reshape(KF, BLOCKS, LANES), ct.reshape(KF, BLOCKS, LANES)], 2),
        ],
        0,
    )
    to_columns = columns.transpose(1, 0, 2, 3).reshape(BLOCKS, PAIR, 2 * LANES)
    from_columns = to_columns.transpose(0, 2, 1)
    low, high = full[:HALO], full[HALO + N :]
    blank = np.zeros((HALO, PAIR), np.float32)
    rims = np.stack(
        [
            np.concatenate([low[::-1], blank], 0),
            np.concatenate([low, blank], 0),
            np.concatenate([high[::-1], blank], 0),
            np.concatenate([high, blank], 0),
        ]
    )
    back = np.concatenate([cos.T, -sin.T], 0)
    back_low, back_high = back[:, :HALO], back[:, HALO + N :]
    blank = np.zeros((PAIR, HALO), np.float32)
    margins = np.stack(
        [
            np.concatenate([back_high[:, ::-1], blank], 1),
            np.concatenate([back_high, blank], 1),
            np.concatenate([blank, back_low[:, ::-1]], 1),
            np.concatenate([blank, back_low], 1),
        ]
    )
    tables = (mid, mid.T, to_columns, from_columns, rims, back[:, HALO : HALO + N], margins)
    return tuple(np.ascontiguousarray(one).astype(ml_dtypes.bfloat16) for one in tables)


def dot(a, b):
    return jnp.dot(a, b, preferred_element_type=F32)


def in_left_half(shape):
    return lax.broadcasted_iota(jnp.int32, shape, 1) < KF


def swap_halves(pair):
    return pltpu.roll(pair, KF, 1)


def sum_step(step, tile, count):
    return (step, count - step)[tile % 2] if count == 4 else step


def destination(k, step, count):
    return k ^ step if count == 4 else (k - step) % count


def call(
    body, name, outs, args, specs, out_specs=None, scratch=(), flops=0, moved=0
):
    vmem = pl.BlockSpec(memory_space=pltpu.VMEM)
    if out_specs is None:
        out_specs = tuple(vmem for _ in outs) if isinstance(outs, tuple) else vmem
    return pl.pallas_call(
        body,
        name=name,
        out_shape=outs,
        in_specs=specs,
        out_specs=out_specs,
        scratch_shapes=list(scratch),
        compiler_params=pltpu.CompilerParams(vmem_limit_bytes=VMEM_LIMIT),
        cost_estimate=pl.CostEstimate(flops=flops, bytes_accessed=moved, transcendentals=0),
    )(*args)


def edges_body(
    mask, mid, mid_t, rims, real, imag, weight, flags, mate, other, side, tall, table, sides_out, rims_out, strips, pair, marks, sems
):
    odd = lax.rem(lax.axis_index("tile"), 2) == 1
    copies = [
        pltpu.make_async_copy(mid_t, table, sems.at[0]),
        pltpu.make_async_copy(mask.at[:, :LANES], strips.at[:, :LANES], sems.at[1]),
        pltpu.make_async_copy(mask.at[:, N - LANES :], strips.at[:, LANES:], sems.at[2]),
        pltpu.make_async_copy(real.at[0], pair.at[0], sems.at[3]),
        pltpu.make_async_copy(imag.at[0], pair.at[1], sems.at[4]),
        pltpu.make_async_copy(flags, marks, sems.at[5]),
    ]
    turned = pltpu.make_async_copy(rims, rims_out, sems.at[6])
    columns = pltpu.make_async_copy(mid, tall, sems.at[7])
    for copy in copies:
        copy.start()
    turned.start()
    columns.start()
    for copy in copies[3:]:
        copy.wait()
    scale = jnp.sqrt(jnp.full((KF, KF), 2.0 * weight[0], F32)) * (1.0 / (NE * KF))
    kernel = jnp.concatenate([pair[0] * scale, pair[1] * scale], 1).astype(BF16)
    row = lax.broadcasted_iota(jnp.int32, (16, LANES), 0)
    sides = jnp.where(row == 0, marks[0, 0].astype(F32), marks[0, 1].astype(F32)).astype(BF16)
    side[...] = kernel
    mate[EDGE : 2 * EDGE, :] = kernel
    mate[2 * EDGE :, :] = sides
    other[EDGE:, :] = sides
    sides_out[...] = sides
    for copy in copies[:3]:
        copy.wait()
    both = dot(table[...], strips[...])
    left = in_left_half((KF, LANES))
    first, last = both[:, :LANES], both[:, LANES:]
    first = jnp.where(left, first[:KF], swap_halves(first[KF:]))
    last = jnp.where(left, swap_halves(last[:KF]), last[KF:])
    mate[:EDGE, :] = jnp.where(odd, first, last).astype(BF16)
    other[:EDGE, :] = jnp.where(odd, last, first).astype(BF16)
    turned.wait()
    columns.wait()


def middle_body(row_count, mask, mid, mid_t, marks, rims, out, tables, rows_t):
    rows_t[...] = own_rows(mid, row_count).astype(F32).T.astype(BF16)
    tile, tiles = lax.axis_index("tile"), lax.axis_size("tile")
    own = marks[...].astype(F32)
    low = jnp.where(own[0:1] == 1.0, rims[1].astype(F32), rims[0].astype(F32))
    high = jnp.where(own[1:2] == 1.0, rims[3].astype(F32), rims[2].astype(F32))
    low = jnp.where(tile == 0, 0.0, low).astype(BF16)
    high = jnp.where(tile == tiles - 1, 0.0, high).astype(BF16)
    odd = lax.rem(tile, 2) == 1
    tables[0] = jnp.where(odd, low, high)
    tables[1] = jnp.where(odd, high, low)
    out[...] = dot(mid_t[...], dot(mask[...], mid[...]).astype(BF16))


def relay_body(value, ready, out):
    out[...] = value[...]


def split_kernel(pair):
    left = in_left_half(pair.shape)
    other = swap_halves(pair)
    return jnp.where(left, pair, other), jnp.where(left, other, pair)


def fields_body(count, row_count, *refs):
    (middle, target, mid, rows_t, to_columns, from_columns, tables, own) = refs[:8]
    near_pack, *others, far_edge = refs[8 : 8 + count]
    out, a_ref, field_a, field_b, bent_a, bent_b, u_ref = refs[8 + count :]
    fields, bent = (field_a, field_b), (bent_a, bent_b)
    left = in_left_half((KF, PAIR))
    blocks = middle[...]
    for pack, table in ((near_pack, tables[0]), (far_edge, tables[1])):
        edge = pack[:EDGE, :].astype(F32)
        edge = jnp.concatenate([edge, swap_halves(edge)], 0).astype(BF16)
        blocks = blocks + dot(edge, table)
    top, bottom = blocks[:KF], swap_halves(blocks[KF:])
    spectrum = jnp.where(left, top - bottom, -(top + bottom))
    turned = swap_halves(spectrum)
    turned = jnp.where(left, -turned, turned)
    kernels = [own[...].astype(F32)]
    kernels.append(near_pack[EDGE : 2 * EDGE, :].astype(F32))
    kernels += [one[...].astype(F32) for one in others]
    kernels = [split_kernel(one) for one in kernels]
    begin = pl.multiple_of(lax.axis_index("kern") * row_count, row_count)
    rows = mid[pl.ds(begin, row_count), :]
    stacks = []
    for real, imag in kernels:
        product = real * spectrum + imag * turned
        other = swap_halves(product)
        other = jnp.where(left, -other, other)
        stacks.append(jnp.concatenate([product, other], 0).astype(BF16))
    waves = dot(rows, jnp.concatenate(stacks, 1)).astype(BF16)
    for index in range(count):
        a_ref[index * row_count : (index + 1) * row_count, :] = waves[:, index * PAIR : (index + 1) * PAIR]
    step = 16
    halves = (slice(0, LANES), slice(LANES, 2 * LANES))
    fields[0][...] = dot(a_ref[...], to_columns[0])
    for block in range(BLOCKS + 1):
        now = block % 2
        if block + 1 < BLOCKS:
            fields[1 - now][...] = dot(a_ref[...], to_columns[block + 1])
        if block > 0:
            part = dot(bent[1 - now][...], from_columns[block - 1])
            u_ref[...] = part if block == 1 else u_ref[...] + part
        if block == BLOCKS:
            continue
        for r in range(0, row_count, step):
            total = None
            for index in range(count):
                at = index * row_count + r
                real, imag = (fields[now][at : at + step, half] for half in halves)
                term = real * real + imag * imag
                total = term if total is None else total + term
            wanted = target[r : r + step, block * LANES : (block + 1) * LANES].astype(F32)
            decay = jnp.exp(4.0 - 2.0 * total)
            resist = pl.reciprocal(1.0 + decay, approx=True)
            slope = (resist - wanted) * (8.0 * decay) * (resist * resist)
            for index in range(count):
                at = index * row_count + r
                for half in halves:
                    field = fields[now][at : at + step, half] * slope
                    bent[now][at : at + step, half] = field.astype(BF16)
    wide = jnp.concatenate(
        [u_ref[i * row_count : (i + 1) * row_count, :].astype(BF16) for i in range(count)], 1
    )
    waves = dot(rows_t[...], wide)
    total = None
    for index, (real, imag) in enumerate(kernels):
        wave = waves[:, index * PAIR : (index + 1) * PAIR]
        top, bottom = wave[:KF], swap_halves(wave[KF:])
        wave = jnp.where(left, top + bottom, top - bottom)
        other = swap_halves(wave)
        other = jnp.where(left, other, -other)
        term = real * wave + imag * other
        total = term if total is None else total + term
    out[...] = total.astype(BF16)


def sum_body(count, *refs):
    total = refs[0][...].astype(F32)
    for one in refs[1:count]:
        total = total + one[...].astype(F32)
    refs[count][...] = total.astype(BF16)


def row_waves(rows, pair):
    pair = pair.astype(F32)
    other = swap_halves(pair)
    other = jnp.where(in_left_half(pair.shape), -other, other)
    return dot(rows, jnp.concatenate([pair, other], 0).astype(BF16)).astype(BF16)


def own_rows(mid, row_count):
    begin = pl.multiple_of(lax.axis_index("kern") * row_count, row_count)
    return mid[pl.ds(begin, row_count), :]


def inner_body(row_count, own, mid, back, out):
    out[...] = dot(row_waves(own_rows(mid, row_count), own[...]), back[...])


def outer_body(
    row_count, near, far, near_pack, far_edge, mid, margins, begun, out, held, sems
):
    inner = pltpu.make_async_copy(
        begun.at[:, LANES : N - LANES], out.at[:, LANES : N - LANES], sems.at[2]
    )
    inner.start()
    rows = own_rows(mid, row_count)
    near_wave, far_wave = row_waves(rows, near[...]), row_waves(rows, far[...])
    odd = lax.rem(lax.axis_index("tile"), 2) == 1
    below, above = jnp.where(odd, near_wave, far_wave), jnp.where(odd, far_wave, near_wave)
    near_marks = near_pack[2 * EDGE :, :].astype(F32)
    far_marks = far_edge[EDGE:, :].astype(F32)
    low_mark = jnp.where(odd, near_marks, far_marks)[1:2]
    high_mark = jnp.where(odd, far_marks, near_marks)[0:1]
    low = jnp.where(low_mark == 1.0, margins[1].astype(F32), margins[0].astype(F32)).astype(BF16)
    high = jnp.where(high_mark == 1.0, margins[3].astype(F32), margins[2].astype(F32)).astype(BF16)
    copies = []
    for side, first, wave, table in ((0, 0, below, low), (1, N - LANES, above, high)):
        columns = slice(first, first + LANES)
        held[side] = begun[:, columns] + dot(wave, table)
        copies.append(pltpu.make_async_copy(held.at[side], out.at[:, columns], sems.at[side]))
        copies[-1].start()
    for copy in (inner, *copies):
        copy.wait()


def far_off(array):
    return pltpu.with_memory_space_constraint(array, pltpu.HBM)


def per_device(mask_pixels, orientation, target_pattern, kernel_real, kernel_imag, eigen_weights):
    tables = tuple(jnp.asarray(one) for one in transform_tables())
    mid, mid_t, to_columns, from_columns, rims, back, margins = tables
    tiles, count = lax.axis_size("tile"), lax.axis_size("kern")
    row_count = target_pattern.shape[0]
    vmem = pl.BlockSpec(memory_space=pltpu.VMEM)
    smem = pl.BlockSpec(memory_space=pltpu.SMEM)
    hbm = pl.BlockSpec(memory_space=pltpu.HBM)
    small = jax.ShapeDtypeStruct((KF, PAIR), BF16)

    mate, other, side, mid, mid_t, marks, rims = call(
        edges_body,
        "edges",
        (
            pltpu.VMEM((2 * EDGE + MARKS, LANES), BF16),
            pltpu.VMEM((EDGE + MARKS, LANES), BF16),
            pltpu.VMEM((KF, PAIR), BF16),
            pltpu.VMEM((N, PAIR), BF16),
            pltpu.VMEM((PAIR, N), BF16),
            pltpu.VMEM((MARKS, LANES), BF16),
            pltpu.VMEM((4, LANES, PAIR), BF16),
        ),
        (
            *(far_off(one) for one in (mask_pixels, mid, mid_t, rims, kernel_real, kernel_imag)),
            eigen_weights,
            far_off(orientation),
        ),
        [hbm] * 6 + [smem, hbm],
        scratch=[
            pltpu.VMEM((N, 2 * LANES), BF16),
            pltpu.VMEM((2, KF, KF), F32),
            pltpu.SMEM((1, 2), jnp.int32),
            pltpu.SemaphoreType.DMA((8,)),
        ],
        flops=2 * N * LANES * PAIR * 2,
        moved=N * LANES * 4,
    )

    def swapped(move_tile, step):
        pairs = []
        for t in range(tiles):
            for k in range(count):
                pairs.append((t * count + k, move_tile(t) * count + destination(k, step, count)))
        return pairs

    def chip_mate(t):
        return t ^ 1

    def other_side(t):
        return (t + 1 if t % 2 else t - 1) % tiles

    both = ("tile", "kern")
    far_edge = lax.ppermute(other, both, swapped(other_side, 0))
    near_pack = lax.ppermute(mate, both, swapped(chip_mate, 1))
    if count == 4:
        pairs = []
        for t in range(tiles):
            pairs += [(t * count + k, t * count + destination(k, 2 + t % 2, count)) for k in range(count)]
        kernels = [lax.ppermute(side, both, pairs)]
    else:
        kernels = [lax.ppermute(side, both, swapped(lambda t: t, step)) for step in range(2, count)]

    middle, edge_tables, rows_t = call(
        functools.partial(middle_body, row_count),
        "middle",
        (
            pltpu.VMEM((PAIR, PAIR), F32),
            pltpu.VMEM((2, PAIR, PAIR), BF16),
            pltpu.VMEM((PAIR, row_count), BF16),
        ),
        (pltpu.with_memory_space_constraint(mask_pixels, pltpu.VMEM), mid, mid_t, marks, rims),
        [vmem] * 5,
        flops=4 * N * N * PAIR,
        moved=N * N * 2,
    )

    if count == 4:
        relayed = call(relay_body, "relay", small, (kernels[0], middle), [vmem] * 2)
        kernels.append(lax.ppermute(relayed, both, swapped(chip_mate, 0)))

    part = call(
        functools.partial(fields_body, count, row_count),
        "fields",
        small,
        (middle, target_pattern, mid, rows_t, to_columns, from_columns, edge_tables, side, near_pack, *kernels, far_edge),
        [vmem] * (8 + count),
        scratch=[
            pltpu.VMEM((count * row_count, PAIR), BF16),
            pltpu.VMEM((count * row_count, 2 * LANES), F32),
            pltpu.VMEM((count * row_count, 2 * LANES), F32),
            pltpu.VMEM((count * row_count, 2 * LANES), BF16),
            pltpu.VMEM((count * row_count, 2 * LANES), BF16),
            pltpu.VMEM((count * row_count, PAIR), F32),
        ],
        flops=8 * count * row_count * N * PAIR,
        moved=4 * row_count * N,
    )

    parts = [part]
    for step in range(1, count):
        pairs = []
        for t in range(tiles):
            own_step = sum_step(step, t, count)
            pairs += [(t * count + k, t * count + destination(k, own_step, count)) for k in range(count)]
        parts.append(lax.ppermute(part, both, pairs))
    own = call(functools.partial(sum_body, count), "total", small, tuple(parts), [vmem] * count)
    near = lax.ppermute(own, "tile", [(t, chip_mate(t)) for t in range(tiles)])
    inner = [t for t in range(tiles) if 0 < t < tiles - 1]
    far = lax.ppermute(own, "tile", [(t, other_side(t)) for t in inner])
    begun = call(
        functools.partial(inner_body, row_count),
        "inner",
        pltpu.VMEM((row_count, N), F32),
        (own, mid, back),
        [vmem] * 3,
        flops=2 * row_count * PAIR * N,
        moved=4 * row_count * N,
    )
    return call(
        functools.partial(outer_body, row_count),
        "outer",
        jax.ShapeDtypeStruct((row_count, N), F32),
        (near, far, near_pack, far_edge, mid, margins, begun),
        [vmem] * 7,
        hbm,
        scratch=[
            pltpu.VMEM((2, row_count, LANES), F32),
            pltpu.SemaphoreType.DMA((3,)),
        ],
        flops=2 * row_count * PAIR * 6 * PAIR,
        moved=4 * row_count * 2 * LANES,
    )


def solution(mesh):
    in_specs = (
        P(None, "tile"),
        P("tile", None),
        P("kern", "tile"),
        P("kern", None, None),
        P("kern", None, None),
        P("kern"),
    )
    out_specs = P("kern", "tile")
    return jax.shard_map(
        per_device, mesh=mesh, in_specs=in_specs, out_specs=out_specs, check_vma=False
    )
```
